32 devices in a mesh: groups: 2 (over y), gx: 4 (over z), gy: 4 (over x, core).
Axes of the slice: x: 2, y: 2, z: 4, core: 2. Of those that a mesh axis runs over, the one named last changes fastest.
Arguments:
- stored_rows: bfloat16 [320, 16384], P(('groups', 'gy'), 'gx'), parts along dimension 0, may hold values from -6 to 6
- new_rows: bfloat16 [16, 16384], P(('groups', 'gy'), 'gx'), parts along dimension 0, may hold values from -6 to 6
- w_query: bfloat16 [16384, 8192], P('gx', 'gy'), may hold values from -0.046875 to 0.046875
- w_key: bfloat16 [16384, 512], P('gx', 'gy'), may hold values from -0.046875 to 0.046875
- w_value: bfloat16 [16384, 512], P('gx', 'gy'), may hold values from -0.046875 to 0.046875
- w_out: bfloat16 [8192, 16384], P('gy', 'gx'), may hold values from -0.0625 to 0.0625
- kv_cache: bfloat16 [2, 16, 512, 512], P(None, ('groups', 'gx'), None, 'gy'), parts along dimension 1, may hold values from -52 to 52
- cache_len: int32 [16], P(('groups', 'gx')), parts along dimension 0, may hold values from 1 to 512, as said below
- owner: int32 [8], P('groups'), parts along dimension 0, may hold values from 0 to 3, as said below
Outputs:
- mixed: bfloat16 [16, 16384], P(('groups', 'gy'), 'gx'), parts along dimension 0
- rebuilt_key: bfloat16 [8, 40, 512], P(('groups', 'gx'), None, 'gy'), parts along dimension 0
- rebuilt_value: bfloat16 [8, 40, 512], P(('groups', 'gx'), None, 'gy'), parts along dimension 0
The draws below stay inside these ranges and needn't reach their ends.
There are 2 independent parts, one for each index of `groups`. The reference program is written for one: setup_inputs(seed, part) draws one part's arguments, and reference() takes and returns one part's arrays. A program takes and returns all parts, laid end to end along the dimension named above; an argument that names none is the same for every part. Nothing has to cross between parts.
Inputs may be any that keep to these rules, and one draw needn't show every extreme that they name: A permutation: each owner index takes exactly one conversation. Only a row's first cache_len slots hold data; some row has all 512 slots in use.
All inputs are finite; a program needn't handle non-finite values.
Results may differ from the reference program's by a relative error of at most 0.013.
Values may be sent and summed in bfloat16 or wider, within the bound.
No kernel may reach another device: no remote copies, remote signals or barrier semaphores. Data moves between devices by JAX's collectives and lax.ppermute only.
A program may use at most 64 MiB of HBM per device.

```python
import math
import jax
import jax.numpy as jnp
from jax import lax

D = 16384
HD = 128
QH = 64
KVH = 4
GROUP = 16
QW = 8192
KVW = 512
L = 512
LC = 40
ROWS_DEV = 2
ROWS = 8
NCONV = 4
STORED = 160


def draw_kv_cache(key, part):
    first_key = jax.random.fold_in(jax.random.fold_in(key, 11), 0)
    shape = (2, ROWS, L, KVW)
    base = jax.random.truncated_normal(first_key, -6.0, 6.0, shape, jnp.float32)
    return base.astype(jnp.bfloat16)


def draw_cache_len(key, part):
    first_key, second_key = jax.random.split(jax.random.fold_in(key, 23))
    lengths = jax.random.randint(first_key, (ROWS,), 1, L + 1)
    chosen = jax.random.randint(second_key, (), 0, ROWS)
    return jnp.where(jnp.arange(ROWS) == chosen, L, lengths).astype(jnp.int32)


def draw_owner(key, part):
    owner_key = jax.random.fold_in(key, 37)
    return jax.random.permutation(owner_key, NCONV).astype(jnp.int32)


def steps_of(key, extent, cuts, smallest, largest):
    factor_of, own = 1.0, jax.random.fold_in(key, 6)
    for dim, parts in cuts:
        steps = jnp.exp(jax.random.uniform(jax.random.fold_in(own, dim), (parts,), jnp.float32, smallest / len(cuts), largest / len(cuts)))
        factor_of = factor_of * jnp.repeat(steps, extent[dim] // parts).reshape([-1 if axis == dim else 1 for axis in range(len(extent))])
    return factor_of


def scatter_about(stream_key, shape, width, reach, cuts=(), kind=jnp.bfloat16):
    level = steps_of(stream_key, shape, cuts, -0.22, 0.18) if cuts else 1.0
    drawn = jax.random.normal(stream_key, shape, jnp.float32) * width * level
    return jnp.minimum(jnp.maximum(drawn, -reach), reach).astype(kind)


def setup_inputs(seed: int = 0, part: int = 0) -> dict:
    seeds = jax.random.split(jax.random.key(seed), 10)
    part_keys = jax.random.split(jax.random.fold_in(seeds[9], part), 10)
    return {
        "stored_rows": scatter_about(part_keys[0], (STORED, D), 1.0, 6.0, ((0, 4), (1, 4))),
        "new_rows": scatter_about(part_keys[1], (ROWS, D), 1.0, 6.0, ((0, 4), (1, 4))),
        "w_query": scatter_about(seeds[2], (D, QW), D ** -0.5, 0.046875, ((0, 4), (1, 4))),
        "w_key": scatter_about(seeds[3], (D, KVW), D ** -0.5, 0.046875, ((0, 4), (1, 4))),
        "w_value": scatter_about(seeds[4], (D, KVW), D ** -0.5, 0.046875, ((0, 4), (1, 4))),
        "w_out": scatter_about(seeds[5], (QW, D), QW ** -0.5, 0.0625, ((0, 4), (1, 4))),
        "kv_cache": draw_kv_cache(jax.random.fold_in(jax.random.fold_in(seeds[9], part), 71), part),
        "cache_len": draw_cache_len(jax.random.fold_in(jax.random.fold_in(seeds[9], part), 71), part),
        "owner": draw_owner(jax.random.fold_in(jax.random.fold_in(seeds[9], part), 71), part),
    }


BASE = 500000.0

def rotate(incoming_values, position):
    half = incoming_values.shape[-1] // 2
    index_row = jnp.arange(half).astype(jnp.float32)
    frequency = jnp.exp(index_row * (-2.0 * math.log(BASE) / incoming_values.shape[-1]))
    angle = position.astype(jnp.float32)[..., None] * frequency
    cosine = jnp.cos(angle)
    sine = jnp.sin(angle)
    first_half = incoming_values[..., :half]
    second_half = incoming_values[..., half:]
    return jnp.concatenate([first_half * cosine - second_half * sine, second_half * cosine + first_half * sine], axis=-1)

def reference(stored_rows, new_rows, w_query, w_key, w_value, w_out, kv_cache, cache_len, owner):
    stored_key = jnp.dot(stored_rows, w_key, preferred_element_type=jnp.float32)
    stored_value = jnp.dot(stored_rows, w_value, preferred_element_type=jnp.float32)
    slot_ids = jnp.arange(NCONV, dtype=jnp.int32)
    inverse = lax.optimization_barrier(jnp.sum(jnp.where(owner[None, :] == slot_ids[:, None], slot_ids[None, :], 0), axis=1)).astype(jnp.int32)
    own_key = stored_key.reshape(NCONV, LC, KVW)[inverse]
    own_value = stored_value.reshape(NCONV, LC, KVW)[inverse]
    first_len = cache_len.reshape(NCONV, ROWS_DEV)[:, 0]
    tail_pos = first_len[:, None] + jnp.arange(LC, dtype=jnp.int32)[None, :]
    rebuilt_key = rotate(own_key.reshape(NCONV, LC, KVH, HD), tail_pos[:, :, None]).reshape(NCONV, LC, KVW).astype(jnp.bfloat16)
    rebuilt_value = own_value.astype(jnp.bfloat16)
    query = jnp.dot(new_rows, w_query, preferred_element_type=jnp.float32)
    fresh_key = jnp.dot(new_rows, w_key, preferred_element_type=jnp.float32)
    fresh_value = jnp.dot(new_rows, w_value, preferred_element_type=jnp.float32)
    resumed = jnp.arange(ROWS, dtype=jnp.int32) % ROWS_DEV == 0
    new_pos = cache_len + jnp.where(resumed, LC, 0).astype(jnp.int32)
    query_rot = rotate(query.reshape(ROWS, QH, HD), new_pos[:, None]).astype(jnp.bfloat16)
    rotary_key_rows = rotate(fresh_key.reshape(ROWS, KVH, HD), new_pos[:, None]).astype(jnp.bfloat16)
    value_new = fresh_value.reshape(ROWS, KVH, HD).astype(jnp.bfloat16)
    score_scaling_factor = 1.0 / math.sqrt(HD)
    grouped_query_heads = query_rot.astype(jnp.float32).reshape(ROWS, KVH, GROUP, HD)
    cached_keys_lookup = kv_cache[0].astype(jnp.float32).reshape(ROWS, L, KVH, HD)
    cache_value = kv_cache[1].astype(jnp.float32).reshape(ROWS, L, KVH, HD)
    row_owner = jnp.arange(ROWS, dtype=jnp.int32) // ROWS_DEV
    tail_key = rebuilt_key.astype(jnp.float32).reshape(NCONV, LC, KVH, HD)[row_owner]
    tail_value = rebuilt_value.astype(jnp.float32).reshape(NCONV, LC, KVH, HD)[row_owner]
    live_row_mask = jnp.arange(L, dtype=jnp.int32)[None, :] < cache_len[:, None]
    s_cache = jnp.einsum('bkgd,blkd->bkgl', grouped_query_heads, cached_keys_lookup) * score_scaling_factor
    s_cache = jnp.where(live_row_mask[:, None, None, :], s_cache, -jnp.inf)
    s_tail = jnp.einsum('bkgd,btkd->bkgt', grouped_query_heads, tail_key) * score_scaling_factor
    s_tail = jnp.where(resumed[:, None, None, None], s_tail, -jnp.inf)
    self_score = jnp.einsum('hzrt,hzt->hzr', grouped_query_heads, rotary_key_rows.astype(jnp.float32)) * score_scaling_factor
    highest = jnp.maximum(jnp.maximum(lax.optimization_barrier(jnp.max(s_cache, axis=-1)), lax.optimization_barrier(jnp.max(s_tail, axis=-1))), self_score)
    e_cache = jnp.exp(s_cache - highest[..., None])
    e_tail = jnp.exp(s_tail - highest[..., None])
    e_self = jnp.exp(self_score - highest)
    denominator = lax.optimization_barrier(jnp.sum(e_cache, axis=-1)) + lax.optimization_barrier(jnp.sum(e_tail, axis=-1)) + e_self
    w_cache = (e_cache / denominator[..., None]).astype(jnp.bfloat16)
    w_tail = (e_tail / denominator[..., None]).astype(jnp.bfloat16)
    w_self = (e_self / denominator).astype(jnp.bfloat16)
    attn = jnp.einsum('bkgl,blkd->bkgd', w_cache.astype(jnp.float32), cache_value)
    attn = attn + jnp.einsum('bkgt,btkd->bkgd', w_tail.astype(jnp.float32), tail_value)
    attn = attn + w_self.astype(jnp.float32)[..., None] * value_new.astype(jnp.float32)[:, :, None, :]
    attn = attn.reshape(ROWS, QW).astype(jnp.bfloat16)
    mixed = jnp.dot(attn, w_out, preferred_element_type=jnp.float32).astype(jnp.bfloat16)
    return (mixed, rebuilt_key, rebuilt_value)
```

```python
import math

import jax
import jax.numpy as jnp
from jax import lax
from jax.experimental import pallas as pl
from jax.experimental.pallas import tpu as pltpu
from jax.sharding import PartitionSpec as P

HD = 128
LC = 40
ROWS_DEV = 2
BASE = 500000.0
DIRECT = 8


def rotate(values, position):
    half = values.shape[-1] // 2
    index_row = jnp.arange(half).astype(jnp.float32)
    frequency = jnp.exp(index_row * (-2.0 * math.log(BASE) / values.shape[-1]))
    angle = position.astype(jnp.float32)[..., None] * frequency
    cosine = jnp.cos(angle)
    sine = jnp.sin(angle)
    first_half = values[..., :half]
    second_half = values[..., half:]
    return jnp.concatenate(
        [first_half * cosine - second_half * sine, second_half * cosine + first_half * sine],
        axis=-1,
    )


def swap(x, axis, k):
    n = lax.axis_size(axis)
    return lax.ppermute(x, axis, [(i, i ^ k) for i in range(n)])


def gather(x, axis):
    n = lax.axis_size(axis)
    if n > DIRECT or n & (n - 1):
        return lax.all_gather(x, axis, axis=0)
    me = lax.axis_index(axis)
    out = jnp.zeros((n,) + x.shape, x.dtype)
    for k in range(n):
        block = x if k == 0 else swap(x, axis, k)
        out = lax.dynamic_update_index_in_dim(out, block, me ^ k, 0)
    return out


def scatter_sum(parts, axis):
    n = lax.axis_size(axis)
    me = lax.axis_index(axis)
    if n > DIRECT or n & (n - 1):
        whole = jnp.stack([parts(d) for d in range(n)])
        return lax.psum_scatter(whole.astype(jnp.float32), axis, scatter_dimension=0)
    total = parts(me).astype(jnp.float32)
    for k in range(1, n):
        total = total + swap(parts(me ^ k).astype(jnp.bfloat16), axis, k).astype(jnp.float32)
    return total


def general(stored_rows, new_rows, w_query, w_key, w_value, w_out, kv_cache, cache_len, owner):
    owners = lax.axis_size("gx")
    key_cols = w_key.shape[1]
    query_cols = w_query.shape[1]
    heads_here = key_cols // HD
    group_size = query_cols // key_cols
    slot_ids = jnp.arange(owners, dtype=jnp.int32)
    inverse = jnp.sum(jnp.where(owner[None, :] == slot_ids[:, None], slot_ids[None, :], 0), axis=1)

    fresh_all = gather(new_rows, "gy").reshape(-1, new_rows.shape[1])
    stored_all = gather(stored_rows, "gy").reshape(owners, LC, stored_rows.shape[1])
    flat = stored_all.reshape(owners * LC, stored_rows.shape[1])
    query_part = jnp.dot(fresh_all, w_query, preferred_element_type=jnp.float32)
    new_key_part = jnp.dot(fresh_all, w_key, preferred_element_type=jnp.float32)
    new_value_part = jnp.dot(fresh_all, w_value, preferred_element_type=jnp.float32)
    key_part = jnp.dot(flat, w_key, preferred_element_type=jnp.float32)
    value_part = jnp.dot(flat, w_value, preferred_element_type=jnp.float32)

    small = jnp.concatenate([query_part, new_key_part, new_value_part], axis=1)
    small = small.reshape(owners, ROWS_DEV, -1)
    large = jnp.concatenate([key_part, value_part], axis=1).reshape(owners, LC, -1)

    small_sum = scatter_sum(lambda d: lax.dynamic_index_in_dim(small, d, 0, False), "gx")
    large_sum = scatter_sum(
        lambda d: lax.dynamic_index_in_dim(
            large, lax.dynamic_index_in_dim(inverse, d, 0, False), 0, False
        ),
        "gx",
    )
    query = small_sum[:, :query_cols]
    fresh_key = small_sum[:, query_cols : query_cols + key_cols]
    fresh_value = small_sum[:, query_cols + key_cols :]
    own_key = large_sum[:, :key_cols]
    own_value = large_sum[:, key_cols:]

    first_len = cache_len[0]
    tail_pos = first_len + jnp.arange(LC, dtype=jnp.int32)
    rebuilt_key = (
        rotate(own_key.reshape(LC, heads_here, HD), tail_pos[:, None])
        .reshape(LC, key_cols)
        .astype(jnp.bfloat16)
    )
    rebuilt_value = own_value.astype(jnp.bfloat16)
    resumed = jnp.arange(ROWS_DEV, dtype=jnp.int32) == 0
    new_pos = cache_len + jnp.where(resumed, LC, 0).astype(jnp.int32)
    query_rot = rotate(query.reshape(ROWS_DEV, query_cols // HD, HD), new_pos[:, None]).astype(
        jnp.bfloat16
    )
    key_rot = rotate(fresh_key.reshape(ROWS_DEV, heads_here, HD), new_pos[:, None]).astype(
        jnp.bfloat16
    )
    value_new = fresh_value.reshape(ROWS_DEV, heads_here, HD).astype(jnp.bfloat16)
    scale = 1.0 / math.sqrt(HD)
    slots = kv_cache.shape[2]
    grouped = query_rot.reshape(ROWS_DEV, heads_here, group_size, HD)
    cache_key = kv_cache[0].reshape(ROWS_DEV, slots, heads_here, HD)
    cache_value = kv_cache[1].reshape(ROWS_DEV, slots, heads_here, HD)
    tail_key = rebuilt_key.reshape(LC, heads_here, HD)
    tail_value = rebuilt_value.reshape(LC, heads_here, HD)
    live = jnp.arange(slots, dtype=jnp.int32)[None, :] < cache_len[:, None]
    dot = lambda spec, a, b: jnp.einsum(spec, a, b, preferred_element_type=jnp.float32)
    s_cache = dot("bkgd,blkd->bkgl", grouped, cache_key) * scale
    s_cache = jnp.where(live[:, None, None, :], s_cache, -jnp.inf)
    s_tail = dot("bkgd,tkd->bkgt", grouped, tail_key) * scale
    s_tail = jnp.where(resumed[:, None, None, None], s_tail, -jnp.inf)
    s_self = dot("bkgd,bkd->bkg", grouped, key_rot) * scale
    highest = jnp.maximum(jnp.maximum(jnp.max(s_cache, axis=-1), jnp.max(s_tail, axis=-1)), s_self)
    e_cache = jnp.exp(s_cache - highest[..., None])
    e_tail = jnp.exp(s_tail - highest[..., None])
    e_self = jnp.exp(s_self - highest)
    denominator = jnp.sum(e_cache, axis=-1) + jnp.sum(e_tail, axis=-1) + e_self
    w_cache = (e_cache / denominator[..., None]).astype(jnp.bfloat16)
    w_tail = (e_tail / denominator[..., None]).astype(jnp.bfloat16)
    w_self = (e_self / denominator).astype(jnp.bfloat16)
    attn = dot("bkgl,blkd->bkgd", w_cache, cache_value)
    attn = attn + dot("bkgt,tkd->bkgd", w_tail, tail_value)
    attn = (
        attn + w_self.astype(jnp.float32)[..., None] * value_new.astype(jnp.float32)[:, :, None, :]
    )
    attn = attn.reshape(ROWS_DEV, query_cols).astype(jnp.bfloat16)

    attn_all = gather(attn, "gx").reshape(owners * ROWS_DEV, query_cols)
    out_part = jnp.dot(attn_all, w_out, preferred_element_type=jnp.float32)
    out_part = out_part.reshape(lax.axis_size("gy"), -1, w_out.shape[1])
    mixed = scatter_sum(lambda d: lax.dynamic_index_in_dim(out_part, d, 0, False), "gy")
    return (mixed.astype(jnp.bfloat16), rebuilt_key[None], rebuilt_value[None])


CHUNK = 512
ROW_TILE = 48
PAY = 128
VALUES = 48
QUERY = 96
F32 = jnp.float32
BF16 = jnp.bfloat16


def whole(space=pltpu.VMEM):
    return pl.BlockSpec(memory_space=space)


def params(limit):
    return pltpu.CompilerParams(vmem_limit_bytes=limit * 1024 * 1024)


def cost(flops, bytes_accessed):
    return pl.CostEstimate(flops=flops, bytes_accessed=bytes_accessed, transcendentals=0)


def exchange_tag():
    return lax.axis_index("gx") ^ lax.axis_index("gy")


def angle_kernel(len_ref, cos_ref, sin_ref):
    first, second = len_ref[0], len_ref[1]
    row = lax.broadcasted_iota(jnp.int32, (PAY, HD), 0)
    lane = lax.broadcasted_iota(jnp.int32, (PAY, HD), 1)
    resumed = (row == LC) | ((row >= QUERY) & (row < QUERY + 16))
    other = (row == LC + 1) | (row >= QUERY + 16)
    position = jnp.where(row < LC, first + row, 0)
    position = jnp.where(resumed, first + LC, jnp.where(other, second, position))
    half = lax.rem(lane, HD // 2).astype(F32)
    frequency = jnp.exp(half * (-2.0 * math.log(BASE) / HD))
    angle = position.astype(F32) * frequency
    sine = jnp.sin(angle)
    cos_ref[...] = jnp.cos(angle)
    sin_ref[...] = jnp.where(lane < HD // 2, -sine, sine)


def query_kernel(b0, b1, b2, b3, w_hbm, out_ref, w, acc, sems):
    copies = []
    for c in range(w.shape[0] // CHUNK):
        rows = pl.ds(c * CHUNK, CHUNK)
        copy = pltpu.make_async_copy(w_hbm.at[rows], w.at[rows], sems.at[c])
        copy.start()
        copies.append(copy)
    lhs = jnp.concatenate([b[...].astype(F32) for b in (b0, b1, b2, b3)], axis=0).astype(BF16)
    for c, copy in enumerate(copies):
        copy.wait()
        rows = slice(c * CHUNK, (c + 1) * CHUNK)
        part = jnp.dot(lhs[:, rows], w[rows, :], preferred_element_type=F32)
        acc[...] = part if c == 0 else acc[...] + part
    for r in range(acc.shape[0]):
        for h in range(out_ref.shape[1]):
            out_ref[r, pl.ds(h, 1), :] = acc[pl.ds(r, 1), pl.ds(h * HD, HD)]


def payload_kernel(
    owner_ref, s0, s1, s2, s3, b0, b1, b2, b3, wk, wv, q_ref, o0, o1, o2, o3, x, pay
):
    gx, gy = lax.axis_index("gx"), lax.axis_index("gy")
    stored = (s0, s1, s2, s3)
    for k, s in enumerate(stored):
        x[pl.ds(k * ROW_TILE, LC), :] = s[...]
    fresh = [b[...].astype(F32) for b in (b0, b1, b2, b3)]
    fresh.append(jnp.zeros((8, x.shape[1]), F32))
    base = len(stored) * ROW_TILE
    x[pl.ds(base, 16), :] = jnp.concatenate(fresh, axis=0).astype(BF16)
    key = jnp.zeros((x.shape[0], HD), F32)
    value = key
    for c in range(x.shape[1] // CHUNK):
        rows = slice(c * CHUNK, (c + 1) * CHUNK)
        lhs = x[:, rows]
        key += jnp.dot(lhs, wk[rows, :], preferred_element_type=F32)
        value += jnp.dot(lhs, wv[rows, :], preferred_element_type=F32)
    empty = jnp.zeros((8 - ROWS_DEV, HD), F32)
    for k in range(len(stored)):
        rows = slice(k * ROW_TILE, k * ROW_TILE + LC)
        target = owner_ref[gy ^ k] ^ gx
        pay[target, pl.ds(0, LC), :] = key[rows]
        pay[target, pl.ds(VALUES, LC), :] = value[rows]
        rows = slice(base + k * ROWS_DEV, base + (k + 1) * ROWS_DEV)
        target = k ^ gx ^ gy
        pay[target, pl.ds(LC, 8), :] = jnp.concatenate([key[rows], empty], axis=0)
        pay[target, pl.ds(VALUES + LC, 8), :] = jnp.concatenate([value[rows], empty], axis=0)
        for r in range(ROWS_DEV):
            pay[target, pl.ds(QUERY + 16 * r, 16), :] = q_ref[k * ROWS_DEV + r]
    o0[...] = pay[0]
    o1[...] = pay[1].astype(BF16)
    o2[...] = pay[2].astype(BF16)
    o3[...] = pay[3].astype(BF16)


def attend_kernel(
    len_ref, p0, p1, p2, p3, cos_ref, sin_ref, kv, key_out, value_out, attn_out, attn
):
    total = p0[...] + p1[...].astype(F32) + p2[...].astype(F32) + p3[...].astype(F32)
    turned = total * cos_ref[...] + pltpu.roll(total, HD // 2, 1) * sin_ref[...]
    turned = turned.astype(BF16)
    key_out[...] = turned[:LC]
    value_out[...] = turned[VALUES : VALUES + LC]
    scale = 1.0 / math.sqrt(HD)
    more_key = turned[:VALUES]
    more_value = turned[VALUES:QUERY]
    slots = kv.shape[2]
    contract = (((1,), (1,)), ((), ()))
    for r in range(ROWS_DEV):
        q = turned[QUERY + 16 * r : QUERY + 16 * (r + 1)]
        s = lax.dot_general(q, kv[0, r], contract, preferred_element_type=F32) * scale
        live = lax.broadcasted_iota(jnp.int32, s.shape, 1) < len_ref[r]
        s = jnp.where(live, s, -jnp.inf)
        s_more = lax.dot_general(q, more_key, contract, preferred_element_type=F32) * scale
        lane = lax.broadcasted_iota(jnp.int32, s_more.shape, 1)
        live = lane <= LC if r == 0 else lane == LC + r
        s_more = jnp.where(live, s_more, -jnp.inf)
        highest = jnp.maximum(
            jnp.max(s, axis=1, keepdims=True), jnp.max(s_more, axis=1, keepdims=True)
        )
        e = jnp.exp(s - highest)
        e_more = jnp.exp(s_more - highest)
        total_e = jnp.sum(e, axis=1, keepdims=True) + jnp.sum(e_more, axis=1, keepdims=True)
        out = jnp.dot((e / total_e).astype(BF16), kv[1, r], preferred_element_type=F32)
        out += jnp.dot((e_more / total_e).astype(BF16), more_value, preferred_element_type=F32)
        for h in range(out.shape[0]):
            attn[pl.ds(r, 1), pl.ds(h * HD, HD)] = out[h : h + 1]
    attn_out[...] = attn[...].astype(BF16)


def out_kernel(a0, a1, a2, a3, w_hbm, o0, o1, o2, o3, w, blocks, sems):
    copies = []
    chunk = CHUNK // 2
    for c in range(w.shape[0] // chunk):
        rows = pl.ds(c * chunk, chunk)
        copy = pltpu.make_async_copy(w_hbm.at[rows], w.at[rows], sems.at[c])
        copy.start()
        copies.append(copy)
    tag = exchange_tag()
    for s, a in enumerate((a0, a1, a2, a3)):
        blocks[s ^ tag] = a[...].astype(F32)
    lhs = jnp.concatenate([blocks[k] for k in range(4)], axis=0).astype(BF16)
    acc = jnp.zeros((lhs.shape[0], w.shape[1]), F32)
    for c, copy in enumerate(copies):
        copy.wait()
        rows = slice(c * chunk, (c + 1) * chunk)
        acc += jnp.dot(lhs[:, rows], w[rows, :], preferred_element_type=F32)
    o0[...] = acc[0:2]
    o1[...] = acc[2:4].astype(BF16)
    o2[...] = acc[4:6].astype(BF16)
    o3[...] = acc[6:8].astype(BF16)


def others(blocks, axis):
    return [swap(b, axis, k + 1) for k, b in enumerate(blocks)]


def per_device(stored_rows, new_rows, w_query, w_key, w_value, w_out, kv_cache, cache_len, owner):
    shape = jax.ShapeDtypeStruct
    depth, query_cols = w_query.shape
    width = w_out.shape[1]
    heads = query_cols // HD
    cos, sin = pl.pallas_call(
        angle_kernel,
        out_shape=[shape((PAY, HD), F32)] * 2,
        in_specs=[whole(pltpu.SMEM)],
        out_specs=[whole()] * 2,
        cost_estimate=cost(2000000, 100000),
        name="angles",
    )(cache_len)
    fresh = [new_rows] + others([new_rows] * 3, "gy")
    near = swap(stored_rows, "gy", 1)
    far = swap(stored_rows, "gy", 2)
    far_near = swap(far, "gy", 1)
    stored = [stored_rows, near, far, far_near]
    query = pl.pallas_call(
        query_kernel,
        out_shape=shape((4 * ROWS_DEV, heads, HD), F32),
        in_specs=[whole()] * 4 + [whole(pl.ANY)],
        out_specs=whole(),
        scratch_shapes=[
            pltpu.VMEM((depth, query_cols), BF16),
            pltpu.VMEM((4 * ROWS_DEV, query_cols), F32),
            pltpu.SemaphoreType.DMA((depth // CHUNK,)),
        ],
        compiler_params=params(28),
        cost_estimate=cost(2 * 8 * depth * query_cols, 2 * depth * query_cols),
        name="query",
    )(*fresh, w_query)
    payload = pl.pallas_call(
        payload_kernel,
        out_shape=[shape((PAY, HD), F32)] + [shape((PAY, HD), BF16)] * 3,
        in_specs=[whole(pltpu.SMEM)] + [whole()] * 11,
        out_specs=[whole()] * 4,
        scratch_shapes=[
            pltpu.VMEM((4 * ROW_TILE + 16, depth), BF16),
            pltpu.VMEM((4, PAY, HD), F32),
        ],
        compiler_params=params(28),
        cost_estimate=cost(2 * 208 * depth * 256, 4 * depth * HD),
        name="payload",
    )(owner, *stored, *fresh, w_key, w_value, query)
    sums = [payload[0]] + others(payload[1:], "gx")
    rebuilt_key, rebuilt_value, attn = pl.pallas_call(
        attend_kernel,
        out_shape=[shape((LC, HD), BF16)] * 2 + [shape((ROWS_DEV, query_cols), BF16)],
        in_specs=[whole(pltpu.SMEM)] + [whole()] * 7,
        out_specs=[whole()] * 3,
        scratch_shapes=[pltpu.VMEM((ROWS_DEV, query_cols), F32)],
        compiler_params=params(28),
        cost_estimate=cost(10000000, 1000000),
        name="attend",
    )(cache_len, *sums, cos, sin, kv_cache)
    attn_all = [attn] + others([attn] * 3, "gx")
    parts = pl.pallas_call(
        out_kernel,
        out_shape=[shape((ROWS_DEV, width), F32)] + [shape((ROWS_DEV, width), BF16)] * 3,
        in_specs=[whole()] * 4 + [whole(pl.ANY)],
        out_specs=[whole()] * 4,
        scratch_shapes=[
            pltpu.VMEM((query_cols, width), BF16),
            pltpu.VMEM((4, ROWS_DEV, query_cols), F32),
            pltpu.SemaphoreType.DMA((2 * query_cols // CHUNK,)),
        ],
        compiler_params=params(28),
        cost_estimate=cost(2 * 8 * width * query_cols, 2 * width * query_cols),
        name="project",
    )(*attn_all, w_out)
    arrived = others(parts[1:], "gy")
    mixed = parts[0] + arrived[0].astype(F32) + arrived[1].astype(F32) + arrived[2].astype(F32)
    return (mixed.astype(BF16), rebuilt_key[None], rebuilt_value[None])


def solution(mesh):
    direct = mesh.shape["gx"] == 4 and mesh.shape["gy"] == 4
    in_specs = (
        P(("groups", "gy"), "gx"),
        P(("groups", "gy"), "gx"),
        P("gx", "gy"),
        P("gx", "gy"),
        P("gx", "gy"),
        P("gy", "gx"),
        P(None, ("groups", "gx"), None, "gy"),
        P(("groups", "gx")),
        P("groups"),
    )
    out_specs = (
        P(("groups", "gy"), "gx"),
        P(("groups", "gx"), None, "gy"),
        P(("groups", "gx"), None, "gy"),
    )
    return jax.shard_map(
        per_device if direct else general, mesh=mesh, in_specs=in_specs, out_specs=out_specs, check_vma=False
    )
```

```python
import math

import jax
import jax.numpy as jnp
from jax import lax
from jax.experimental import pallas as pl
from jax.experimental.pallas import tpu as pltpu
from jax.sharding import PartitionSpec as P

HD = 128
LC = 40
ROWS_DEV = 2
BASE = 500000.0
DIRECT = 8


def rotate(values, position):
    half = values.shape[-1] // 2
    index_row = jnp.arange(half).astype(jnp.float32)
    frequency = jnp.exp(index_row * (-2.0 * math.log(BASE) / values.shape[-1]))
    angle = position.astype(jnp.float32)[..., None] * frequency
    cosine = jnp.cos(angle)
    sine = jnp.sin(angle)
    first_half = values[..., :half]
    second_half = values[..., half:]
    return jnp.concatenate(
        [first_half * cosine - second_half * sine, second_half * cosine + first_half * sine],
        axis=-1,
    )


def swap(x, axis, k):
    n = lax.axis_size(axis)
    return lax.ppermute(x, axis, [(i, i ^ k) for i in range(n)])


def gather(x, axis):
    n = lax.axis_size(axis)
    if n > DIRECT or n & (n - 1):
        return lax.all_gather(x, axis, axis=0)
    me = lax.axis_index(axis)
    out = jnp.zeros((n,) + x.shape, x.dtype)
    for k in range(n):
        block = x if k == 0 else swap(x, axis, k)
        out = lax.dynamic_update_index_in_dim(out, block, me ^ k, 0)
    return out


def scatter_sum(parts, axis):
    n = lax.axis_size(axis)
    me = lax.axis_index(axis)
    if n > DIRECT or n & (n - 1):
        whole = jnp.stack([parts(d) for d in range(n)])
        return lax.psum_scatter(whole.astype(jnp.float32), axis, scatter_dimension=0)
    total = parts(me).astype(jnp.float32)
    for k in range(1, n):
        total = total + swap(parts(me ^ k).astype(jnp.bfloat16), axis, k).astype(jnp.float32)
    return total


def general(stored_rows, new_rows, w_query, w_key, w_value, w_out, kv_cache, cache_len, owner):
    owners = lax.axis_size("gx")
    key_cols = w_key.shape[1]
    query_cols = w_query.shape[1]
    heads_here = key_cols // HD
    group_size = query_cols // key_cols
    slot_ids = jnp.arange(owners, dtype=jnp.int32)
    inverse = jnp.sum(jnp.where(owner[None, :] == slot_ids[:, None], slot_ids[None, :], 0), axis=1)

    fresh_all = gather(new_rows, "gy").reshape(-1, new_rows.shape[1])
    stored_all = gather(stored_rows, "gy").reshape(owners, LC, stored_rows.shape[1])
    flat = stored_all.reshape(owners * LC, stored_rows.shape[1])
    query_part = jnp.dot(fresh_all, w_query, preferred_element_type=jnp.float32)
    new_key_part = jnp.dot(fresh_all, w_key, preferred_element_type=jnp.float32)
    new_value_part = jnp.dot(fresh_all, w_value, preferred_element_type=jnp.float32)
    key_part = jnp.dot(flat, w_key, preferred_element_type=jnp.float32)
    value_part = jnp.dot(flat, w_value, preferred_element_type=jnp.float32)

    small = jnp.concatenate([query_part, new_key_part, new_value_part], axis=1)
    small = small.reshape(owners, ROWS_DEV, -1)
    large = jnp.concatenate([key_part, value_part], axis=1).reshape(owners, LC, -1)

    small_sum = scatter_sum(lambda d: lax.dynamic_index_in_dim(small, d, 0, False), "gx")
    large_sum = scatter_sum(
        lambda d: lax.dynamic_index_in_dim(
            large, lax.dynamic_index_in_dim(inverse, d, 0, False), 0, False
        ),
        "gx",
    )
    query = small_sum[:, :query_cols]
    fresh_key = small_sum[:, query_cols : query_cols + key_cols]
    fresh_value = small_sum[:, query_cols + key_cols :]
    own_key = large_sum[:, :key_cols]
    own_value = large_sum[:, key_cols:]

    first_len = cache_len[0]
    tail_pos = first_len + jnp.arange(LC, dtype=jnp.int32)
    rebuilt_key = (
        rotate(own_key.reshape(LC, heads_here, HD), tail_pos[:, None])
        .reshape(LC, key_cols)
        .astype(jnp.bfloat16)
    )
    rebuilt_value = own_value.astype(jnp.bfloat16)
    resumed = jnp.arange(ROWS_DEV, dtype=jnp.int32) == 0
    new_pos = cache_len + jnp.where(resumed, LC, 0).astype(jnp.int32)
    query_rot = rotate(query.reshape(ROWS_DEV, query_cols // HD, HD), new_pos[:, None]).astype(
        jnp.bfloat16
    )
    key_rot = rotate(fresh_key.reshape(ROWS_DEV, heads_here, HD), new_pos[:, None]).astype(
        jnp.bfloat16
    )
    value_new = fresh_value.reshape(ROWS_DEV, heads_here, HD).astype(jnp.bfloat16)
    scale = 1.0 / math.sqrt(HD)
    slots = kv_cache.shape[2]
    grouped = query_rot.reshape(ROWS_DEV, heads_here, group_size, HD)
    cache_key = kv_cache[0].reshape(ROWS_DEV, slots, heads_here, HD)
    cache_value = kv_cache[1].reshape(ROWS_DEV, slots, heads_here, HD)
    tail_key = rebuilt_key.reshape(LC, heads_here, HD)
    tail_value = rebuilt_value.reshape(LC, heads_here, HD)
    live = jnp.arange(slots, dtype=jnp.int32)[None, :] < cache_len[:, None]
    dot = lambda spec, a, b: jnp.einsum(spec, a, b, preferred_element_type=jnp.float32)
    s_cache = dot("bkgd,blkd->bkgl", grouped, cache_key) * scale
    s_cache = jnp.where(live[:, None, None, :], s_cache, -jnp.inf)
    s_tail = dot("bkgd,tkd->bkgt", grouped, tail_key) * scale
    s_tail = jnp.where(resumed[:, None, None, None], s_tail, -jnp.inf)
    s_self = dot("bkgd,bkd->bkg", grouped, key_rot) * scale
    highest = jnp.maximum(jnp.maximum(jnp.max(s_cache, axis=-1), jnp.max(s_tail, axis=-1)), s_self)
    e_cache = jnp.exp(s_cache - highest[..., None])
    e_tail = jnp.exp(s_tail - highest[..., None])
    e_self = jnp.exp(s_self - highest)
    denominator = jnp.sum(e_cache, axis=-1) + jnp.sum(e_tail, axis=-1) + e_self
    w_cache = (e_cache / denominator[..., None]).astype(jnp.bfloat16)
    w_tail = (e_tail / denominator[..., None]).astype(jnp.bfloat16)
    w_self = (e_self / denominator).astype(jnp.bfloat16)
    attn = dot("bkgl,blkd->bkgd", w_cache, cache_value)
    attn = attn + dot("bkgt,tkd->bkgd", w_tail, tail_value)
    attn = (
        attn + w_self.astype(jnp.float32)[..., None] * value_new.astype(jnp.float32)[:, :, None, :]
    )
    attn = attn.reshape(ROWS_DEV, query_cols).astype(jnp.bfloat16)

    attn_all = gather(attn, "gx").reshape(owners * ROWS_DEV, query_cols)
    out_part = jnp.dot(attn_all, w_out, preferred_element_type=jnp.float32)
    out_part = out_part.reshape(lax.axis_size("gy"), -1, w_out.shape[1])
    mixed = scatter_sum(lambda d: lax.dynamic_index_in_dim(out_part, d, 0, False), "gy")
    return (mixed.astype(jnp.bfloat16), rebuilt_key[None], rebuilt_value[None])


CHUNK = 512
ROW_TILE = 48
PAY = 128
VALUES = 48
QUERY = 96
F32 = jnp.float32
BF16 = jnp.bfloat16


def whole(space=pltpu.VMEM):
    return pl.BlockSpec(memory_space=space)


def params(limit):
    return pltpu.CompilerParams(vmem_limit_bytes=limit * 1024 * 1024)


def cost(flops, bytes_accessed):
    return pl.CostEstimate(flops=flops, bytes_accessed=bytes_accessed, transcendentals=0)


def angle_kernel(ready, len_ref, cos_ref, sin_ref):
    first, second = len_ref[0], len_ref[1]
    row = lax.broadcasted_iota(jnp.int32, (PAY, HD), 0)
    lane = lax.broadcasted_iota(jnp.int32, (PAY, HD), 1)
    resumed = (row == LC) | ((row >= QUERY) & (row < QUERY + 16))
    other = (row == LC + 1) | (row >= QUERY + 16)
    position = jnp.where(row < LC, first + row, 0)
    position = jnp.where(resumed, first + LC, jnp.where(other, second, position))
    half = lax.rem(lane, HD // 2).astype(F32)
    frequency = jnp.exp(half * (-2.0 * math.log(BASE) / HD))
    angle = position.astype(F32) * frequency
    sine = jnp.sin(angle)
    cos_ref[...] = jnp.cos(angle)
    sin_ref[...] = jnp.where(lane < HD // 2, -sine, sine)


def start_load(source, target, sems, first, pieces):
    copies = []
    rows = source.shape[0] // pieces
    for c in range(pieces):
        part = pl.ds(c * rows, rows)
        copy = pltpu.make_async_copy(source.at[part], target.at[part], sems.at[first + c])
        copy.start()
        copies.append(copy)
    return copies


def load_kernel(wq_hbm, b_hbm, wq, b, sems):
    copies = start_load(wq_hbm, wq, sems, 0, 8)
    copies += start_load(b_hbm, b, sems, 8, 1)
    for copy in copies:
        copy.wait()


def query_kernel(far, b0, b1, b2, b3, w, wk_hbm, wv_hbm, out_ref, wkv, acc, sems):
    copies = start_load(wk_hbm, wkv.at[:, pl.ds(0, HD)], sems, 0, 1)
    copies += start_load(wv_hbm, wkv.at[:, pl.ds(HD, HD)], sems, 1, 1)
    lhs = jnp.concatenate([b[...].astype(F32) for b in (b0, b1, b2, b3)], axis=0).astype(BF16)
    acc[...] = jnp.dot(lhs, w[...], preferred_element_type=F32)
    for r in range(acc.shape[0]):
        for h in range(out_ref.shape[1]):
            out_ref[r, pl.ds(h, 1), :] = acc[pl.ds(r, 1), pl.ds(h * HD, HD)]
    for copy in copies:
        copy.wait()


def payload_kernel(
    owner_ref, s0, s1, s2, s3, b0, b1, b2, b3, wkv, q_ref, out, x, pay
):
    gy = lax.axis_index("gy")
    stored = (s0, s1, s2, s3)
    for k, s in enumerate(stored):
        x[pl.ds(k * ROW_TILE, LC), :] = s[...]
    fresh = [b[...].astype(F32) for b in (b0, b1, b2, b3)]
    fresh.append(jnp.zeros((8, x.shape[1]), F32))
    base = len(stored) * ROW_TILE
    x[pl.ds(base, 16), :] = jnp.concatenate(fresh, axis=0).astype(BF16)
    both = jnp.zeros((x.shape[0], 2 * HD), F32)
    for c in range(x.shape[1] // CHUNK):
        rows = slice(c * CHUNK, (c + 1) * CHUNK)
        both += jnp.dot(x[:, rows], wkv[rows, :], preferred_element_type=F32)
    key, value = both[:, :HD], both[:, HD:]
    empty = jnp.zeros((8 - ROWS_DEV, HD), F32)
    for k in range(len(stored)):
        rows = slice(k * ROW_TILE, k * ROW_TILE + LC)
        target = owner_ref[gy ^ k]
        pay[target, pl.ds(0, LC), :] = key[rows]
        pay[target, pl.ds(VALUES, LC), :] = value[rows]
        rows = slice(base + k * ROWS_DEV, base + (k + 1) * ROWS_DEV)
        target = k ^ gy
        pay[target, pl.ds(LC, 8), :] = jnp.concatenate([key[rows], empty], axis=0)
        pay[target, pl.ds(VALUES + LC, 8), :] = jnp.concatenate([value[rows], empty], axis=0)
        for r in range(ROWS_DEV):
            pay[target, pl.ds(QUERY + 16 * r, 16), :] = q_ref[k * ROWS_DEV + r]
    out[...] = pay[...].astype(BF16)


def attend_kernel(
    len_ref, terms, cos_ref, sin_ref, kv, key_out, value_out, attn_out, attn
):
    total = jnp.sum(terms[...].astype(F32), axis=0)
    turned = total * cos_ref[...] + pltpu.roll(total, HD // 2, 1) * sin_ref[...]
    turned = turned.astype(BF16)
    key_out[...] = turned[:LC]
    value_out[...] = turned[VALUES : VALUES + LC]
    scale = 1.0 / math.sqrt(HD)
    more_key = turned[:VALUES]
    more_value = turned[VALUES:QUERY]
    slots = kv.shape[2]
    contract = (((1,), (1,)), ((), ()))
    for r in range(ROWS_DEV):
        q = turned[QUERY + 16 * r : QUERY + 16 * (r + 1)]
        s = lax.dot_general(q, kv[0, r], contract, preferred_element_type=F32) * scale
        live = lax.broadcasted_iota(jnp.int32, s.shape, 1) < len_ref[r]
        s = jnp.where(live, s, -jnp.inf)
        s_more = lax.dot_general(q, more_key, contract, preferred_element_type=F32) * scale
        lane = lax.broadcasted_iota(jnp.int32, s_more.shape, 1)
        live = lane <= LC if r == 0 else lane == LC + r
        s_more = jnp.where(live, s_more, -jnp.inf)
        highest = jnp.maximum(
            jnp.max(s, axis=1, keepdims=True), jnp.max(s_more, axis=1, keepdims=True)
        )
        e = jnp.exp(s - highest)
        e_more = jnp.exp(s_more - highest)
        total_e = jnp.sum(e, axis=1, keepdims=True) + jnp.sum(e_more, axis=1, keepdims=True)
        out = jnp.dot((e / total_e).astype(BF16), kv[1, r], preferred_element_type=F32)
        out += jnp.dot((e_more / total_e).astype(BF16), more_value, preferred_element_type=F32)
        for h in range(out.shape[0]):
            attn[pl.ds(r, 1), pl.ds(h * HD, HD)] = out[h : h + 1]
    attn_out[...] = attn[...].astype(BF16)


def out_kernel(a0, a1, a2, a3, w, out, blocks):
    gx = lax.axis_index("gx")
    for s, a in enumerate((a0, a1, a2, a3)):
        blocks[s ^ gx] = a[...].astype(F32)
    lhs = jnp.concatenate([blocks[k] for k in range(4)], axis=0).astype(BF16)
    acc = jnp.dot(lhs, w[...], preferred_element_type=F32)
    for k in range(4):
        out[k] = acc[k * ROWS_DEV : (k + 1) * ROWS_DEV].astype(BF16)


def others(blocks, axis):
    return [swap(b, axis, k + 1) for k, b in enumerate(blocks)]


def per_device(stored_rows, new_rows, w_query, w_key, w_value, w_out, kv_cache, cache_len, owner):
    shape = jax.ShapeDtypeStruct
    depth, query_cols = w_query.shape
    width = w_out.shape[1]
    heads = query_cols // HD
    semaphores = pltpu.SemaphoreType.DMA
    in_hbm = lambda x: pltpu.with_memory_space_constraint(x, pltpu.HBM)
    far = swap(stored_rows, "gy", 2)
    near = swap(stored_rows, "gy", 1)
    fresh = others([new_rows] * 3, "gy")
    wq, own_fresh = pl.pallas_call(
        load_kernel,
        out_shape=[pltpu.VMEM((depth, query_cols), BF16), pltpu.VMEM(new_rows.shape, BF16)],
        in_specs=[whole(pltpu.HBM)] * 2,
        out_specs=[whole()] * 2,
        scratch_shapes=[semaphores((9,))],
        compiler_params=params(8),
        cost_estimate=cost(1000, 2 * depth * query_cols),
        name="load",
    )(in_hbm(w_query), in_hbm(new_rows))
    far, own_fresh, *fresh = lax.optimization_barrier((far, own_fresh, *fresh))
    far_near = swap(far, "gy", 1)
    fresh = [own_fresh] + fresh
    stored = [stored_rows, near, far, far_near]
    query, wkv = pl.pallas_call(
        query_kernel,
        out_shape=[
            pltpu.VMEM((4 * ROWS_DEV, heads, HD), F32),
            pltpu.VMEM((depth, 2 * HD), BF16),
        ],
        in_specs=[whole(pl.ANY)] + [whole()] * 5 + [whole(pltpu.HBM)] * 2,
        out_specs=[whole()] * 2,
        scratch_shapes=[pltpu.VMEM((4 * ROWS_DEV, query_cols), F32), semaphores((2,))],
        compiler_params=params(8),
        cost_estimate=cost(2 * 8 * depth * query_cols, 4 * depth * HD),
        name="query",
    )(far, *fresh, wq, in_hbm(w_key), in_hbm(w_value))
    payload = pl.pallas_call(
        payload_kernel,
        out_shape=shape((4, PAY, HD), BF16),
        in_specs=[whole(pltpu.SMEM)] + [whole()] * 10,
        out_specs=whole(),
        scratch_shapes=[
            pltpu.VMEM((4 * ROW_TILE + 16, depth), BF16),
            pltpu.VMEM((4, PAY, HD), F32),
        ],
        compiler_params=params(8),
        cost_estimate=cost(2 * 208 * depth * 256, 4 * depth * HD),
        name="payload",
    )(owner, *stored, *fresh, wkv, query)
    terms = lax.all_to_all(payload, "gx", 0, 0)
    cos, sin = pl.pallas_call(
        angle_kernel,
        out_shape=[pltpu.VMEM((PAY, HD), F32)] * 2,
        in_specs=[whole(pl.ANY), whole(pltpu.SMEM)],
        out_specs=[whole()] * 2,
        cost_estimate=cost(2000000, 100000),
        name="angles",
    )(payload, cache_len)
    rebuilt_key, rebuilt_value, attn = pl.pallas_call(
        attend_kernel,
        out_shape=[shape((LC, HD), BF16)] * 2 + [shape((ROWS_DEV, query_cols), BF16)],
        in_specs=[whole(pltpu.SMEM)] + [whole()] * 4,
        out_specs=[whole()] * 3,
        scratch_shapes=[pltpu.VMEM((ROWS_DEV, query_cols), F32)],
        compiler_params=params(8),
        cost_estimate=cost(10000000, 1000000),
        name="attend",
    )(cache_len, terms, cos, sin, kv_cache)
    attn_all = [attn] + others([attn] * 3, "gx")
    parts = pl.pallas_call(
        out_kernel,
        out_shape=shape((4, ROWS_DEV, width), BF16),
        in_specs=[whole()] * 5,
        out_specs=whole(),
        scratch_shapes=[pltpu.VMEM((4, ROWS_DEV, query_cols), F32)],
        compiler_params=params(8),
        cost_estimate=cost(2 * 8 * width * query_cols, 2 * width * query_cols),
        name="project",
    )(*attn_all, pltpu.with_memory_space_constraint(w_out, pltpu.VMEM))
    arrived = lax.all_to_all(parts, "gy", 0, 0)
    mixed = jnp.sum(arrived.astype(F32), axis=0)
    return (mixed.astype(BF16), rebuilt_key[None], rebuilt_value[None])


def solution(mesh):
    direct = mesh.shape["gx"] == 4 and mesh.shape["gy"] == 4
    in_specs = (
        P(("groups", "gy"), "gx"),
        P(("groups", "gy"), "gx"),
        P("gx", "gy"),
        P("gx", "gy"),
        P("gx", "gy"),
        P("gy", "gx"),
        P(None, ("groups", "gx"), None, "gy"),
        P(("groups", "gx")),
        P("groups"),
    )
    out_specs = (
        P(("groups", "gy"), "gx"),
        P(("groups", "gx"), None, "gy"),
        P(("groups", "gx"), None, "gy"),
    )
    return jax.shard_map(
        per_device if direct else general, mesh=mesh, in_specs=in_specs, out_specs=out_specs, check_vma=False
    )
```

```python
import math

import jax
import jax.numpy as jnp
from jax import lax
from jax.experimental import pallas as pl
from jax.experimental.pallas import tpu as pltpu
from jax.sharding import PartitionSpec as P

HD = 128
LC = 40
ROWS_DEV = 2
BASE = 500000.0
DIRECT = 8


def rotate(values, position):
    half = values.shape[-1] // 2
    index_row = jnp.arange(half).astype(jnp.float32)
    frequency = jnp.exp(index_row * (-2.0 * math.log(BASE) / values.shape[-1]))
    angle = position.astype(jnp.float32)[..., None] * frequency
    cosine = jnp.cos(angle)
    sine = jnp.sin(angle)
    first_half = values[..., :half]
    second_half = values[..., half:]
    return jnp.concatenate(
        [first_half * cosine - second_half * sine, second_half * cosine + first_half * sine],
        axis=-1,
    )


def swap(x, axis, k):
    n = lax.axis_size(axis)
    return lax.ppermute(x, axis, [(i, i ^ k) for i in range(n)])


def gather(x, axis):
    n = lax.axis_size(axis)
    if n > DIRECT or n & (n - 1):
        return lax.all_gather(x, axis, axis=0)
    me = lax.axis_index(axis)
    out = jnp.zeros((n,) + x.shape, x.dtype)
    for k in range(n):
        block = x if k == 0 else swap(x, axis, k)
        out = lax.dynamic_update_index_in_dim(out, block, me ^ k, 0)
    return out


def scatter_sum(parts, axis):
    n = lax.axis_size(axis)
    me = lax.axis_index(axis)
    if n > DIRECT or n & (n - 1):
        whole = jnp.stack([parts(d) for d in range(n)])
        return lax.psum_scatter(whole.astype(jnp.float32), axis, scatter_dimension=0)
    total = parts(me).astype(jnp.float32)
    for k in range(1, n):
        total = total + swap(parts(me ^ k).astype(jnp.bfloat16), axis, k).astype(jnp.float32)
    return total


def general(stored_rows, new_rows, w_query, w_key, w_value, w_out, kv_cache, cache_len, owner):
    owners = lax.axis_size("gx")
    key_cols = w_key.shape[1]
    query_cols = w_query.shape[1]
    heads_here = key_cols // HD
    group_size = query_cols // key_cols
    slot_ids = jnp.arange(owners, dtype=jnp.int32)
    inverse = jnp.sum(jnp.where(owner[None, :] == slot_ids[:, None], slot_ids[None, :], 0), axis=1)

    fresh_all = gather(new_rows, "gy").reshape(-1, new_rows.shape[1])
    stored_all = gather(stored_rows, "gy").reshape(owners, LC, stored_rows.shape[1])
    flat = stored_all.reshape(owners * LC, stored_rows.shape[1])
    query_part = jnp.dot(fresh_all, w_query, preferred_element_type=jnp.float32)
    new_key_part = jnp.dot(fresh_all, w_key, preferred_element_type=jnp.float32)
    new_value_part = jnp.dot(fresh_all, w_value, preferred_element_type=jnp.float32)
    key_part = jnp.dot(flat, w_key, preferred_element_type=jnp.float32)
    value_part = jnp.dot(flat, w_value, preferred_element_type=jnp.float32)

    small = jnp.concatenate([query_part, new_key_part, new_value_part], axis=1)
    small = small.reshape(owners, ROWS_DEV, -1)
    large = jnp.concatenate([key_part, value_part], axis=1).reshape(owners, LC, -1)

    small_sum = scatter_sum(lambda d: lax.dynamic_index_in_dim(small, d, 0, False), "gx")
    large_sum = scatter_sum(
        lambda d: lax.dynamic_index_in_dim(
            large, lax.dynamic_index_in_dim(inverse, d, 0, False), 0, False
        ),
        "gx",
    )
    query = small_sum[:, :query_cols]
    fresh_key = small_sum[:, query_cols : query_cols + key_cols]
    fresh_value = small_sum[:, query_cols + key_cols :]
    own_key = large_sum[:, :key_cols]
    own_value = large_sum[:, key_cols:]

    first_len = cache_len[0]
    tail_pos = first_len + jnp.arange(LC, dtype=jnp.int32)
    rebuilt_key = (
        rotate(own_key.reshape(LC, heads_here, HD), tail_pos[:, None])
        .reshape(LC, key_cols)
        .astype(jnp.bfloat16)
    )
    rebuilt_value = own_value.astype(jnp.bfloat16)
    resumed = jnp.arange(ROWS_DEV, dtype=jnp.int32) == 0
    new_pos = cache_len + jnp.where(resumed, LC, 0).astype(jnp.int32)
    query_rot = rotate(query.reshape(ROWS_DEV, query_cols // HD, HD), new_pos[:, None]).astype(
        jnp.bfloat16
    )
    key_rot = rotate(fresh_key.reshape(ROWS_DEV, heads_here, HD), new_pos[:, None]).astype(
        jnp.bfloat16
    )
    value_new = fresh_value.reshape(ROWS_DEV, heads_here, HD).astype(jnp.bfloat16)
    scale = 1.0 / math.sqrt(HD)
    slots = kv_cache.shape[2]
    grouped = query_rot.reshape(ROWS_DEV, heads_here, group_size, HD)
    cache_key = kv_cache[0].reshape(ROWS_DEV, slots, heads_here, HD)
    cache_value = kv_cache[1].reshape(ROWS_DEV, slots, heads_here, HD)
    tail_key = rebuilt_key.reshape(LC, heads_here, HD)
    tail_value = rebuilt_value.reshape(LC, heads_here, HD)
    live = jnp.arange(slots, dtype=jnp.int32)[None, :] < cache_len[:, None]
    dot = lambda spec, a, b: jnp.einsum(spec, a, b, preferred_element_type=jnp.float32)
    s_cache = dot("bkgd,blkd->bkgl", grouped, cache_key) * scale
    s_cache = jnp.where(live[:, None, None, :], s_cache, -jnp.inf)
    s_tail = dot("bkgd,tkd->bkgt", grouped, tail_key) * scale
    s_tail = jnp.where(resumed[:, None, None, None], s_tail, -jnp.inf)
    s_self = dot("bkgd,bkd->bkg", grouped, key_rot) * scale
    highest = jnp.maximum(jnp.maximum(jnp.max(s_cache, axis=-1), jnp.max(s_tail, axis=-1)), s_self)
    e_cache = jnp.exp(s_cache - highest[..., None])
    e_tail = jnp.exp(s_tail - highest[..., None])
    e_self = jnp.exp(s_self - highest)
    denominator = jnp.sum(e_cache, axis=-1) + jnp.sum(e_tail, axis=-1) + e_self
    w_cache = (e_cache / denominator[..., None]).astype(jnp.bfloat16)
    w_tail = (e_tail / denominator[..., None]).astype(jnp.bfloat16)
    w_self = (e_self / denominator).astype(jnp.bfloat16)
    attn = dot("bkgl,blkd->bkgd", w_cache, cache_value)
    attn = attn + dot("bkgt,tkd->bkgd", w_tail, tail_value)
    attn = (
        attn + w_self.astype(jnp.float32)[..., None] * value_new.astype(jnp.float32)[:, :, None, :]
    )
    attn = attn.reshape(ROWS_DEV, query_cols).astype(jnp.bfloat16)

    attn_all = gather(attn, "gx").reshape(owners * ROWS_DEV, query_cols)
    out_part = jnp.dot(attn_all, w_out, preferred_element_type=jnp.float32)
    out_part = out_part.reshape(lax.axis_size("gy"), -1, w_out.shape[1])
    mixed = scatter_sum(lambda d: lax.dynamic_index_in_dim(out_part, d, 0, False), "gy")
    return (mixed.astype(jnp.bfloat16), rebuilt_key[None], rebuilt_value[None])


CHUNK = 512
ROW_TILE = 48
PAY = 128
VALUES = 48
QUERY = 96
F32 = jnp.float32
BF16 = jnp.bfloat16


def whole(space=pltpu.VMEM):
    return pl.BlockSpec(memory_space=space)


def params(limit):
    return pltpu.CompilerParams(vmem_limit_bytes=limit * 1024 * 1024)


def cost(flops, bytes_accessed):
    return pl.CostEstimate(flops=flops, bytes_accessed=bytes_accessed, transcendentals=0)


def angles(len_ref, cos_ref, sin_ref):
    first, second = len_ref[0], len_ref[1]
    row = lax.broadcasted_iota(jnp.int32, (PAY, HD), 0)
    lane = lax.broadcasted_iota(jnp.int32, (PAY, HD), 1)
    resumed = (row == LC) | ((row >= QUERY) & (row < QUERY + 16))
    other = (row == LC + 1) | (row >= QUERY + 16)
    position = jnp.where(row < LC, first + row, 0)
    position = jnp.where(resumed, first + LC, jnp.where(other, second, position))
    half = lax.rem(lane, HD // 2).astype(F32)
    frequency = jnp.exp(half * (-2.0 * math.log(BASE) / HD))
    angle = position.astype(F32) * frequency
    sine = jnp.sin(angle)
    cos_ref[...] = jnp.cos(angle)
    sin_ref[...] = jnp.where(lane < HD // 2, -sine, sine)


def start_load(source, target, sems, first, pieces):
    copies = []
    rows = source.shape[0] // pieces
    for c in range(pieces):
        part = pl.ds(c * rows, rows)
        copy = pltpu.make_async_copy(source.at[part], target.at[part], sems.at[first + c])
        copy.start()
        copies.append(copy)
    return copies


def load_kernel(wo_hbm, wk_hbm, wv_hbm, b_hbm, wo, wkv, b, sems):
    copies = start_load(b_hbm, b, sems, 0, 1)
    copies += start_load(wk_hbm, wkv.at[:, pl.ds(0, HD)], sems, 1, 1)
    copies += start_load(wv_hbm, wkv.at[:, pl.ds(HD, HD)], sems, 2, 1)
    copies += start_load(wo_hbm.at[pl.ds(0, wo.shape[0])], wo, sems, 3, 2)
    for copy in copies:
        copy.wait()


def query_kernel(far, b0, b1, b2, b3, w, wo_hbm, out_ref, wo, acc, sems):
    rows = wo.shape[0]
    copies = start_load(wo_hbm.at[pl.ds(rows, rows)], wo, sems, 0, 2)
    lhs = jnp.concatenate([b[...].astype(F32) for b in (b0, b1, b2, b3)], axis=0).astype(BF16)
    acc[...] = jnp.dot(lhs, w[...], preferred_element_type=F32)
    for r in range(acc.shape[0]):
        for h in range(out_ref.shape[1]):
            out_ref[r, pl.ds(h, 1), :] = acc[pl.ds(r, 1), pl.ds(h * HD, HD)]
    for copy in copies:
        copy.wait()


def rest_kernel(ready, len_ref, wo_hbm, cos_ref, sin_ref, wo, sems):
    rows = wo.shape[0]
    copies = start_load(wo_hbm.at[pl.ds(wo_hbm.shape[0] - rows, rows)], wo, sems, 0, 4)
    angles(len_ref, cos_ref, sin_ref)
    for copy in copies:
        copy.wait()


def payload_kernel(
    owner_ref, s0, s1, s2, s3, b0, b1, b2, b3, wkv, q_ref, o0, o1, o2, o3, x, pay
):
    gx, gy = lax.axis_index("gx"), lax.axis_index("gy")
    stored = (s0, s1, s2, s3)
    for k, s in enumerate(stored):
        x[pl.ds(k * ROW_TILE, LC), :] = s[...]
    fresh = [b[...].astype(F32) for b in (b0, b1, b2, b3)]
    fresh.append(jnp.zeros((8, x.shape[1]), F32))
    base = len(stored) * ROW_TILE
    x[pl.ds(base, 16), :] = jnp.concatenate(fresh, axis=0).astype(BF16)
    both = jnp.zeros((x.shape[0], 2 * HD), F32)
    for c in range(x.shape[1] // CHUNK):
        rows = slice(c * CHUNK, (c + 1) * CHUNK)
        both += jnp.dot(x[:, rows], wkv[rows, :], preferred_element_type=F32)
    key, value = both[:, :HD], both[:, HD:]
    empty = jnp.zeros((8 - ROWS_DEV, HD), F32)
    for k in range(len(stored)):
        rows = slice(k * ROW_TILE, k * ROW_TILE + LC)
        target = owner_ref[gy ^ k] ^ gx
        pay[target, pl.ds(0, LC), :] = key[rows]
        pay[target, pl.ds(VALUES, LC), :] = value[rows]
        rows = slice(base + k * ROWS_DEV, base + (k + 1) * ROWS_DEV)
        target = k ^ gx ^ gy
        pay[target, pl.ds(LC, 8), :] = jnp.concatenate([key[rows], empty], axis=0)
        pay[target, pl.ds(VALUES + LC, 8), :] = jnp.concatenate([value[rows], empty], axis=0)
        for r in range(ROWS_DEV):
            pay[target, pl.ds(QUERY + 16 * r, 16), :] = q_ref[k * ROWS_DEV + r]
    o0[...] = pay[0]
    o1[...] = pay[1].astype(BF16)
    o2[...] = pay[2].astype(BF16)
    o3[...] = pay[3].astype(BF16)


def attend_kernel(
    len_ref, ready, p0, p1, p2, p3, cos_ref, sin_ref, kv, key_out, value_out, attn_out, attn
):
    total = p0[...] + p1[...].astype(F32) + p2[...].astype(F32) + p3[...].astype(F32)
    turned = total * cos_ref[...] + pltpu.roll(total, HD // 2, 1) * sin_ref[...]
    turned = turned.astype(BF16)
    key_out[...] = turned[:LC]
    value_out[...] = turned[VALUES : VALUES + LC]
    scale = 1.0 / math.sqrt(HD)
    more_key = turned[:VALUES]
    more_value = turned[VALUES:QUERY]
    slots = kv.shape[2]
    contract = (((1,), (1,)), ((), ()))
    for r in range(ROWS_DEV):
        q = turned[QUERY + 16 * r : QUERY + 16 * (r + 1)]
        s = lax.dot_general(q, kv[0, r], contract, preferred_element_type=F32) * scale
        live = lax.broadcasted_iota(jnp.int32, s.shape, 1) < len_ref[r]
        s = jnp.where(live, s, -jnp.inf)
        s_more = lax.dot_general(q, more_key, contract, preferred_element_type=F32) * scale
        lane = lax.broadcasted_iota(jnp.int32, s_more.shape, 1)
        live = lane <= LC if r == 0 else lane == LC + r
        s_more = jnp.where(live, s_more, -jnp.inf)
        highest = jnp.maximum(
            jnp.max(s, axis=1, keepdims=True), jnp.max(s_more, axis=1, keepdims=True)
        )
        e = jnp.exp(s - highest)
        e_more = jnp.exp(s_more - highest)
        total_e = jnp.sum(e, axis=1, keepdims=True) + jnp.sum(e_more, axis=1, keepdims=True)
        out = jnp.dot((e / total_e).astype(BF16), kv[1, r], preferred_element_type=F32)
        out += jnp.dot((e_more / total_e).astype(BF16), more_value, preferred_element_type=F32)
        for h in range(out.shape[0]):
            attn[pl.ds(r, 1), pl.ds(h * HD, HD)] = out[h : h + 1]
    attn_out[...] = attn[...].astype(BF16)


def out_kernel(a0, a1, a2, a3, w0, w1, w2, o0, o1, o2, o3, blocks):
    tag = lax.axis_index("gx") ^ lax.axis_index("gy")
    for s, a in enumerate((a0, a1, a2, a3)):
        blocks[s ^ tag] = a[...].astype(F32)
    lhs = jnp.concatenate([blocks[k] for k in range(4)], axis=0).astype(BF16)
    first = 0
    acc = jnp.zeros((lhs.shape[0], w0.shape[1]), F32)
    for w in (w0, w1, w2):
        last = first + w.shape[0]
        acc += jnp.dot(lhs[:, first:last], w[...], preferred_element_type=F32)
        first = last
    o0[...] = acc[0:2]
    o1[...] = acc[2:4].astype(BF16)
    o2[...] = acc[4:6].astype(BF16)
    o3[...] = acc[6:8].astype(BF16)


def others(blocks, axis):
    return [swap(b, axis, k + 1) for k, b in enumerate(blocks)]


def per_device(stored_rows, new_rows, w_query, w_key, w_value, w_out, kv_cache, cache_len, owner):
    shape = jax.ShapeDtypeStruct
    depth, query_cols = w_query.shape
    width = w_out.shape[1]
    heads = query_cols // HD
    cut = query_cols * 5 // 16
    semaphores = pltpu.SemaphoreType.DMA
    in_vmem = lambda x: pltpu.with_memory_space_constraint(x, pltpu.VMEM)
    in_hbm = lambda x: pltpu.with_memory_space_constraint(x, pltpu.HBM)
    far = swap(stored_rows, "gy", 2)
    near = swap(stored_rows, "gy", 1)
    fresh = others([new_rows] * 3, "gy")
    wo_first, wkv, own_fresh = pl.pallas_call(
        load_kernel,
        out_shape=[
            pltpu.VMEM((cut, width), BF16),
            pltpu.VMEM((depth, 2 * HD), BF16),
            pltpu.VMEM(new_rows.shape, BF16),
        ],
        in_specs=[whole(pltpu.HBM)] * 4,
        out_specs=[whole()] * 3,
        scratch_shapes=[semaphores((5,))],
        compiler_params=params(4),
        cost_estimate=cost(1000, 2 * depth * query_cols),
        name="load",
    )(in_hbm(w_out), in_hbm(w_key), in_hbm(w_value), in_hbm(new_rows))
    far, own_fresh, *fresh = lax.optimization_barrier((far, own_fresh, *fresh))
    far_near = swap(far, "gy", 1)
    fresh = [own_fresh] + fresh
    stored = [stored_rows, near, far, far_near]
    query, wo_second = pl.pallas_call(
        query_kernel,
        out_shape=[
            pltpu.VMEM((4 * ROWS_DEV, heads, HD), F32),
            pltpu.VMEM((cut, width), BF16),
        ],
        in_specs=[whole(pl.ANY)] + [whole()] * 5 + [whole(pltpu.HBM)],
        out_specs=[whole()] * 2,
        scratch_shapes=[pltpu.VMEM((4 * ROWS_DEV, query_cols), F32), semaphores((2,))],
        compiler_params=params(4),
        cost_estimate=cost(2 * 8 * depth * query_cols, 4 * depth * HD),
        name="query",
    )(far, *fresh, in_vmem(w_query), in_hbm(w_out))
    payload = pl.pallas_call(
        payload_kernel,
        out_shape=[shape((PAY, HD), F32)] + [shape((PAY, HD), BF16)] * 3,
        in_specs=[whole(pltpu.SMEM)] + [whole()] * 10,
        out_specs=[whole()] * 4,
        scratch_shapes=[
            pltpu.VMEM((4 * ROW_TILE + 16, depth), BF16),
            pltpu.VMEM((4, PAY, HD), F32),
        ],
        compiler_params=params(8),
        cost_estimate=cost(2 * 208 * depth * 256, 4 * depth * HD),
        name="payload",
    )(owner, *stored, *fresh, wkv, query)
    sums = [payload[0]] + others(payload[1:], "gx")
    cos, sin, wo_third = pl.pallas_call(
        rest_kernel,
        out_shape=[pltpu.VMEM((PAY, HD), F32)] * 2
        + [pltpu.VMEM((query_cols - 2 * cut, width), BF16)],
        in_specs=[whole(pl.ANY), whole(pltpu.SMEM), whole(pltpu.HBM)],
        out_specs=[whole()] * 3,
        scratch_shapes=[semaphores((4,))],
        compiler_params=params(4),
        cost_estimate=cost(2000000, 2 * (query_cols - 2 * cut) * width),
        name="rest",
    )(payload[0], cache_len, in_hbm(w_out))
    rebuilt_key, rebuilt_value, attn = pl.pallas_call(
        attend_kernel,
        out_shape=[shape((LC, HD), BF16)] * 2 + [shape((ROWS_DEV, query_cols), BF16)],
        in_specs=[whole(pltpu.SMEM), whole(pl.ANY)] + [whole()] * 7,
        out_specs=[whole()] * 3,
        scratch_shapes=[pltpu.VMEM((ROWS_DEV, query_cols), F32)],
        compiler_params=params(4),
        cost_estimate=cost(10000000, 1000000),
        name="attend",
    )(cache_len, wo_third, *sums, cos, sin, kv_cache)
    attn_all = [attn] + others([attn] * 3, "gx")
    parts = pl.pallas_call(
        out_kernel,
        out_shape=[shape((ROWS_DEV, width), F32)] + [shape((ROWS_DEV, width), BF16)] * 3,
        in_specs=[whole()] * 7,
        out_specs=[whole()] * 4,
        scratch_shapes=[pltpu.VMEM((4, ROWS_DEV, query_cols), F32)],
        compiler_params=params(4),
        cost_estimate=cost(2 * 8 * width * query_cols, 2 * width * query_cols),
        name="project",
    )(*attn_all, wo_first, wo_second, wo_third)
    arrived = others(parts[1:], "gy")
    mixed = parts[0] + arrived[0].astype(F32) + arrived[1].astype(F32) + arrived[2].astype(F32)
    return (mixed.astype(BF16), rebuilt_key[None], rebuilt_value[None])


def solution(mesh):
    direct = mesh.shape["gx"] == 4 and mesh.shape["gy"] == 4
    in_specs = (
        P(("groups", "gy"), "gx"),
        P(("groups", "gy"), "gx"),
        P("gx", "gy"),
        P("gx", "gy"),
        P("gx", "gy"),
        P("gy", "gx"),
        P(None, ("groups", "gx"), None, "gy"),
        P(("groups", "gx")),
        P("groups"),
    )
    out_specs = (
        P(("groups", "gy"), "gx"),
        P(("groups", "gx"), None, "gy"),
        P(("groups", "gx"), None, "gy"),
    )
    return jax.shard_map(
        per_device if direct else general, mesh=mesh, in_specs=in_specs, out_specs=out_specs, check_vma=False
    )
```

```python
import math

import jax
import jax.numpy as jnp
from jax import lax
from jax.experimental import pallas as pl
from jax.experimental.pallas import tpu as pltpu
from jax.sharding import PartitionSpec as P

HD = 128
LC = 40
ROWS_DEV = 2
BASE = 500000.0
DIRECT = 8


def rotate(values, position):
    half = values.shape[-1] // 2
    index_row = jnp.arange(half).astype(jnp.float32)
    frequency = jnp.exp(index_row * (-2.0 * math.log(BASE) / values.shape[-1]))
    angle = position.astype(jnp.float32)[..., None] * frequency
    cosine = jnp.cos(angle)
    sine = jnp.sin(angle)
    first_half = values[..., :half]
    second_half = values[..., half:]
    return jnp.concatenate(
        [first_half * cosine - second_half * sine, second_half * cosine + first_half * sine],
        axis=-1,
    )


def swap(x, axis, k):
    n = lax.axis_size(axis)
    return lax.ppermute(x, axis, [(i, i ^ k) for i in range(n)])


def gather(x, axis):
    n = lax.axis_size(axis)
    if n > DIRECT or n & (n - 1):
        return lax.all_gather(x, axis, axis=0)
    me = lax.axis_index(axis)
    out = jnp.zeros((n,) + x.shape, x.dtype)
    for k in range(n):
        block = x if k == 0 else swap(x, axis, k)
        out = lax.dynamic_update_index_in_dim(out, block, me ^ k, 0)
    return out


def scatter_sum(parts, axis):
    n = lax.axis_size(axis)
    me = lax.axis_index(axis)
    if n > DIRECT or n & (n - 1):
        whole = jnp.stack([parts(d) for d in range(n)])
        return lax.psum_scatter(whole.astype(jnp.float32), axis, scatter_dimension=0)
    total = parts(me).astype(jnp.float32)
    for k in range(1, n):
        total = total + swap(parts(me ^ k).astype(jnp.bfloat16), axis, k).astype(jnp.float32)
    return total


def general(stored_rows, new_rows, w_query, w_key, w_value, w_out, kv_cache, cache_len, owner):
    owners = lax.axis_size("gx")
    key_cols = w_key.shape[1]
    query_cols = w_query.shape[1]
    heads_here = key_cols // HD
    group_size = query_cols // key_cols
    slot_ids = jnp.arange(owners, dtype=jnp.int32)
    inverse = jnp.sum(jnp.where(owner[None, :] == slot_ids[:, None], slot_ids[None, :], 0), axis=1)

    fresh_all = gather(new_rows, "gy").reshape(-1, new_rows.shape[1])
    stored_all = gather(stored_rows, "gy").reshape(owners, LC, stored_rows.shape[1])
    flat = stored_all.reshape(owners * LC, stored_rows.shape[1])
    query_part = jnp.dot(fresh_all, w_query, preferred_element_type=jnp.float32)
    new_key_part = jnp.dot(fresh_all, w_key, preferred_element_type=jnp.float32)
    new_value_part = jnp.dot(fresh_all, w_value, preferred_element_type=jnp.float32)
    key_part = jnp.dot(flat, w_key, preferred_element_type=jnp.float32)
    value_part = jnp.dot(flat, w_value, preferred_element_type=jnp.float32)

    small = jnp.concatenate([query_part, new_key_part, new_value_part], axis=1)
    small = small.reshape(owners, ROWS_DEV, -1)
    large = jnp.concatenate([key_part, value_part], axis=1).reshape(owners, LC, -1)

    small_sum = scatter_sum(lambda d: lax.dynamic_index_in_dim(small, d, 0, False), "gx")
    large_sum = scatter_sum(
        lambda d: lax.dynamic_index_in_dim(
            large, lax.dynamic_index_in_dim(inverse, d, 0, False), 0, False
        ),
        "gx",
    )
    query = small_sum[:, :query_cols]
    fresh_key = small_sum[:, query_cols : query_cols + key_cols]
    fresh_value = small_sum[:, query_cols + key_cols :]
    own_key = large_sum[:, :key_cols]
    own_value = large_sum[:, key_cols:]

    first_len = cache_len[0]
    tail_pos = first_len + jnp.arange(LC, dtype=jnp.int32)
    rebuilt_key = (
        rotate(own_key.reshape(LC, heads_here, HD), tail_pos[:, None])
        .reshape(LC, key_cols)
        .astype(jnp.bfloat16)
    )
    rebuilt_value = own_value.astype(jnp.bfloat16)
    resumed = jnp.arange(ROWS_DEV, dtype=jnp.int32) == 0
    new_pos = cache_len + jnp.where(resumed, LC, 0).astype(jnp.int32)
    query_rot = rotate(query.reshape(ROWS_DEV, query_cols // HD, HD), new_pos[:, None]).astype(
        jnp.bfloat16
    )
    key_rot = rotate(fresh_key.reshape(ROWS_DEV, heads_here, HD), new_pos[:, None]).astype(
        jnp.bfloat16
    )
    value_new = fresh_value.reshape(ROWS_DEV, heads_here, HD).astype(jnp.bfloat16)
    scale = 1.0 / math.sqrt(HD)
    slots = kv_cache.shape[2]
    grouped = query_rot.reshape(ROWS_DEV, heads_here, group_size, HD)
    cache_key = kv_cache[0].reshape(ROWS_DEV, slots, heads_here, HD)
    cache_value = kv_cache[1].reshape(ROWS_DEV, slots, heads_here, HD)
    tail_key = rebuilt_key.reshape(LC, heads_here, HD)
    tail_value = rebuilt_value.reshape(LC, heads_here, HD)
    live = jnp.arange(slots, dtype=jnp.int32)[None, :] < cache_len[:, None]
    dot = lambda spec, a, b: jnp.einsum(spec, a, b, preferred_element_type=jnp.float32)
    s_cache = dot("bkgd,blkd->bkgl", grouped, cache_key) * scale
    s_cache = jnp.where(live[:, None, None, :], s_cache, -jnp.inf)
    s_tail = dot("bkgd,tkd->bkgt", grouped, tail_key) * scale
    s_tail = jnp.where(resumed[:, None, None, None], s_tail, -jnp.inf)
    s_self = dot("bkgd,bkd->bkg", grouped, key_rot) * scale
    highest = jnp.maximum(jnp.maximum(jnp.max(s_cache, axis=-1), jnp.max(s_tail, axis=-1)), s_self)
    e_cache = jnp.exp(s_cache - highest[..., None])
    e_tail = jnp.exp(s_tail - highest[..., None])
    e_self = jnp.exp(s_self - highest)
    denominator = jnp.sum(e_cache, axis=-1) + jnp.sum(e_tail, axis=-1) + e_self
    w_cache = (e_cache / denominator[..., None]).astype(jnp.bfloat16)
    w_tail = (e_tail / denominator[..., None]).astype(jnp.bfloat16)
    w_self = (e_self / denominator).astype(jnp.bfloat16)
    attn = dot("bkgl,blkd->bkgd", w_cache, cache_value)
    attn = attn + dot("bkgt,tkd->bkgd", w_tail, tail_value)
    attn = (
        attn + w_self.astype(jnp.float32)[..., None] * value_new.astype(jnp.float32)[:, :, None, :]
    )
    attn = attn.reshape(ROWS_DEV, query_cols).astype(jnp.bfloat16)

    attn_all = gather(attn, "gx").reshape(owners * ROWS_DEV, query_cols)
    out_part = jnp.dot(attn_all, w_out, preferred_element_type=jnp.float32)
    out_part = out_part.reshape(lax.axis_size("gy"), -1, w_out.shape[1])
    mixed = scatter_sum(lambda d: lax.dynamic_index_in_dim(out_part, d, 0, False), "gy")
    return (mixed.astype(jnp.bfloat16), rebuilt_key[None], rebuilt_value[None])


CHUNK = 512
ROW_TILE = 48
PAY = 128
VALUES = 48
QUERY = 96
F32 = jnp.float32
BF16 = jnp.bfloat16


def ring(step):
    return lax.rem(step + 8, 4)


def whole(space=pltpu.VMEM):
    return pl.BlockSpec(memory_space=space)


def params(limit):
    return pltpu.CompilerParams(vmem_limit_bytes=limit * 1024 * 1024)


def cost(flops, bytes_accessed):
    return pl.CostEstimate(flops=flops, bytes_accessed=bytes_accessed, transcendentals=0)


def angles(len_ref, cos_ref, sin_ref):
    first, second = len_ref[0], len_ref[1]
    row = lax.broadcasted_iota(jnp.int32, (PAY, HD), 0)
    lane = lax.broadcasted_iota(jnp.int32, (PAY, HD), 1)
    resumed = (row == LC) | ((row >= QUERY) & (row < QUERY + 16))
    other = (row == LC + 1) | (row >= QUERY + 16)
    position = jnp.where(row < LC, first + row, 0)
    position = jnp.where(resumed, first + LC, jnp.where(other, second, position))
    half = lax.rem(lane, HD // 2).astype(F32)
    frequency = jnp.exp(half * (-2.0 * math.log(BASE) / HD))
    angle = position.astype(F32) * frequency
    sine = jnp.sin(angle)
    cos_ref[...] = jnp.cos(angle)
    sin_ref[...] = jnp.where(lane < HD // 2, -sine, sine)


def start_load(source, target, sems, first, pieces):
    copies = []
    rows = source.shape[0] // pieces
    for c in range(pieces):
        part = pl.ds(c * rows, rows)
        copy = pltpu.make_async_copy(source.at[part], target.at[part], sems.at[first + c])
        copy.start()
        copies.append(copy)
    return copies


def load_kernel(wo_hbm, wk_hbm, wv_hbm, b_hbm, wo, wkv, b, sems):
    copies = start_load(b_hbm, b, sems, 0, 1)
    copies += start_load(wk_hbm, wkv.at[:, pl.ds(0, HD)], sems, 1, 1)
    copies += start_load(wv_hbm, wkv.at[:, pl.ds(HD, HD)], sems, 2, 1)
    copies += start_load(wo_hbm.at[pl.ds(0, wo.shape[0])], wo, sems, 3, 2)
    for copy in copies:
        copy.wait()


def query_kernel(far, b0, b1, b2, b3, w, wo_hbm, out_ref, wo, acc, sems):
    rows = wo.shape[0]
    copies = start_load(wo_hbm.at[pl.ds(2 * rows, rows)], wo, sems, 0, 2)
    lhs = jnp.concatenate([b[...].astype(F32) for b in (b0, b1, b2, b3)], axis=0).astype(BF16)
    acc[...] = jnp.dot(lhs, w[...], preferred_element_type=F32)
    for r in range(acc.shape[0]):
        for h in range(out_ref.shape[1]):
            out_ref[r, pl.ds(h, 1), :] = acc[pl.ds(r, 1), pl.ds(h * HD, HD)]
    for copy in copies:
        copy.wait()


def rest_kernel(ready, len_ref, wo_hbm, cos_ref, sin_ref, wo, sems):
    rows = wo.shape[0]
    copies = start_load(wo_hbm.at[pl.ds(wo_hbm.shape[0] - rows, rows)], wo, sems, 0, 4)
    angles(len_ref, cos_ref, sin_ref)
    for copy in copies:
        copy.wait()


def payload_kernel(
    owner_ref, s0, s1, s2, s3, b0, b1, b2, b3, wkv, q_ref, o0, o1, o2, o3, x, pay
):
    gx, gy = lax.axis_index("gx"), lax.axis_index("gy")
    stored = (s0, s1, s2, s3)
    for k, s in enumerate(stored):
        x[pl.ds(k * ROW_TILE, LC), :] = s[...]
    fresh = [b[...].astype(F32) for b in (b0, b1, b2, b3)]
    fresh.append(jnp.zeros((8, x.shape[1]), F32))
    base = len(stored) * ROW_TILE
    x[pl.ds(base, 16), :] = jnp.concatenate(fresh, axis=0).astype(BF16)
    both = jnp.zeros((x.shape[0], 2 * HD), F32)
    for c in range(x.shape[1] // CHUNK):
        rows = slice(c * CHUNK, (c + 1) * CHUNK)
        both += jnp.dot(x[:, rows], wkv[rows, :], preferred_element_type=F32)
    key, value = both[:, :HD], both[:, HD:]
    empty = jnp.zeros((8 - ROWS_DEV, HD), F32)
    for k in range(len(stored)):
        rows = slice(k * ROW_TILE, k * ROW_TILE + LC)
        target = ring(owner_ref[gy ^ k] - gx)
        pay[target, pl.ds(0, LC), :] = key[rows]
        pay[target, pl.ds(VALUES, LC), :] = value[rows]
        rows = slice(base + k * ROWS_DEV, base + (k + 1) * ROWS_DEV)
        target = ring((gy ^ k) - gx)
        pay[target, pl.ds(LC, 8), :] = jnp.concatenate([key[rows], empty], axis=0)
        pay[target, pl.ds(VALUES + LC, 8), :] = jnp.concatenate([value[rows], empty], axis=0)
        for r in range(ROWS_DEV):
            pay[target, pl.ds(QUERY + 16 * r, 16), :] = q_ref[k * ROWS_DEV + r]
    o0[...] = pay[0]
    o1[...] = pay[1].astype(BF16)
    o2[...] = pay[2].astype(BF16)
    o3[...] = pay[3].astype(BF16)


def attend_kernel(
    len_ref, ready, p0, p1, p2, p3, cos_ref, sin_ref, kv, key_out, value_out, attn_out, attn
):
    total = p0[...] + p1[...].astype(F32) + p2[...].astype(F32) + p3[...].astype(F32)
    turned = total * cos_ref[...] + pltpu.roll(total, HD // 2, 1) * sin_ref[...]
    turned = turned.astype(BF16)
    key_out[...] = turned[:LC]
    value_out[...] = turned[VALUES : VALUES + LC]
    scale = 1.0 / math.sqrt(HD)
    more_key = turned[:VALUES]
    more_value = turned[VALUES:QUERY]
    slots = kv.shape[2]
    contract = (((1,), (1,)), ((), ()))
    for r in range(ROWS_DEV):
        q = turned[QUERY + 16 * r : QUERY + 16 * (r + 1)]
        s = lax.dot_general(q, kv[0, r], contract, preferred_element_type=F32) * scale
        live = lax.broadcasted_iota(jnp.int32, s.shape, 1) < len_ref[r]
        s = jnp.where(live, s, -jnp.inf)
        s_more = lax.dot_general(q, more_key, contract, preferred_element_type=F32) * scale
        lane = lax.broadcasted_iota(jnp.int32, s_more.shape, 1)
        live = lane <= LC if r == 0 else lane == LC + r
        s_more = jnp.where(live, s_more, -jnp.inf)
        highest = jnp.maximum(
            jnp.max(s, axis=1, keepdims=True), jnp.max(s_more, axis=1, keepdims=True)
        )
        e = jnp.exp(s - highest)
        e_more = jnp.exp(s_more - highest)
        total_e = jnp.sum(e, axis=1, keepdims=True) + jnp.sum(e_more, axis=1, keepdims=True)
        out = jnp.dot((e / total_e).astype(BF16), kv[1, r], preferred_element_type=F32)
        out += jnp.dot((e_more / total_e).astype(BF16), more_value, preferred_element_type=F32)
        for h in range(out.shape[0]):
            attn[pl.ds(r, 1), pl.ds(h * HD, HD)] = out[h : h + 1]
    attn_out[...] = attn[...].astype(BF16)


def out_kernel(a0, a1, a2, a3, w0, w1, w2, o0, o1, o2, o3, blocks):
    tag = lax.axis_index("gx") - lax.axis_index("gy")
    for s, a in enumerate((a0, a1, a2, a3)):
        blocks[ring(tag - s)] = a[...].astype(F32)
    lhs = jnp.concatenate([blocks[k] for k in range(4)], axis=0).astype(BF16)
    first = 0
    acc = jnp.zeros((lhs.shape[0], w0.shape[1]), F32)
    for w in (w0, w1, w2):
        last = first + w.shape[0]
        acc += jnp.dot(lhs[:, first:last], w[...], preferred_element_type=F32)
        first = last
    o0[...] = acc[0:2]
    o1[...] = acc[2:4].astype(BF16)
    o2[...] = acc[4:6].astype(BF16)
    o3[...] = acc[6:8].astype(BF16)


def others(blocks, axis):
    return [swap(b, axis, k + 1) for k, b in enumerate(blocks)]


def rotated(blocks, axis):
    n = lax.axis_size(axis)
    return [
        lax.ppermute(b, axis, [(i, (i + k + 1) % n) for i in range(n)])
        for k, b in enumerate(blocks)
    ]


def per_device(stored_rows, new_rows, w_query, w_key, w_value, w_out, kv_cache, cache_len, owner):
    shape = jax.ShapeDtypeStruct
    depth, query_cols = w_query.shape
    width = w_out.shape[1]
    heads = query_cols // HD
    half, quarter = query_cols // 2, query_cols // 4
    semaphores = pltpu.SemaphoreType.DMA
    in_vmem = lambda x: pltpu.with_memory_space_constraint(x, pltpu.VMEM)
    in_hbm = lambda x: pltpu.with_memory_space_constraint(x, pltpu.HBM)
    far = swap(stored_rows, "gy", 2)
    near = swap(stored_rows, "gy", 1)
    fresh = others([new_rows] * 3, "gy")
    wo_first, wkv, own_fresh = pl.pallas_call(
        load_kernel,
        out_shape=[
            pltpu.VMEM((half, width), BF16),
            pltpu.VMEM((depth, 2 * HD), BF16),
            pltpu.VMEM(new_rows.shape, BF16),
        ],
        in_specs=[whole(pltpu.HBM)] * 4,
        out_specs=[whole()] * 3,
        scratch_shapes=[semaphores((5,))],
        compiler_params=params(4),
        cost_estimate=cost(1000, 2 * depth * query_cols),
        name="load",
    )(in_hbm(w_out), in_hbm(w_key), in_hbm(w_value), in_hbm(new_rows))
    far, own_fresh, *fresh = lax.optimization_barrier((far, own_fresh, *fresh))
    far_near = swap(far, "gy", 1)
    fresh = [own_fresh] + fresh
    stored = [stored_rows, near, far, far_near]
    query, wo_second = pl.pallas_call(
        query_kernel,
        out_shape=[
            pltpu.VMEM((4 * ROWS_DEV, heads, HD), F32),
            pltpu.VMEM((quarter, width), BF16),
        ],
        in_specs=[whole(pl.ANY)] + [whole()] * 5 + [whole(pltpu.HBM)],
        out_specs=[whole()] * 2,
        scratch_shapes=[pltpu.VMEM((4 * ROWS_DEV, query_cols), F32), semaphores((2,))],
        compiler_params=params(4),
        cost_estimate=cost(2 * 8 * depth * query_cols, 4 * depth * HD),
        name="query",
    )(far, *fresh, in_vmem(w_query), in_hbm(w_out))
    payload = pl.pallas_call(
        payload_kernel,
        out_shape=[shape((PAY, HD), F32)] + [shape((PAY, HD), BF16)] * 3,
        in_specs=[whole(pltpu.SMEM)] + [whole()] * 10,
        out_specs=[whole()] * 4,
        scratch_shapes=[
            pltpu.VMEM((4 * ROW_TILE + 16, depth), BF16),
            pltpu.VMEM((4, PAY, HD), F32),
        ],
        compiler_params=params(8),
        cost_estimate=cost(2 * 208 * depth * 256, 4 * depth * HD),
        name="payload",
    )(owner, *stored, *fresh, wkv, query)
    sums = [payload[0]] + rotated(payload[1:], "gx")
    cos, sin, wo_third = pl.pallas_call(
        rest_kernel,
        out_shape=[pltpu.VMEM((PAY, HD), F32)] * 2
        + [pltpu.VMEM((quarter, width), BF16)],
        in_specs=[whole(pl.ANY), whole(pltpu.SMEM), whole(pltpu.HBM)],
        out_specs=[whole()] * 3,
        scratch_shapes=[semaphores((4,))],
        compiler_params=params(4),
        cost_estimate=cost(2000000, 2 * quarter * width),
        name="rest",
    )(payload[0], cache_len, in_hbm(w_out))
    rebuilt_key, rebuilt_value, attn = pl.pallas_call(
        attend_kernel,
        out_shape=[shape((LC, HD), BF16)] * 2 + [shape((ROWS_DEV, query_cols), BF16)],
        in_specs=[whole(pltpu.SMEM), whole(pl.ANY)] + [whole()] * 7,
        out_specs=[whole()] * 3,
        scratch_shapes=[pltpu.VMEM((ROWS_DEV, query_cols), F32)],
        compiler_params=params(4),
        cost_estimate=cost(10000000, 1000000),
        name="attend",
    )(cache_len, wo_third, *sums, cos, sin, kv_cache)
    attn_all = [attn] + rotated([attn] * 3, "gx")
    parts = pl.pallas_call(
        out_kernel,
        out_shape=[shape((ROWS_DEV, width), F32)] + [shape((ROWS_DEV, width), BF16)] * 3,
        in_specs=[whole()] * 7,
        out_specs=[whole()] * 4,
        scratch_shapes=[pltpu.VMEM((4, ROWS_DEV, query_cols), F32)],
        compiler_params=params(4),
        cost_estimate=cost(2 * 8 * width * query_cols, 2 * width * query_cols),
        name="project",
    )(*attn_all, wo_first, wo_second, wo_third)
    arrived = rotated(parts[1:], "gy")
    mixed = parts[0] + arrived[0].astype(F32) + arrived[1].astype(F32) + arrived[2].astype(F32)
    return (mixed.astype(BF16), rebuilt_key[None], rebuilt_value[None])


def solution(mesh):
    direct = mesh.shape["gx"] == 4 and mesh.shape["gy"] == 4
    in_specs = (
        P(("groups", "gy"), "gx"),
        P(("groups", "gy"), "gx"),
        P("gx", "gy"),
        P("gx", "gy"),
        P("gx", "gy"),
        P("gy", "gx"),
        P(None, ("groups", "gx"), None, "gy"),
        P(("groups", "gx")),
        P("groups"),
    )
    out_specs = (
        P(("groups", "gy"), "gx"),
        P(("groups", "gx"), None, "gy"),
        P(("groups", "gx"), None, "gy"),
    )
    return jax.shard_map(
        per_device if direct else general, mesh=mesh, in_specs=in_specs, out_specs=out_specs, check_vma=False
    )
```

```python
import math

import jax
import jax.numpy as jnp
from jax import lax
from jax.experimental import pallas as pl
from jax.experimental.pallas import tpu as pltpu
from jax.sharding import PartitionSpec as P

HD = 128
LC = 40
ROWS_DEV = 2
BASE = 500000.0
DIRECT = 8


def rotate(values, position):
    half = values.shape[-1] // 2
    index_row = jnp.arange(half).astype(jnp.float32)
    frequency = jnp.exp(index_row * (-2.0 * math.log(BASE) / values.shape[-1]))
    angle = position.astype(jnp.float32)[..., None] * frequency
    cosine = jnp.cos(angle)
    sine = jnp.sin(angle)
    first_half = values[..., :half]
    second_half = values[..., half:]
    return jnp.concatenate(
        [first_half * cosine - second_half * sine, second_half * cosine + first_half * sine],
        axis=-1,
    )


def swap(x, axis, k):
    n = lax.axis_size(axis)
    return lax.ppermute(x, axis, [(i, i ^ k) for i in range(n)])


def gather(x, axis):
    n = lax.axis_size(axis)
    if n > DIRECT or n & (n - 1):
        return lax.all_gather(x, axis, axis=0)
    me = lax.axis_index(axis)
    out = jnp.zeros((n,) + x.shape, x.dtype)
    for k in range(n):
        block = x if k == 0 else swap(x, axis, k)
        out = lax.dynamic_update_index_in_dim(out, block, me ^ k, 0)
    return out


def scatter_sum(parts, axis):
    n = lax.axis_size(axis)
    me = lax.axis_index(axis)
    if n > DIRECT or n & (n - 1):
        whole = jnp.stack([parts(d) for d in range(n)])
        return lax.psum_scatter(whole.astype(jnp.float32), axis, scatter_dimension=0)
    total = parts(me).astype(jnp.float32)
    for k in range(1, n):
        total = total + swap(parts(me ^ k).astype(jnp.bfloat16), axis, k).astype(jnp.float32)
    return total


def general(stored_rows, new_rows, w_query, w_key, w_value, w_out, kv_cache, cache_len, owner):
    owners = lax.axis_size("gx")
    key_cols = w_key.shape[1]
    query_cols = w_query.shape[1]
    heads_here = key_cols // HD
    group_size = query_cols // key_cols
    slot_ids = jnp.arange(owners, dtype=jnp.int32)
    inverse = jnp.sum(jnp.where(owner[None, :] == slot_ids[:, None], slot_ids[None, :], 0), axis=1)

    fresh_all = gather(new_rows, "gy").reshape(-1, new_rows.shape[1])
    stored_all = gather(stored_rows, "gy").reshape(owners, LC, stored_rows.shape[1])
    flat = stored_all.reshape(owners * LC, stored_rows.shape[1])
    query_part = jnp.dot(fresh_all, w_query, preferred_element_type=jnp.float32)
    new_key_part = jnp.dot(fresh_all, w_key, preferred_element_type=jnp.float32)
    new_value_part = jnp.dot(fresh_all, w_value, preferred_element_type=jnp.float32)
    key_part = jnp.dot(flat, w_key, preferred_element_type=jnp.float32)
    value_part = jnp.dot(flat, w_value, preferred_element_type=jnp.float32)

    small = jnp.concatenate([query_part, new_key_part, new_value_part], axis=1)
    small = small.reshape(owners, ROWS_DEV, -1)
    large = jnp.concatenate([key_part, value_part], axis=1).reshape(owners, LC, -1)

    small_sum = scatter_sum(lambda d: lax.dynamic_index_in_dim(small, d, 0, False), "gx")
    large_sum = scatter_sum(
        lambda d: lax.dynamic_index_in_dim(
            large, lax.dynamic_index_in_dim(inverse, d, 0, False), 0, False
        ),
        "gx",
    )
    query = small_sum[:, :query_cols]
    fresh_key = small_sum[:, query_cols : query_cols + key_cols]
    fresh_value = small_sum[:, query_cols + key_cols :]
    own_key = large_sum[:, :key_cols]
    own_value = large_sum[:, key_cols:]

    first_len = cache_len[0]
    tail_pos = first_len + jnp.arange(LC, dtype=jnp.int32)
    rebuilt_key = (
        rotate(own_key.reshape(LC, heads_here, HD), tail_pos[:, None])
        .reshape(LC, key_cols)
        .astype(jnp.bfloat16)
    )
    rebuilt_value = own_value.astype(jnp.bfloat16)
    resumed = jnp.arange(ROWS_DEV, dtype=jnp.int32) == 0
    new_pos = cache_len + jnp.where(resumed, LC, 0).astype(jnp.int32)
    query_rot = rotate(query.reshape(ROWS_DEV, query_cols // HD, HD), new_pos[:, None]).astype(
        jnp.bfloat16
    )
    key_rot = rotate(fresh_key.reshape(ROWS_DEV, heads_here, HD), new_pos[:, None]).astype(
        jnp.bfloat16
    )
    value_new = fresh_value.reshape(ROWS_DEV, heads_here, HD).astype(jnp.bfloat16)
    scale = 1.0 / math.sqrt(HD)
    slots = kv_cache.shape[2]
    grouped = query_rot.reshape(ROWS_DEV, heads_here, group_size, HD)
    cache_key = kv_cache[0].reshape(ROWS_DEV, slots, heads_here, HD)
    cache_value = kv_cache[1].reshape(ROWS_DEV, slots, heads_here, HD)
    tail_key = rebuilt_key.reshape(LC, heads_here, HD)
    tail_value = rebuilt_value.reshape(LC, heads_here, HD)
    live = jnp.arange(slots, dtype=jnp.int32)[None, :] < cache_len[:, None]
    dot = lambda spec, a, b: jnp.einsum(spec, a, b, preferred_element_type=jnp.float32)
    s_cache = dot("bkgd,blkd->bkgl", grouped, cache_key) * scale
    s_cache = jnp.where(live[:, None, None, :], s_cache, -jnp.inf)
    s_tail = dot("bkgd,tkd->bkgt", grouped, tail_key) * scale
    s_tail = jnp.where(resumed[:, None, None, None], s_tail, -jnp.inf)
    s_self = dot("bkgd,bkd->bkg", grouped, key_rot) * scale
    highest = jnp.maximum(jnp.maximum(jnp.max(s_cache, axis=-1), jnp.max(s_tail, axis=-1)), s_self)
    e_cache = jnp.exp(s_cache - highest[..., None])
    e_tail = jnp.exp(s_tail - highest[..., None])
    e_self = jnp.exp(s_self - highest)
    denominator = jnp.sum(e_cache, axis=-1) + jnp.sum(e_tail, axis=-1) + e_self
    w_cache = (e_cache / denominator[..., None]).astype(jnp.bfloat16)
    w_tail = (e_tail / denominator[..., None]).astype(jnp.bfloat16)
    w_self = (e_self / denominator).astype(jnp.bfloat16)
    attn = dot("bkgl,blkd->bkgd", w_cache, cache_value)
    attn = attn + dot("bkgt,tkd->bkgd", w_tail, tail_value)
    attn = (
        attn + w_self.astype(jnp.float32)[..., None] * value_new.astype(jnp.float32)[:, :, None, :]
    )
    attn = attn.reshape(ROWS_DEV, query_cols).astype(jnp.bfloat16)

    attn_all = gather(attn, "gx").reshape(owners * ROWS_DEV, query_cols)
    out_part = jnp.dot(attn_all, w_out, preferred_element_type=jnp.float32)
    out_part = out_part.reshape(lax.axis_size("gy"), -1, w_out.shape[1])
    mixed = scatter_sum(lambda d: lax.dynamic_index_in_dim(out_part, d, 0, False), "gy")
    return (mixed.astype(jnp.bfloat16), rebuilt_key[None], rebuilt_value[None])


CHUNK = 512
ROW_TILE = 48
PAY = 128
VALUES = 48
QUERY = 96
F32 = jnp.float32
BF16 = jnp.bfloat16


def whole(space=pltpu.VMEM):
    return pl.BlockSpec(memory_space=space)


def params(limit):
    return pltpu.CompilerParams(vmem_limit_bytes=limit * 1024 * 1024)


def cost(flops, bytes_accessed):
    return pl.CostEstimate(flops=flops, bytes_accessed=bytes_accessed, transcendentals=0)


def angles(len_ref, cos_ref, sin_ref):
    first, second = len_ref[0], len_ref[1]
    row = lax.broadcasted_iota(jnp.int32, (PAY, HD), 0)
    lane = lax.broadcasted_iota(jnp.int32, (PAY, HD), 1)
    resumed = (row == LC) | ((row >= QUERY) & (row < QUERY + 16))
    other = (row == LC + 1) | (row >= QUERY + 16)
    position = jnp.where(row < LC, first + row, 0)
    position = jnp.where(resumed, first + LC, jnp.where(other, second, position))
    half = lax.rem(lane, HD // 2).astype(F32)
    frequency = jnp.exp(half * (-2.0 * math.log(BASE) / HD))
    angle = position.astype(F32) * frequency
    sine = jnp.sin(angle)
    cos_ref[...] = jnp.cos(angle)
    sin_ref[...] = jnp.where(lane < HD // 2, -sine, sine)


def start_load(source, target, sems, first, pieces):
    copies = []
    rows = source.shape[0] // pieces
    for c in range(pieces):
        part = pl.ds(c * rows, rows)
        copy = pltpu.make_async_copy(source.at[part], target.at[part], sems.at[first + c])
        copy.start()
        copies.append(copy)
    return copies


def load_kernel(
    len_ref, wo_hbm, wk_hbm, wv_hbm, b_hbm, cos_ref, sin_ref, wo, wkv, b, sems
):
    copies = start_load(b_hbm, b, sems, 0, 1)
    copies += start_load(wk_hbm, wkv.at[:, pl.ds(0, HD)], sems, 1, 1)
    copies += start_load(wv_hbm, wkv.at[:, pl.ds(HD, HD)], sems, 2, 1)
    copies += start_load(wo_hbm.at[pl.ds(0, wo.shape[0])], wo, sems, 3, 6)
    angles(len_ref, cos_ref, sin_ref)
    for copy in copies:
        copy.wait()


def query_kernel(far, b0, b1, b2, b3, w, wo_hbm, out_ref, wo, acc, sems):
    rows = wo.shape[0]
    copies = start_load(wo_hbm.at[pl.ds(wo_hbm.shape[0] - rows, rows)], wo, sems, 0, 2)
    lhs = jnp.concatenate([b[...].astype(F32) for b in (b0, b1, b2, b3)], axis=0).astype(BF16)
    left = jnp.zeros((lhs.shape[0], w.shape[1] // 2), F32)
    right = left
    for c in range(w.shape[0] // 256):
        rows = slice(c * 256, (c + 1) * 256)
        left += jnp.dot(lhs[:, rows], w[rows, : left.shape[1]], preferred_element_type=F32)
        right += jnp.dot(lhs[:, rows], w[rows, left.shape[1] :], preferred_element_type=F32)
    acc[...] = jnp.concatenate([left, right], axis=1)
    for r in range(acc.shape[0]):
        for h in range(out_ref.shape[1]):
            out_ref[r, pl.ds(h, 1), :] = acc[pl.ds(r, 1), pl.ds(h * HD, HD)]
    for copy in copies:
        copy.wait()


def payload_kernel(
    owner_ref, s0, s1, s2, s3, b0, b1, b2, b3, wkv, q_ref, o0, o3, o2, o1, x, pay
):
    gx, gy = lax.axis_index("gx"), lax.axis_index("gy")
    stored = (s0, s1, s2, s3)
    for k, s in enumerate(stored):
        x[pl.ds(k * ROW_TILE, LC), :] = s[...]
    fresh = [b[...].astype(F32) for b in (b0, b1, b2, b3)]
    fresh.append(jnp.zeros((8, x.shape[1]), F32))
    base = len(stored) * ROW_TILE
    x[pl.ds(base, 16), :] = jnp.concatenate(fresh, axis=0).astype(BF16)
    both = jnp.zeros((x.shape[0], 2 * HD), F32)
    for c in range(x.shape[1] // CHUNK):
        rows = slice(c * CHUNK, (c + 1) * CHUNK)
        both += jnp.dot(x[:, rows], wkv[rows, :], preferred_element_type=F32)
    key, value = both[:, :HD], both[:, HD:]
    empty = jnp.zeros((8 - ROWS_DEV, HD), F32)
    for k in range(len(stored)):
        rows = slice(k * ROW_TILE, k * ROW_TILE + LC)
        target = owner_ref[gy ^ k] ^ gx
        pay[target, pl.ds(0, LC), :] = key[rows]
        pay[target, pl.ds(VALUES, LC), :] = value[rows]
        rows = slice(base + k * ROWS_DEV, base + (k + 1) * ROWS_DEV)
        target = k ^ gx ^ gy
        pay[target, pl.ds(LC, 8), :] = jnp.concatenate([key[rows], empty], axis=0)
        pay[target, pl.ds(VALUES + LC, 8), :] = jnp.concatenate([value[rows], empty], axis=0)
        for r in range(ROWS_DEV):
            pay[target, pl.ds(QUERY + 16 * r, 16), :] = q_ref[k * ROWS_DEV + r]
    o0[...] = pay[0]
    o3[...] = pay[3].astype(BF16)
    o2[...] = pay[2].astype(BF16)
    o1[...] = pay[1].astype(BF16)


def attend_kernel(
    len_ref, p0, p1, p2, p3, cos_ref, sin_ref, kv, key_out, value_out, attn_out, attn
):
    total = p0[...] + p1[...].astype(F32) + p2[...].astype(F32) + p3[...].astype(F32)
    turned = total * cos_ref[...] + pltpu.roll(total, HD // 2, 1) * sin_ref[...]
    turned = turned.astype(BF16)
    key_out[...] = turned[:LC]
    value_out[...] = turned[VALUES : VALUES + LC]
    scale = 1.0 / math.sqrt(HD)
    more_key = turned[:VALUES]
    more_value = turned[VALUES:QUERY]
    slots = kv.shape[2]
    contract = (((1,), (1,)), ((), ()))
    for r in range(ROWS_DEV):
        q = turned[QUERY + 16 * r : QUERY + 16 * (r + 1)]
        s = lax.dot_general(q, kv[0, r], contract, preferred_element_type=F32) * scale
        live = lax.broadcasted_iota(jnp.int32, s.shape, 1) < len_ref[r]
        s = jnp.where(live, s, -jnp.inf)
        s_more = lax.dot_general(q, more_key, contract, preferred_element_type=F32) * scale
        lane = lax.broadcasted_iota(jnp.int32, s_more.shape, 1)
        live = lane <= LC if r == 0 else lane == LC + r
        s_more = jnp.where(live, s_more, -jnp.inf)
        highest = jnp.maximum(
            jnp.max(s, axis=1, keepdims=True), jnp.max(s_more, axis=1, keepdims=True)
        )
        e = jnp.exp(s - highest)
        e_more = jnp.exp(s_more - highest)
        total_e = jnp.sum(e, axis=1, keepdims=True) + jnp.sum(e_more, axis=1, keepdims=True)
        out = jnp.dot((e / total_e).astype(BF16), kv[1, r], preferred_element_type=F32)
        out += jnp.dot((e_more / total_e).astype(BF16), more_value, preferred_element_type=F32)
        for h in range(out.shape[0]):
            attn[pl.ds(r, 1), pl.ds(h * HD, HD)] = out[h : h + 1]
    attn_out[...] = attn[...].astype(BF16)


def out_kernel(a0, a1, a2, a3, w0, w1, o0, o3, o2, o1, blocks):
    tag = lax.axis_index("gx") ^ lax.axis_index("gy")
    for s, a in enumerate((a0, a1, a2, a3)):
        blocks[s ^ tag] = a[...].astype(F32)
    lhs = jnp.concatenate([blocks[k] for k in range(4)], axis=0).astype(BF16)
    first = 0
    acc = jnp.zeros((lhs.shape[0], w0.shape[1]), F32)
    for w in (w0, w1):
        last = first + w.shape[0]
        acc += jnp.dot(lhs[:, first:last], w[...], preferred_element_type=F32)
        first = last
    o0[...] = acc[0:2]
    o1[...] = acc[2:4].astype(BF16)
    o2[...] = acc[4:6].astype(BF16)
    o3[...] = acc[6:8].astype(BF16)


def others(blocks, axis):
    return [swap(b, axis, 3 - k) for k, b in enumerate(blocks)]


def per_device(stored_rows, new_rows, w_query, w_key, w_value, w_out, kv_cache, cache_len, owner):
    shape = jax.ShapeDtypeStruct
    depth, query_cols = w_query.shape
    width = w_out.shape[1]
    heads = query_cols // HD
    quarter = query_cols // 4
    semaphores = pltpu.SemaphoreType.DMA
    in_vmem = lambda x: pltpu.with_memory_space_constraint(x, pltpu.VMEM)
    in_hbm = lambda x: pltpu.with_memory_space_constraint(x, pltpu.HBM)
    far = swap(stored_rows, "gy", 2)
    near = swap(stored_rows, "gy", 1)
    fresh = [swap(new_rows, "gy", k) for k in (1, 2, 3)]
    cos, sin, wo_first, wkv, own_fresh = pl.pallas_call(
        load_kernel,
        out_shape=[pltpu.VMEM((PAY, HD), F32)] * 2
        + [
            pltpu.VMEM((query_cols - quarter, width), BF16),
            pltpu.VMEM((depth, 2 * HD), BF16),
            pltpu.VMEM(new_rows.shape, BF16),
        ],
        in_specs=[whole(pltpu.SMEM)] + [whole(pltpu.HBM)] * 4,
        out_specs=[whole()] * 5,
        scratch_shapes=[semaphores((9,))],
        compiler_params=params(4),
        cost_estimate=cost(1000, 2 * depth * query_cols),
        name="load",
    )(cache_len, in_hbm(w_out), in_hbm(w_key), in_hbm(w_value), in_hbm(new_rows))
    far, own_fresh, *fresh = lax.optimization_barrier((far, own_fresh, *fresh))
    far_near = swap(far, "gy", 1)
    fresh = [own_fresh] + fresh
    stored = [stored_rows, near, far, far_near]
    query, wo_second = pl.pallas_call(
        query_kernel,
        out_shape=[
            pltpu.VMEM((4 * ROWS_DEV, heads, HD), F32),
            pltpu.VMEM((quarter, width), BF16),
        ],
        in_specs=[whole(pl.ANY)] + [whole()] * 5 + [whole(pltpu.HBM)],
        out_specs=[whole()] * 2,
        scratch_shapes=[pltpu.VMEM((4 * ROWS_DEV, query_cols), F32), semaphores((2,))],
        compiler_params=params(4),
        cost_estimate=cost(2 * 8 * depth * query_cols, 4 * depth * HD),
        name="query",
    )(far, *fresh, in_vmem(w_query), in_hbm(w_out))
    payload = pl.pallas_call(
        payload_kernel,
        out_shape=[shape((PAY, HD), F32)] + [shape((PAY, HD), BF16)] * 3,
        in_specs=[whole(pltpu.SMEM)] + [whole()] * 10,
        out_specs=[whole()] * 4,
        scratch_shapes=[
            pltpu.VMEM((4 * ROW_TILE + 16, depth), BF16),
            pltpu.VMEM((4, PAY, HD), F32),
        ],
        compiler_params=params(8),
        cost_estimate=cost(2 * 208 * depth * 256, 4 * depth * HD),
        name="payload",
    )(owner, *stored, *fresh, wkv, query)
    sums = [payload[0]] + others(payload[1:], "gx")
    rebuilt_key, rebuilt_value, attn = pl.pallas_call(
        attend_kernel,
        out_shape=[shape((LC, HD), BF16)] * 2 + [shape((ROWS_DEV, query_cols), BF16)],
        in_specs=[whole(pltpu.SMEM)] + [whole()] * 7,
        out_specs=[whole()] * 3,
        scratch_shapes=[pltpu.VMEM((ROWS_DEV, query_cols), F32)],
        compiler_params=params(4),
        cost_estimate=cost(10000000, 1000000),
        name="attend",
    )(cache_len, *sums, cos, sin, kv_cache)
    attn_all = [attn] + [swap(attn, "gx", k) for k in (1, 2, 3)]
    parts = pl.pallas_call(
        out_kernel,
        out_shape=[shape((ROWS_DEV, width), F32)] + [shape((ROWS_DEV, width), BF16)] * 3,
        in_specs=[whole()] * 6,
        out_specs=[whole()] * 4,
        scratch_shapes=[pltpu.VMEM((4, ROWS_DEV, query_cols), F32)],
        compiler_params=params(4),
        cost_estimate=cost(2 * 8 * width * query_cols, 2 * width * query_cols),
        name="project",
    )(*attn_all, wo_first, wo_second)
    arrived = others(parts[1:], "gy")
    mixed = parts[0] + arrived[0].astype(F32) + arrived[1].astype(F32) + arrived[2].astype(F32)
    return (mixed.astype(BF16), rebuilt_key[None], rebuilt_value[None])


def solution(mesh):
    direct = mesh.shape["gx"] == 4 and mesh.shape["gy"] == 4
    in_specs = (
        P(("groups", "gy"), "gx"),
        P(("groups", "gy"), "gx"),
        P("gx", "gy"),
        P("gx", "gy"),
        P("gx", "gy"),
        P("gy", "gx"),
        P(None, ("groups", "gx"), None, "gy"),
        P(("groups", "gx")),
        P("groups"),
    )
    out_specs = (
        P(("groups", "gy"), "gx"),
        P(("groups", "gx"), None, "gy"),
        P(("groups", "gx"), None, "gy"),
    )
    return jax.shard_map(
        per_device if direct else general, mesh=mesh, in_specs=in_specs, out_specs=out_specs, check_vma=False
    )
```

```python
import functools
import math

import jax
import jax.numpy as jnp
from jax import lax
from jax.experimental import pallas as pl
from jax.experimental.pallas import tpu as pltpu
from jax.sharding import PartitionSpec as P

HD = 128
LC = 40
ROWS_DEV = 2
BASE = 500000.0
DIRECT = 8


def rotate(values, position):
    half = values.shape[-1] // 2
    index_row = jnp.arange(half).astype(jnp.float32)
    frequency = jnp.exp(index_row * (-2.0 * math.log(BASE) / values.shape[-1]))
    angle = position.astype(jnp.float32)[..., None] * frequency
    cosine = jnp.cos(angle)
    sine = jnp.sin(angle)
    first_half = values[..., :half]
    second_half = values[..., half:]
    return jnp.concatenate(
        [first_half * cosine - second_half * sine, second_half * cosine + first_half * sine],
        axis=-1,
    )


def swap(x, axis, k):
    n = lax.axis_size(axis)
    return lax.ppermute(x, axis, [(i, i ^ k) for i in range(n)])


def gather(x, axis):
    n = lax.axis_size(axis)
    if n > DIRECT or n & (n - 1):
        return lax.all_gather(x, axis, axis=0)
    me = lax.axis_index(axis)
    out = jnp.zeros((n,) + x.shape, x.dtype)
    for k in range(n):
        block = x if k == 0 else swap(x, axis, k)
        out = lax.dynamic_update_index_in_dim(out, block, me ^ k, 0)
    return out


def scatter_sum(parts, axis):
    n = lax.axis_size(axis)
    me = lax.axis_index(axis)
    if n > DIRECT or n & (n - 1):
        whole = jnp.stack([parts(d) for d in range(n)])
        return lax.psum_scatter(whole.astype(jnp.float32), axis, scatter_dimension=0)
    total = parts(me).astype(jnp.float32)
    for k in range(1, n):
        total = total + swap(parts(me ^ k).astype(jnp.bfloat16), axis, k).astype(jnp.float32)
    return total


def general(stored_rows, new_rows, w_query, w_key, w_value, w_out, kv_cache, cache_len, owner):
    owners = lax.axis_size("gx")
    key_cols = w_key.shape[1]
    query_cols = w_query.shape[1]
    heads_here = key_cols // HD
    group_size = query_cols // key_cols
    slot_ids = jnp.arange(owners, dtype=jnp.int32)
    inverse = jnp.sum(jnp.where(owner[None, :] == slot_ids[:, None], slot_ids[None, :], 0), axis=1)

    fresh_all = gather(new_rows, "gy").reshape(-1, new_rows.shape[1])
    stored_all = gather(stored_rows, "gy").reshape(owners, LC, stored_rows.shape[1])
    flat = stored_all.reshape(owners * LC, stored_rows.shape[1])
    query_part = jnp.dot(fresh_all, w_query, preferred_element_type=jnp.float32)
    new_key_part = jnp.dot(fresh_all, w_key, preferred_element_type=jnp.float32)
    new_value_part = jnp.dot(fresh_all, w_value, preferred_element_type=jnp.float32)
    key_part = jnp.dot(flat, w_key, preferred_element_type=jnp.float32)
    value_part = jnp.dot(flat, w_value, preferred_element_type=jnp.float32)

    small = jnp.concatenate([query_part, new_key_part, new_value_part], axis=1)
    small = small.reshape(owners, ROWS_DEV, -1)
    large = jnp.concatenate([key_part, value_part], axis=1).reshape(owners, LC, -1)

    small_sum = scatter_sum(lambda d: lax.dynamic_index_in_dim(small, d, 0, False), "gx")
    large_sum = scatter_sum(
        lambda d: lax.dynamic_index_in_dim(
            large, lax.dynamic_index_in_dim(inverse, d, 0, False), 0, False
        ),
        "gx",
    )
    query = small_sum[:, :query_cols]
    fresh_key = small_sum[:, query_cols : query_cols + key_cols]
    fresh_value = small_sum[:, query_cols + key_cols :]
    own_key = large_sum[:, :key_cols]
    own_value = large_sum[:, key_cols:]

    first_len = cache_len[0]
    tail_pos = first_len + jnp.arange(LC, dtype=jnp.int32)
    rebuilt_key = (
        rotate(own_key.reshape(LC, heads_here, HD), tail_pos[:, None])
        .reshape(LC, key_cols)
        .astype(jnp.bfloat16)
    )
    rebuilt_value = own_value.astype(jnp.bfloat16)
    resumed = jnp.arange(ROWS_DEV, dtype=jnp.int32) == 0
    new_pos = cache_len + jnp.where(resumed, LC, 0).astype(jnp.int32)
    query_rot = rotate(query.reshape(ROWS_DEV, query_cols // HD, HD), new_pos[:, None]).astype(
        jnp.bfloat16
    )
    key_rot = rotate(fresh_key.reshape(ROWS_DEV, heads_here, HD), new_pos[:, None]).astype(
        jnp.bfloat16
    )
    value_new = fresh_value.reshape(ROWS_DEV, heads_here, HD).astype(jnp.bfloat16)
    scale = 1.0 / math.sqrt(HD)
    slots = kv_cache.shape[2]
    grouped = query_rot.reshape(ROWS_DEV, heads_here, group_size, HD)
    cache_key = kv_cache[0].reshape(ROWS_DEV, slots, heads_here, HD)
    cache_value = kv_cache[1].reshape(ROWS_DEV, slots, heads_here, HD)
    tail_key = rebuilt_key.reshape(LC, heads_here, HD)
    tail_value = rebuilt_value.reshape(LC, heads_here, HD)
    live = jnp.arange(slots, dtype=jnp.int32)[None, :] < cache_len[:, None]
    dot = lambda spec, a, b: jnp.einsum(spec, a, b, preferred_element_type=jnp.float32)
    s_cache = dot("bkgd,blkd->bkgl", grouped, cache_key) * scale
    s_cache = jnp.where(live[:, None, None, :], s_cache, -jnp.inf)
    s_tail = dot("bkgd,tkd->bkgt", grouped, tail_key) * scale
    s_tail = jnp.where(resumed[:, None, None, None], s_tail, -jnp.inf)
    s_self = dot("bkgd,bkd->bkg", grouped, key_rot) * scale
    highest = jnp.maximum(jnp.maximum(jnp.max(s_cache, axis=-1), jnp.max(s_tail, axis=-1)), s_self)
    e_cache = jnp.exp(s_cache - highest[..., None])
    e_tail = jnp.exp(s_tail - highest[..., None])
    e_self = jnp.exp(s_self - highest)
    denominator = jnp.sum(e_cache, axis=-1) + jnp.sum(e_tail, axis=-1) + e_self
    w_cache = (e_cache / denominator[..., None]).astype(jnp.bfloat16)
    w_tail = (e_tail / denominator[..., None]).astype(jnp.bfloat16)
    w_self = (e_self / denominator).astype(jnp.bfloat16)
    attn = dot("bkgl,blkd->bkgd", w_cache, cache_value)
    attn = attn + dot("bkgt,tkd->bkgd", w_tail, tail_value)
    attn = (
        attn + w_self.astype(jnp.float32)[..., None] * value_new.astype(jnp.float32)[:, :, None, :]
    )
    attn = attn.reshape(ROWS_DEV, query_cols).astype(jnp.bfloat16)

    attn_all = gather(attn, "gx").reshape(owners * ROWS_DEV, query_cols)
    out_part = jnp.dot(attn_all, w_out, preferred_element_type=jnp.float32)
    out_part = out_part.reshape(lax.axis_size("gy"), -1, w_out.shape[1])
    mixed = scatter_sum(lambda d: lax.dynamic_index_in_dim(out_part, d, 0, False), "gy")
    return (mixed.astype(jnp.bfloat16), rebuilt_key[None], rebuilt_value[None])


CHUNK = 512
ROW_TILE = 48
PAY = 128
VALUES = 48
QUERY = 96
F32 = jnp.float32
BF16 = jnp.bfloat16


def whole(space=pltpu.VMEM):
    return pl.BlockSpec(memory_space=space)


def params(limit):
    return pltpu.CompilerParams(vmem_limit_bytes=limit * 1024 * 1024)


def cost(flops, bytes_accessed):
    return pl.CostEstimate(flops=flops, bytes_accessed=bytes_accessed, transcendentals=0)


def angles(len_ref, cos_ref, sin_ref):
    first, second = len_ref[0], len_ref[1]
    row = lax.broadcasted_iota(jnp.int32, (PAY, HD), 0)
    lane = lax.broadcasted_iota(jnp.int32, (PAY, HD), 1)
    resumed = (row == LC) | ((row >= QUERY) & (row < QUERY + 16))
    other = (row == LC + 1) | (row >= QUERY + 16)
    position = jnp.where(row < LC, first + row, 0)
    position = jnp.where(resumed, first + LC, jnp.where(other, second, position))
    half = lax.rem(lane, HD // 2).astype(F32)
    frequency = jnp.exp(half * (-2.0 * math.log(BASE) / HD))
    angle = position.astype(F32) * frequency
    sine = jnp.sin(angle)
    cos_ref[...] = jnp.cos(angle)
    sin_ref[...] = jnp.where(lane < HD // 2, -sine, sine)


def start_load(source, target, sems, first, pieces):
    copies = []
    rows = source.shape[0] // pieces
    for c in range(pieces):
        part = pl.ds(c * rows, rows)
        copy = pltpu.make_async_copy(source.at[part], target.at[part], sems.at[first + c])
        copy.start()
        copies.append(copy)
    return copies


def load_kernel(
    len_hbm, wo_hbm, wk_hbm, wv_hbm, b_hbm, cos_ref, sin_ref, wo, wkv, b, len_ref, sems
):
    lengths = pltpu.make_async_copy(len_hbm, len_ref, sems.at[9])
    lengths.start()
    copies = start_load(b_hbm, b, sems, 0, 1)
    copies += start_load(wk_hbm, wkv.at[:, pl.ds(0, HD)], sems, 1, 1)
    copies += start_load(wv_hbm, wkv.at[:, pl.ds(HD, HD)], sems, 2, 1)
    copies += start_load(wo_hbm.at[pl.ds(0, wo.shape[0])], wo, sems, 3, 5)
    lengths.wait()
    angles(len_ref, cos_ref, sin_ref)
    for copy in copies:
        copy.wait()


def rest_kernel(ready, wo_hbm, wo, sems):
    rows = wo.shape[0]
    for copy in start_load(wo_hbm.at[pl.ds(wo_hbm.shape[0] - rows, rows)], wo, sems, 0, 2):
        copy.wait()


def query_kernel(first, far, b0, b1, b2, b3, w, wo_hbm, out_ref, wo, acc, sems):
    rows = wo.shape[0]
    copies = start_load(wo_hbm.at[pl.ds(first, rows)], wo, sems, 0, 2)
    lhs = jnp.concatenate([b[...].astype(F32) for b in (b0, b1, b2, b3)], axis=0).astype(BF16)
    acc[...] = jnp.dot(lhs, w[...], preferred_element_type=F32)
    for r in range(acc.shape[0]):
        for h in range(out_ref.shape[1]):
            out_ref[r, pl.ds(h, 1), :] = acc[pl.ds(r, 1), pl.ds(h * HD, HD)]
    for copy in copies:
        copy.wait()


def payload_kernel(
    owner_ref, s0, s1, s2, s3, b0, b1, b2, b3, wkv, q_ref, o0, o3, o2, o1, x, pay
):
    gx, gy = lax.axis_index("gx"), lax.axis_index("gy")
    stored = (s0, s1, s2, s3)
    for k, s in enumerate(stored):
        x[pl.ds(k * ROW_TILE, LC), :] = s[...]
    fresh = [b[...].astype(F32) for b in (b0, b1, b2, b3)]
    fresh.append(jnp.zeros((8, x.shape[1]), F32))
    base = len(stored) * ROW_TILE
    x[pl.ds(base, 16), :] = jnp.concatenate(fresh, axis=0).astype(BF16)
    both = jnp.zeros((x.shape[0], 2 * HD), F32)
    for c in range(x.shape[1] // CHUNK):
        rows = slice(c * CHUNK, (c + 1) * CHUNK)
        both += jnp.dot(x[:, rows], wkv[rows, :], preferred_element_type=F32)
    key, value = both[:, :HD], both[:, HD:]
    empty = jnp.zeros((8 - ROWS_DEV, HD), F32)
    for k in range(len(stored)):
        rows = slice(k * ROW_TILE, k * ROW_TILE + LC)
        target = owner_ref[gy ^ k] ^ gx
        pay[target, pl.ds(0, LC), :] = key[rows]
        pay[target, pl.ds(VALUES, LC), :] = value[rows]
        rows = slice(base + k * ROWS_DEV, base + (k + 1) * ROWS_DEV)
        target = k ^ gx ^ gy
        pay[target, pl.ds(LC, 8), :] = jnp.concatenate([key[rows], empty], axis=0)
        pay[target, pl.ds(VALUES + LC, 8), :] = jnp.concatenate([value[rows], empty], axis=0)
        for r in range(ROWS_DEV):
            pay[target, pl.ds(QUERY + 16 * r, 16), :] = q_ref[k * ROWS_DEV + r]
    o0[...] = pay[0]
    o3[...] = pay[3].astype(BF16)
    o2[...] = pay[2].astype(BF16)
    o1[...] = pay[1].astype(BF16)


def attend_kernel(
    len_ref, ready, p0, p1, p2, p3, cos_ref, sin_ref, kv, key_out, value_out, attn_out, attn
):
    total = p0[...] + p1[...].astype(F32) + p2[...].astype(F32) + p3[...].astype(F32)
    turned = total * cos_ref[...] + pltpu.roll(total, HD // 2, 1) * sin_ref[...]
    turned = turned.astype(BF16)
    key_out[...] = turned[:LC]
    value_out[...] = turned[VALUES : VALUES + LC]
    scale = 1.0 / math.sqrt(HD)
    more_key = turned[:VALUES]
    more_value = turned[VALUES:QUERY]
    slots = kv.shape[2]
    contract = (((1,), (1,)), ((), ()))
    for r in range(ROWS_DEV):
        q = turned[QUERY + 16 * r : QUERY + 16 * (r + 1)]
        s = lax.dot_general(q, kv[0, r], contract, preferred_element_type=F32) * scale
        live = lax.broadcasted_iota(jnp.int32, s.shape, 1) < len_ref[r]
        s = jnp.where(live, s, -jnp.inf)
        s_more = lax.dot_general(q, more_key, contract, preferred_element_type=F32) * scale
        lane = lax.broadcasted_iota(jnp.int32, s_more.shape, 1)
        live = lane <= LC if r == 0 else lane == LC + r
        s_more = jnp.where(live, s_more, -jnp.inf)
        highest = jnp.maximum(
            jnp.max(s, axis=1, keepdims=True), jnp.max(s_more, axis=1, keepdims=True)
        )
        e = jnp.exp(s - highest)
        e_more = jnp.exp(s_more - highest)
        total_e = jnp.sum(e, axis=1, keepdims=True) + jnp.sum(e_more, axis=1, keepdims=True)
        out = jnp.dot((e / total_e).astype(BF16), kv[1, r], preferred_element_type=F32)
        out += jnp.dot((e_more / total_e).astype(BF16), more_value, preferred_element_type=F32)
        for h in range(out.shape[0]):
            attn[pl.ds(r, 1), pl.ds(h * HD, HD)] = out[h : h + 1]
    attn_out[...] = attn[...].astype(BF16)


def out_kernel(a0, a1, a2, a3, w0, w1, w2, o0, o3, o2, o1, blocks):
    tag = lax.axis_index("gx") ^ lax.axis_index("gy")
    for s, a in enumerate((a0, a1, a2, a3)):
        blocks[s ^ tag] = a[...].astype(F32)
    lhs = jnp.concatenate([blocks[k] for k in range(4)], axis=0).astype(BF16)
    first = 0
    acc = jnp.zeros((lhs.shape[0], w0.shape[1]), F32)
    for w in (w0, w1, w2):
        last = first + w.shape[0]
        acc += jnp.dot(lhs[:, first:last], w[...], preferred_element_type=F32)
        first = last
    o0[...] = acc[0:2]
    o1[...] = acc[2:4].astype(BF16)
    o2[...] = acc[4:6].astype(BF16)
    o3[...] = acc[6:8].astype(BF16)


def others(blocks, axis):
    return [swap(b, axis, 3 - k) for k, b in enumerate(blocks)]


def per_device(stored_rows, new_rows, w_query, w_key, w_value, w_out, kv_cache, cache_len, owner):
    shape = jax.ShapeDtypeStruct
    depth, query_cols = w_query.shape
    width = w_out.shape[1]
    heads = query_cols // HD
    last, quarter = query_cols // 8, query_cols // 4
    semaphores = pltpu.SemaphoreType.DMA
    in_vmem = lambda x: pltpu.with_memory_space_constraint(x, pltpu.VMEM)
    in_hbm = lambda x: pltpu.with_memory_space_constraint(x, pltpu.HBM)
    far = swap(stored_rows, "gy", 2)
    near = swap(stored_rows, "gy", 1)
    fresh = [swap(new_rows, "gy", k) for k in (1, 2, 3)]
    cos, sin, wo_first, wkv, own_fresh = pl.pallas_call(
        load_kernel,
        out_shape=[pltpu.VMEM((PAY, HD), F32)] * 2
        + [
            pltpu.VMEM((query_cols - quarter - last, width), BF16),
            pltpu.VMEM((depth, 2 * HD), BF16),
            pltpu.VMEM(new_rows.shape, BF16),
        ],
        in_specs=[whole(pltpu.HBM)] * 5,
        out_specs=[whole()] * 5,
        scratch_shapes=[pltpu.SMEM(cache_len.shape, jnp.int32), semaphores((10,))],
        compiler_params=params(4),
        cost_estimate=cost(1000, 2 * depth * query_cols),
        name="load",
    )(in_hbm(cache_len), in_hbm(w_out), in_hbm(w_key), in_hbm(w_value), in_hbm(new_rows))
    far, own_fresh, *fresh = lax.optimization_barrier((far, own_fresh, *fresh))
    far_near = swap(far, "gy", 1)
    fresh = [own_fresh] + fresh
    stored = [stored_rows, near, far, far_near]
    query, wo_second = pl.pallas_call(
        functools.partial(query_kernel, query_cols - quarter - last),
        out_shape=[
            pltpu.VMEM((4 * ROWS_DEV, heads, HD), F32),
            pltpu.VMEM((quarter, width), BF16),
        ],
        in_specs=[whole(pl.ANY)] + [whole()] * 5 + [whole(pltpu.HBM)],
        out_specs=[whole()] * 2,
        scratch_shapes=[pltpu.VMEM((4 * ROWS_DEV, query_cols), F32), semaphores((2,))],
        compiler_params=params(4),
        cost_estimate=cost(2 * 8 * depth * query_cols, 4 * depth * HD),
        name="query",
    )(far, *fresh, in_vmem(w_query), in_hbm(w_out))
    payload = pl.pallas_call(
        payload_kernel,
        out_shape=[shape((PAY, HD), F32)] + [shape((PAY, HD), BF16)] * 3,
        in_specs=[whole(pltpu.SMEM)] + [whole()] * 10,
        out_specs=[whole()] * 4,
        scratch_shapes=[
            pltpu.VMEM((4 * ROW_TILE + 16, depth), BF16),
            pltpu.VMEM((4, PAY, HD), F32),
        ],
        compiler_params=params(8),
        cost_estimate=cost(2 * 208 * depth * 256, 4 * depth * HD),
        name="payload",
    )(owner, *stored, *fresh, wkv, query)
    sums = [payload[0]] + others(payload[1:], "gx")
    wo_third = pl.pallas_call(
        rest_kernel,
        out_shape=pltpu.VMEM((last, width), BF16),
        in_specs=[whole(pl.ANY), whole(pltpu.HBM)],
        out_specs=whole(),
        scratch_shapes=[semaphores((2,))],
        compiler_params=params(4),
        cost_estimate=cost(1000, 2 * last * width),
        name="rest",
    )(payload[0], in_hbm(w_out))
    rebuilt_key, rebuilt_value, attn = pl.pallas_call(
        attend_kernel,
        out_shape=[shape((LC, HD), BF16)] * 2 + [shape((ROWS_DEV, query_cols), BF16)],
        in_specs=[whole(pltpu.SMEM), whole(pl.ANY)] + [whole()] * 7,
        out_specs=[whole()] * 3,
        scratch_shapes=[pltpu.VMEM((ROWS_DEV, query_cols), F32)],
        compiler_params=params(4),
        cost_estimate=cost(10000000, 1000000),
        name="attend",
    )(cache_len, wo_third, *sums, cos, sin, kv_cache)
    attn_all = [attn] + [swap(attn, "gx", k) for k in (1, 2, 3)]
    parts = pl.pallas_call(
        out_kernel,
        out_shape=[shape((ROWS_DEV, width), F32)] + [shape((ROWS_DEV, width), BF16)] * 3,
        in_specs=[whole()] * 7,
        out_specs=[whole()] * 4,
        scratch_shapes=[pltpu.VMEM((4, ROWS_DEV, query_cols), F32)],
        compiler_params=params(4),
        cost_estimate=cost(2 * 8 * width * query_cols, 2 * width * query_cols),
        name="project",
    )(*attn_all, wo_first, wo_second, wo_third)
    arrived = others(parts[1:], "gy")
    mixed = parts[0] + arrived[0].astype(F32) + arrived[1].astype(F32) + arrived[2].astype(F32)
    return (mixed.astype(BF16), rebuilt_key[None], rebuilt_value[None])


def solution(mesh):
    direct = mesh.shape["gx"] == 4 and mesh.shape["gy"] == 4
    in_specs = (
        P(("groups", "gy"), "gx"),
        P(("groups", "gy"), "gx"),
        P("gx", "gy"),
        P("gx", "gy"),
        P("gx", "gy"),
        P("gy", "gx"),
        P(None, ("groups", "gx"), None, "gy"),
        P(("groups", "gx")),
        P("groups"),
    )
    out_specs = (
        P(("groups", "gy"), "gx"),
        P(("groups", "gx"), None, "gy"),
        P(("groups", "gx"), None, "gy"),
    )
    return jax.shard_map(
        per_device if direct else general, mesh=mesh, in_specs=in_specs, out_specs=out_specs, check_vma=False
    )
```

```python
import functools
import math

import jax
import jax.numpy as jnp
from jax import lax
from jax.experimental import pallas as pl
from jax.experimental.pallas import tpu as pltpu
from jax.sharding import PartitionSpec as P

HD = 128
LC = 40
ROWS_DEV = 2
BASE = 500000.0
DIRECT = 8


def rotate(values, position):
    half = values.shape[-1] // 2
    index_row = jnp.arange(half).astype(jnp.float32)
    frequency = jnp.exp(index_row * (-2.0 * math.log(BASE) / values.shape[-1]))
    angle = position.astype(jnp.float32)[..., None] * frequency
    cosine = jnp.cos(angle)
    sine = jnp.sin(angle)
    first_half = values[..., :half]
    second_half = values[..., half:]
    return jnp.concatenate(
        [first_half * cosine - second_half * sine, second_half * cosine + first_half * sine],
        axis=-1,
    )


def swap(x, axis, k):
    n = lax.axis_size(axis)
    return lax.ppermute(x, axis, [(i, i ^ k) for i in range(n)])


def gather(x, axis):
    n = lax.axis_size(axis)
    if n > DIRECT or n & (n - 1):
        return lax.all_gather(x, axis, axis=0)
    me = lax.axis_index(axis)
    out = jnp.zeros((n,) + x.shape, x.dtype)
    for k in range(n):
        block = x if k == 0 else swap(x, axis, k)
        out = lax.dynamic_update_index_in_dim(out, block, me ^ k, 0)
    return out


def scatter_sum(parts, axis):
    n = lax.axis_size(axis)
    me = lax.axis_index(axis)
    if n > DIRECT or n & (n - 1):
        whole = jnp.stack([parts(d) for d in range(n)])
        return lax.psum_scatter(whole.astype(jnp.float32), axis, scatter_dimension=0)
    total = parts(me).astype(jnp.float32)
    for k in range(1, n):
        total = total + swap(parts(me ^ k).astype(jnp.bfloat16), axis, k).astype(jnp.float32)
    return total


def general(stored_rows, new_rows, w_query, w_key, w_value, w_out, kv_cache, cache_len, owner):
    owners = lax.axis_size("gx")
    key_cols = w_key.shape[1]
    query_cols = w_query.shape[1]
    heads_here = key_cols // HD
    group_size = query_cols // key_cols
    slot_ids = jnp.arange(owners, dtype=jnp.int32)
    inverse = jnp.sum(jnp.where(owner[None, :] == slot_ids[:, None], slot_ids[None, :], 0), axis=1)

    fresh_all = gather(new_rows, "gy").reshape(-1, new_rows.shape[1])
    stored_all = gather(stored_rows, "gy").reshape(owners, LC, stored_rows.shape[1])
    flat = stored_all.reshape(owners * LC, stored_rows.shape[1])
    query_part = jnp.dot(fresh_all, w_query, preferred_element_type=jnp.float32)
    new_key_part = jnp.dot(fresh_all, w_key, preferred_element_type=jnp.float32)
    new_value_part = jnp.dot(fresh_all, w_value, preferred_element_type=jnp.float32)
    key_part = jnp.dot(flat, w_key, preferred_element_type=jnp.float32)
    value_part = jnp.dot(flat, w_value, preferred_element_type=jnp.float32)

    small = jnp.concatenate([query_part, new_key_part, new_value_part], axis=1)
    small = small.reshape(owners, ROWS_DEV, -1)
    large = jnp.concatenate([key_part, value_part], axis=1).reshape(owners, LC, -1)

    small_sum = scatter_sum(lambda d: lax.dynamic_index_in_dim(small, d, 0, False), "gx")
    large_sum = scatter_sum(
        lambda d: lax.dynamic_index_in_dim(
            large, lax.dynamic_index_in_dim(inverse, d, 0, False), 0, False
        ),
        "gx",
    )
    query = small_sum[:, :query_cols]
    fresh_key = small_sum[:, query_cols : query_cols + key_cols]
    fresh_value = small_sum[:, query_cols + key_cols :]
    own_key = large_sum[:, :key_cols]
    own_value = large_sum[:, key_cols:]

    first_len = cache_len[0]
    tail_pos = first_len + jnp.arange(LC, dtype=jnp.int32)
    rebuilt_key = (
        rotate(own_key.reshape(LC, heads_here, HD), tail_pos[:, None])
        .reshape(LC, key_cols)
        .astype(jnp.bfloat16)
    )
    rebuilt_value = own_value.astype(jnp.bfloat16)
    resumed = jnp.arange(ROWS_DEV, dtype=jnp.int32) == 0
    new_pos = cache_len + jnp.where(resumed, LC, 0).astype(jnp.int32)
    query_rot = rotate(query.reshape(ROWS_DEV, query_cols // HD, HD), new_pos[:, None]).astype(
        jnp.bfloat16
    )
    key_rot = rotate(fresh_key.reshape(ROWS_DEV, heads_here, HD), new_pos[:, None]).astype(
        jnp.bfloat16
    )
    value_new = fresh_value.reshape(ROWS_DEV, heads_here, HD).astype(jnp.bfloat16)
    scale = 1.0 / math.sqrt(HD)
    slots = kv_cache.shape[2]
    grouped = query_rot.reshape(ROWS_DEV, heads_here, group_size, HD)
    cache_key = kv_cache[0].reshape(ROWS_DEV, slots, heads_here, HD)
    cache_value = kv_cache[1].reshape(ROWS_DEV, slots, heads_here, HD)
    tail_key = rebuilt_key.reshape(LC, heads_here, HD)
    tail_value = rebuilt_value.reshape(LC, heads_here, HD)
    live = jnp.arange(slots, dtype=jnp.int32)[None, :] < cache_len[:, None]
    dot = lambda spec, a, b: jnp.einsum(spec, a, b, preferred_element_type=jnp.float32)
    s_cache = dot("bkgd,blkd->bkgl", grouped, cache_key) * scale
    s_cache = jnp.where(live[:, None, None, :], s_cache, -jnp.inf)
    s_tail = dot("bkgd,tkd->bkgt", grouped, tail_key) * scale
    s_tail = jnp.where(resumed[:, None, None, None], s_tail, -jnp.inf)
    s_self = dot("bkgd,bkd->bkg", grouped, key_rot) * scale
    highest = jnp.maximum(jnp.maximum(jnp.max(s_cache, axis=-1), jnp.max(s_tail, axis=-1)), s_self)
    e_cache = jnp.exp(s_cache - highest[..., None])
    e_tail = jnp.exp(s_tail - highest[..., None])
    e_self = jnp.exp(s_self - highest)
    denominator = jnp.sum(e_cache, axis=-1) + jnp.sum(e_tail, axis=-1) + e_self
    w_cache = (e_cache / denominator[..., None]).astype(jnp.bfloat16)
    w_tail = (e_tail / denominator[..., None]).astype(jnp.bfloat16)
    w_self = (e_self / denominator).astype(jnp.bfloat16)
    attn = dot("bkgl,blkd->bkgd", w_cache, cache_value)
    attn = attn + dot("bkgt,tkd->bkgd", w_tail, tail_value)
    attn = (
        attn + w_self.astype(jnp.float32)[..., None] * value_new.astype(jnp.float32)[:, :, None, :]
    )
    attn = attn.reshape(ROWS_DEV, query_cols).astype(jnp.bfloat16)

    attn_all = gather(attn, "gx").reshape(owners * ROWS_DEV, query_cols)
    out_part = jnp.dot(attn_all, w_out, preferred_element_type=jnp.float32)
    out_part = out_part.reshape(lax.axis_size("gy"), -1, w_out.shape[1])
    mixed = scatter_sum(lambda d: lax.dynamic_index_in_dim(out_part, d, 0, False), "gy")
    return (mixed.astype(jnp.bfloat16), rebuilt_key[None], rebuilt_value[None])


CHUNK = 512
ROW_TILE = 48
PAY = 128
VALUES = 48
QUERY = 96
F32 = jnp.float32
BF16 = jnp.bfloat16


def whole(space=pltpu.VMEM):
    return pl.BlockSpec(memory_space=space)


def params(limit):
    return pltpu.CompilerParams(vmem_limit_bytes=limit * 1024 * 1024)


def cost(flops, bytes_accessed):
    return pl.CostEstimate(flops=flops, bytes_accessed=bytes_accessed, transcendentals=0)


def angles(len_ref, cos_ref, sin_ref):
    first, second = len_ref[0], len_ref[1]
    row = lax.broadcasted_iota(jnp.int32, (PAY, HD), 0)
    lane = lax.broadcasted_iota(jnp.int32, (PAY, HD), 1)
    resumed = (row == LC) | ((row >= QUERY) & (row < QUERY + 16))
    other = (row == LC + 1) | (row >= QUERY + 16)
    position = jnp.where(row < LC, first + row, 0)
    position = jnp.where(resumed, first + LC, jnp.where(other, second, position))
    half = lax.rem(lane, HD // 2).astype(F32)
    frequency = jnp.exp(half * (-2.0 * math.log(BASE) / HD))
    angle = position.astype(F32) * frequency
    sine = jnp.sin(angle)
    cos_ref[...] = jnp.cos(angle)
    sin_ref[...] = jnp.where(lane < HD // 2, -sine, sine)


def start_load(source, target, sems, first, pieces):
    copies = []
    rows = source.shape[0] // pieces
    for c in range(pieces):
        part = pl.ds(c * rows, rows)
        copy = pltpu.make_async_copy(source.at[part], target.at[part], sems.at[first + c])
        copy.start()
        copies.append(copy)
    return copies


def project_rows(x, wkv):
    both = jnp.zeros((x.shape[0], wkv.shape[1]), F32)
    for c in range(x.shape[1] // CHUNK):
        part = slice(c * CHUNK, (c + 1) * CHUNK)
        both += jnp.dot(x[:, part], wkv[part, :], preferred_element_type=F32)
    return both


def load_kernel(
    len_hbm, wo_hbm, wk_hbm, wv_hbm, cos_ref, sin_ref, wo, wkv, len_ref, sems
):
    lengths = pltpu.make_async_copy(len_hbm, len_ref, sems.at[0])
    lengths.start()
    copies = start_load(wk_hbm, wkv.at[:, pl.ds(0, HD)], sems, 1, 1)
    copies += start_load(wv_hbm, wkv.at[:, pl.ds(HD, HD)], sems, 2, 1)
    copies += start_load(wo_hbm.at[pl.ds(0, wo.shape[0])], wo, sems, 3, 6)
    lengths.wait()
    angles(len_ref, cos_ref, sin_ref)
    for copy in copies:
        copy.wait()


def own_kernel(s, wkv, out):
    out[...] = project_rows(s, wkv)


def query_kernel(first, far, b0, b1, b2, b3, w, wo_hbm, out_ref, wo, acc, sems):
    rows = wo.shape[0]
    copies = start_load(wo_hbm.at[pl.ds(first, rows)], wo, sems, 0, 2)
    lhs = jnp.concatenate([b[...].astype(F32) for b in (b0, b1, b2, b3)], axis=0).astype(BF16)
    acc[...] = jnp.dot(lhs, w[...], preferred_element_type=F32)
    for r in range(acc.shape[0]):
        for h in range(out_ref.shape[1]):
            out_ref[r, pl.ds(h, 1), :] = acc[pl.ds(r, 1), pl.ds(h * HD, HD)]
    for copy in copies:
        copy.wait()


def payload_kernel(
    owner_ref, own, s1, s2, s3, b0, b1, b2, b3, wkv, q_ref, o0, o3, o2, o1, x, pay
):
    gx, gy = lax.axis_index("gx"), lax.axis_index("gy")
    for k, s in enumerate((s1, s2, s3)):
        x[pl.ds(k * ROW_TILE, LC), :] = s[...]
    fresh = [b[...].astype(F32) for b in (b0, b1, b2, b3)]
    fresh.append(jnp.zeros((8, x.shape[1]), F32))
    base = 3 * ROW_TILE
    x[pl.ds(base, 16), :] = jnp.concatenate(fresh, axis=0).astype(BF16)
    late = project_rows(x, wkv)
    empty = jnp.zeros((8 - ROWS_DEV, HD), F32)
    for k in range(4):
        target = owner_ref[gy ^ k] ^ gx
        both = late[(k - 1) * ROW_TILE : (k - 1) * ROW_TILE + LC] if k else own[...]
        pay[target, pl.ds(0, LC), :] = both[:, :HD]
        pay[target, pl.ds(VALUES, LC), :] = both[:, HD:]
        both = late[base + k * ROWS_DEV : base + (k + 1) * ROWS_DEV]
        target = k ^ gx ^ gy
        pay[target, pl.ds(LC, 8), :] = jnp.concatenate([both[:, :HD], empty], axis=0)
        pay[target, pl.ds(VALUES + LC, 8), :] = jnp.concatenate([both[:, HD:], empty], axis=0)
        for r in range(ROWS_DEV):
            pay[target, pl.ds(QUERY + 16 * r, 16), :] = q_ref[k * ROWS_DEV + r]
    o0[...] = pay[0]
    o3[...] = pay[3].astype(BF16)
    o2[...] = pay[2].astype(BF16)
    o1[...] = pay[1].astype(BF16)


def attend_kernel(
    len_ref, p0, p1, p2, p3, cos_ref, sin_ref, kv, key_out, value_out, attn_out, attn
):
    total = p0[...] + p1[...].astype(F32) + p2[...].astype(F32) + p3[...].astype(F32)
    turned = total * cos_ref[...] + pltpu.roll(total, HD // 2, 1) * sin_ref[...]
    turned = turned.astype(BF16)
    key_out[...] = turned[:LC]
    value_out[...] = turned[VALUES : VALUES + LC]
    scale = 1.0 / math.sqrt(HD)
    more_key = turned[:VALUES]
    more_value = turned[VALUES:QUERY]
    slots = kv.shape[2]
    contract = (((1,), (1,)), ((), ()))
    for r in range(ROWS_DEV):
        q = turned[QUERY + 16 * r : QUERY + 16 * (r + 1)]
        s = lax.dot_general(q, kv[0, r], contract, preferred_element_type=F32) * scale
        live = lax.broadcasted_iota(jnp.int32, s.shape, 1) < len_ref[r]
        s = jnp.where(live, s, -jnp.inf)
        s_more = lax.dot_general(q, more_key, contract, preferred_element_type=F32) * scale
        lane = lax.broadcasted_iota(jnp.int32, s_more.shape, 1)
        live = lane <= LC if r == 0 else lane == LC + r
        s_more = jnp.where(live, s_more, -jnp.inf)
        highest = jnp.maximum(
            jnp.max(s, axis=1, keepdims=True), jnp.max(s_more, axis=1, keepdims=True)
        )
        e = jnp.exp(s - highest)
        e_more = jnp.exp(s_more - highest)
        total_e = jnp.sum(e, axis=1, keepdims=True) + jnp.sum(e_more, axis=1, keepdims=True)
        out = jnp.dot((e / total_e).astype(BF16), kv[1, r], preferred_element_type=F32)
        out += jnp.dot((e_more / total_e).astype(BF16), more_value, preferred_element_type=F32)
        for h in range(out.shape[0]):
            attn[pl.ds(r, 1), pl.ds(h * HD, HD)] = out[h : h + 1]
    attn_out[...] = attn[...].astype(BF16)


def out_kernel(a0, a1, a2, a3, w0, w1, o0, o3, o2, o1, blocks):
    tag = lax.axis_index("gx") ^ lax.axis_index("gy")
    for s, a in enumerate((a0, a1, a2, a3)):
        blocks[s ^ tag] = a[...].astype(F32)
    lhs = jnp.concatenate([blocks[k] for k in range(4)], axis=0).astype(BF16)
    first = 0
    acc = jnp.zeros((lhs.shape[0], w0.shape[1]), F32)
    for w in (w0, w1):
        last = first + w.shape[0]
        acc += jnp.dot(lhs[:, first:last], w[...], preferred_element_type=F32)
        first = last
    o0[...] = acc[0:2]
    o1[...] = acc[2:4].astype(BF16)
    o2[...] = acc[4:6].astype(BF16)
    o3[...] = acc[6:8].astype(BF16)


def others(blocks, axis):
    return [swap(b, axis, 3 - k) for k, b in enumerate(blocks)]


def per_device(stored_rows, new_rows, w_query, w_key, w_value, w_out, kv_cache, cache_len, owner):
    shape = jax.ShapeDtypeStruct
    depth, query_cols = w_query.shape
    width = w_out.shape[1]
    heads = query_cols // HD
    quarter = query_cols // 4
    semaphores = pltpu.SemaphoreType.DMA
    in_vmem = lambda x: pltpu.with_memory_space_constraint(x, pltpu.VMEM)
    in_hbm = lambda x: pltpu.with_memory_space_constraint(x, pltpu.HBM)
    far = swap(stored_rows, "gy", 2)
    near = swap(stored_rows, "gy", 1)
    fresh = [swap(new_rows, "gy", k) for k in (1, 2, 3)]
    cos, sin, wo_first, wkv = pl.pallas_call(
        load_kernel,
        out_shape=[pltpu.VMEM((PAY, HD), F32)] * 2
        + [
            pltpu.VMEM((query_cols - quarter, width), BF16),
            pltpu.VMEM((depth, 2 * HD), BF16),
        ],
        in_specs=[whole(pltpu.HBM)] * 4,
        out_specs=[whole()] * 4,
        scratch_shapes=[pltpu.SMEM(cache_len.shape, jnp.int32), semaphores((9,))],
        compiler_params=params(4),
        cost_estimate=cost(1000, 2 * depth * query_cols),
        name="load",
    )(
        in_hbm(cache_len), in_hbm(w_out), in_hbm(w_key), in_hbm(w_value)
    )
    own = pl.pallas_call(
        own_kernel,
        out_shape=pltpu.VMEM((LC, 2 * HD), F32),
        in_specs=[whole()] * 2,
        out_specs=whole(),
        compiler_params=params(4),
        cost_estimate=cost(2 * LC * depth * 256, 4 * depth * HD),
        name="own",
    )(stored_rows, wkv)
    far, own, *fresh = lax.optimization_barrier((far, own, *fresh))
    far_near = swap(far, "gy", 1)
    fresh = [new_rows] + fresh
    query, wo_second = pl.pallas_call(
        functools.partial(query_kernel, query_cols - quarter),
        out_shape=[
            pltpu.VMEM((4 * ROWS_DEV, heads, HD), F32),
            pltpu.VMEM((quarter, width), BF16),
        ],
        in_specs=[whole(pl.ANY)] + [whole()] * 5 + [whole(pltpu.HBM)],
        out_specs=[whole()] * 2,
        scratch_shapes=[pltpu.VMEM((4 * ROWS_DEV, query_cols), F32), semaphores((2,))],
        compiler_params=params(4),
        cost_estimate=cost(2 * 8 * depth * query_cols, 4 * depth * HD),
        name="query",
    )(far, *fresh, in_vmem(w_query), in_hbm(w_out))
    payload = pl.pallas_call(
        payload_kernel,
        out_shape=[shape((PAY, HD), F32)] + [shape((PAY, HD), BF16)] * 3,
        in_specs=[whole(pltpu.SMEM)] + [whole()] * 10,
        out_specs=[whole()] * 4,
        scratch_shapes=[
            pltpu.VMEM((3 * ROW_TILE + 16, depth), BF16),
            pltpu.VMEM((4, PAY, HD), F32),
        ],
        compiler_params=params(8),
        cost_estimate=cost(2 * 208 * depth * 256, 4 * depth * HD),
        name="payload",
    )(owner, own, near, far, far_near, *fresh, wkv, query)
    sums = [payload[0]] + others(payload[1:], "gx")
    rebuilt_key, rebuilt_value, attn = pl.pallas_call(
        attend_kernel,
        out_shape=[pltpu.VMEM((LC, HD), BF16)] * 2 + [pltpu.VMEM((ROWS_DEV, query_cols), BF16)],
        in_specs=[whole(pltpu.SMEM)] + [whole()] * 7,
        out_specs=[whole()] * 3,
        scratch_shapes=[pltpu.VMEM((ROWS_DEV, query_cols), F32)],
        compiler_params=params(4),
        cost_estimate=cost(10000000, 1000000),
        name="attend",
    )(cache_len, *sums, cos, sin, kv_cache)
    attn_all = [attn] + [swap(attn, "gx", k) for k in (1, 2, 3)]
    parts = pl.pallas_call(
        out_kernel,
        out_shape=[shape((ROWS_DEV, width), F32)] + [shape((ROWS_DEV, width), BF16)] * 3,
        in_specs=[whole()] * 6,
        out_specs=[whole()] * 4,
        scratch_shapes=[pltpu.VMEM((4, ROWS_DEV, query_cols), F32)],
        compiler_params=params(4),
        cost_estimate=cost(2 * 8 * width * query_cols, 2 * width * query_cols),
        name="project",
    )(*attn_all, wo_first, wo_second)
    arrived = others(parts[1:], "gy")
    mixed = parts[0] + arrived[0].astype(F32) + arrived[1].astype(F32) + arrived[2].astype(F32)
    return (mixed.astype(BF16), rebuilt_key[None], rebuilt_value[None])


def solution(mesh):
    direct = mesh.shape["gx"] == 4 and mesh.shape["gy"] == 4
    in_specs = (
        P(("groups", "gy"), "gx"),
        P(("groups", "gy"), "gx"),
        P("gx", "gy"),
        P("gx", "gy"),
        P("gx", "gy"),
        P("gy", "gx"),
        P(None, ("groups", "gx"), None, "gy"),
        P(("groups", "gx")),
        P("groups"),
    )
    out_specs = (
        P(("groups", "gy"), "gx"),
        P(("groups", "gx"), None, "gy"),
        P(("groups", "gx"), None, "gy"),
    )
    return jax.shard_map(
        per_device if direct else general, mesh=mesh, in_specs=in_specs, out_specs=out_specs, check_vma=False
    )
```

```python
import functools
import math

import jax
import jax.numpy as jnp
from jax import lax
from jax.experimental import pallas as pl
from jax.experimental.pallas import tpu as pltpu
from jax.sharding import PartitionSpec as P

HD = 128
LC = 40
ROWS_DEV = 2
BASE = 500000.0
DIRECT = 8


def rotate(values, position):
    half = values.shape[-1] // 2
    index_row = jnp.arange(half).astype(jnp.float32)
    frequency = jnp.exp(index_row * (-2.0 * math.log(BASE) / values.shape[-1]))
    angle = position.astype(jnp.float32)[..., None] * frequency
    cosine = jnp.cos(angle)
    sine = jnp.sin(angle)
    first_half = values[..., :half]
    second_half = values[..., half:]
    return jnp.concatenate(
        [first_half * cosine - second_half * sine, second_half * cosine + first_half * sine],
        axis=-1,
    )


def swap(x, axis, k):
    n = lax.axis_size(axis)
    return lax.ppermute(x, axis, [(i, i ^ k) for i in range(n)])


def gather(x, axis):
    n = lax.axis_size(axis)
    if n > DIRECT or n & (n - 1):
        return lax.all_gather(x, axis, axis=0)
    me = lax.axis_index(axis)
    out = jnp.zeros((n,) + x.shape, x.dtype)
    for k in range(n):
        block = x if k == 0 else swap(x, axis, k)
        out = lax.dynamic_update_index_in_dim(out, block, me ^ k, 0)
    return out


def scatter_sum(parts, axis):
    n = lax.axis_size(axis)
    me = lax.axis_index(axis)
    if n > DIRECT or n & (n - 1):
        whole = jnp.stack([parts(d) for d in range(n)])
        return lax.psum_scatter(whole.astype(jnp.float32), axis, scatter_dimension=0)
    total = parts(me).astype(jnp.float32)
    for k in range(1, n):
        total = total + swap(parts(me ^ k).astype(jnp.bfloat16), axis, k).astype(jnp.float32)
    return total


def general(stored_rows, new_rows, w_query, w_key, w_value, w_out, kv_cache, cache_len, owner):
    owners = lax.axis_size("gx")
    key_cols = w_key.shape[1]
    query_cols = w_query.shape[1]
    heads_here = key_cols // HD
    group_size = query_cols // key_cols
    slot_ids = jnp.arange(owners, dtype=jnp.int32)
    inverse = jnp.sum(jnp.where(owner[None, :] == slot_ids[:, None], slot_ids[None, :], 0), axis=1)

    fresh_all = gather(new_rows, "gy").reshape(-1, new_rows.shape[1])
    stored_all = gather(stored_rows, "gy").reshape(owners, LC, stored_rows.shape[1])
    flat = stored_all.reshape(owners * LC, stored_rows.shape[1])
    query_part = jnp.dot(fresh_all, w_query, preferred_element_type=jnp.float32)
    new_key_part = jnp.dot(fresh_all, w_key, preferred_element_type=jnp.float32)
    new_value_part = jnp.dot(fresh_all, w_value, preferred_element_type=jnp.float32)
    key_part = jnp.dot(flat, w_key, preferred_element_type=jnp.float32)
    value_part = jnp.dot(flat, w_value, preferred_element_type=jnp.float32)

    small = jnp.concatenate([query_part, new_key_part, new_value_part], axis=1)
    small = small.reshape(owners, ROWS_DEV, -1)
    large = jnp.concatenate([key_part, value_part], axis=1).reshape(owners, LC, -1)

    small_sum = scatter_sum(lambda d: lax.dynamic_index_in_dim(small, d, 0, False), "gx")
    large_sum = scatter_sum(
        lambda d: lax.dynamic_index_in_dim(
            large, lax.dynamic_index_in_dim(inverse, d, 0, False), 0, False
        ),
        "gx",
    )
    query = small_sum[:, :query_cols]
    fresh_key = small_sum[:, query_cols : query_cols + key_cols]
    fresh_value = small_sum[:, query_cols + key_cols :]
    own_key = large_sum[:, :key_cols]
    own_value = large_sum[:, key_cols:]

    first_len = cache_len[0]
    tail_pos = first_len + jnp.arange(LC, dtype=jnp.int32)
    rebuilt_key = (
        rotate(own_key.reshape(LC, heads_here, HD), tail_pos[:, None])
        .reshape(LC, key_cols)
        .astype(jnp.bfloat16)
    )
    rebuilt_value = own_value.astype(jnp.bfloat16)
    resumed = jnp.arange(ROWS_DEV, dtype=jnp.int32) == 0
    new_pos = cache_len + jnp.where(resumed, LC, 0).astype(jnp.int32)
    query_rot = rotate(query.reshape(ROWS_DEV, query_cols // HD, HD), new_pos[:, None]).astype(
        jnp.bfloat16
    )
    key_rot = rotate(fresh_key.reshape(ROWS_DEV, heads_here, HD), new_pos[:, None]).astype(
        jnp.bfloat16
    )
    value_new = fresh_value.reshape(ROWS_DEV, heads_here, HD).astype(jnp.bfloat16)
    scale = 1.0 / math.sqrt(HD)
    slots = kv_cache.shape[2]
    grouped = query_rot.reshape(ROWS_DEV, heads_here, group_size, HD)
    cache_key = kv_cache[0].reshape(ROWS_DEV, slots, heads_here, HD)
    cache_value = kv_cache[1].reshape(ROWS_DEV, slots, heads_here, HD)
    tail_key = rebuilt_key.reshape(LC, heads_here, HD)
    tail_value = rebuilt_value.reshape(LC, heads_here, HD)
    live = jnp.arange(slots, dtype=jnp.int32)[None, :] < cache_len[:, None]
    dot = lambda spec, a, b: jnp.einsum(spec, a, b, preferred_element_type=jnp.float32)
    s_cache = dot("bkgd,blkd->bkgl", grouped, cache_key) * scale
    s_cache = jnp.where(live[:, None, None, :], s_cache, -jnp.inf)
    s_tail = dot("bkgd,tkd->bkgt", grouped, tail_key) * scale
    s_tail = jnp.where(resumed[:, None, None, None], s_tail, -jnp.inf)
    s_self = dot("bkgd,bkd->bkg", grouped, key_rot) * scale
    highest = jnp.maximum(jnp.maximum(jnp.max(s_cache, axis=-1), jnp.max(s_tail, axis=-1)), s_self)
    e_cache = jnp.exp(s_cache - highest[..., None])
    e_tail = jnp.exp(s_tail - highest[..., None])
    e_self = jnp.exp(s_self - highest)
    denominator = jnp.sum(e_cache, axis=-1) + jnp.sum(e_tail, axis=-1) + e_self
    w_cache = (e_cache / denominator[..., None]).astype(jnp.bfloat16)
    w_tail = (e_tail / denominator[..., None]).astype(jnp.bfloat16)
    w_self = (e_self / denominator).astype(jnp.bfloat16)
    attn = dot("bkgl,blkd->bkgd", w_cache, cache_value)
    attn = attn + dot("bkgt,tkd->bkgd", w_tail, tail_value)
    attn = (
        attn + w_self.astype(jnp.float32)[..., None] * value_new.astype(jnp.float32)[:, :, None, :]
    )
    attn = attn.reshape(ROWS_DEV, query_cols).astype(jnp.bfloat16)

    attn_all = gather(attn, "gx").reshape(owners * ROWS_DEV, query_cols)
    out_part = jnp.dot(attn_all, w_out, preferred_element_type=jnp.float32)
    out_part = out_part.reshape(lax.axis_size("gy"), -1, w_out.shape[1])
    mixed = scatter_sum(lambda d: lax.dynamic_index_in_dim(out_part, d, 0, False), "gy")
    return (mixed.astype(jnp.bfloat16), rebuilt_key[None], rebuilt_value[None])


ROW_TILE = 48
PAY = 128
VALUES = 48
QUERY = 96
F32 = jnp.float32
BF16 = jnp.bfloat16


def whole(space=pltpu.VMEM):
    return pl.BlockSpec(memory_space=space)


def params(limit):
    return pltpu.CompilerParams(vmem_limit_bytes=limit * 1024 * 1024)


def cost(flops, bytes_accessed):
    return pl.CostEstimate(flops=flops, bytes_accessed=bytes_accessed, transcendentals=0)


def angles(len_ref, cos_ref, sin_ref):
    first, second = len_ref[0], len_ref[1]
    row = lax.broadcasted_iota(jnp.int32, (PAY, HD), 0)
    lane = lax.broadcasted_iota(jnp.int32, (PAY, HD), 1)
    resumed = (row == LC) | ((row >= QUERY) & (row < QUERY + 16))
    other = (row == LC + 1) | (row >= QUERY + 16)
    position = jnp.where(row < LC, first + row, 0)
    position = jnp.where(resumed, first + LC, jnp.where(other, second, position))
    half = lax.rem(lane, HD // 2).astype(F32)
    frequency = jnp.exp(half * (-2.0 * math.log(BASE) / HD))
    angle = position.astype(F32) * frequency
    sine = jnp.sin(angle)
    cos_ref[...] = jnp.cos(angle)
    sin_ref[...] = jnp.where(lane < HD // 2, -sine, sine)


def start_load(source, target, sems, first, pieces):
    copies = []
    rows = source.shape[0] // pieces
    for c in range(pieces):
        part = pl.ds(c * rows, rows)
        copy = pltpu.make_async_copy(source.at[part], target.at[part], sems.at[first + c])
        copy.start()
        copies.append(copy)
    return copies


def load_kernel(
    len_hbm, wo_hbm, wk_hbm, wv_hbm, cos_ref, sin_ref, wo, wkv, len_ref, sems
):
    lengths = pltpu.make_async_copy(len_hbm, len_ref, sems.at[0])
    lengths.start()
    copies = start_load(wk_hbm, wkv.at[:, pl.ds(0, HD)], sems, 1, 1)
    copies += start_load(wv_hbm, wkv.at[:, pl.ds(HD, HD)], sems, 2, 1)
    copies += start_load(wo_hbm.at[pl.ds(0, wo.shape[0])], wo, sems, 3, 6)
    lengths.wait()
    angles(len_ref, cos_ref, sin_ref)
    for copy in copies:
        copy.wait()


def own_kernel(s, wkv, out):
    out[...] = jnp.dot(s[...], wkv[...], preferred_element_type=F32)


def query_kernel(first, far, b0, b1, b2, b3, w, wo_hbm, out_ref, wo, acc, sems):
    rows = wo.shape[0]
    copies = start_load(wo_hbm.at[pl.ds(first, rows)], wo, sems, 0, 2)
    lhs = jnp.concatenate([b[...].astype(F32) for b in (b0, b1, b2, b3)], axis=0).astype(BF16)
    acc[...] = jnp.dot(lhs, w[...], preferred_element_type=F32)
    for r in range(acc.shape[0]):
        for h in range(out_ref.shape[1]):
            out_ref[r, pl.ds(h, 1), :] = acc[pl.ds(r, 1), pl.ds(h * HD, HD)]
    for copy in copies:
        copy.wait()


def payload_kernel(
    owner_ref, own, s1, s2, s3, b0, b1, b2, b3, wkv, q_ref, o0, o3, o2, o1, x, pay
):
    gx, gy = lax.axis_index("gx"), lax.axis_index("gy")
    for k, s in enumerate((s1, s2, s3)):
        x[pl.ds(k * ROW_TILE, LC), :] = s[...]
    fresh = [b[...].astype(F32) for b in (b0, b1, b2, b3)]
    fresh.append(jnp.zeros((8, x.shape[1]), F32))
    base = 3 * ROW_TILE
    x[pl.ds(base, 16), :] = jnp.concatenate(fresh, axis=0).astype(BF16)
    late = jnp.dot(x[...], wkv[...], preferred_element_type=F32)
    empty = jnp.zeros((8 - ROWS_DEV, HD), F32)
    for k in range(4):
        target = owner_ref[gy ^ k] ^ gx
        both = late[(k - 1) * ROW_TILE : (k - 1) * ROW_TILE + LC] if k else own[...]
        pay[target, pl.ds(0, LC), :] = both[:, :HD]
        pay[target, pl.ds(VALUES, LC), :] = both[:, HD:]
        both = late[base + k * ROWS_DEV : base + (k + 1) * ROWS_DEV]
        target = k ^ gx ^ gy
        pay[target, pl.ds(LC, 8), :] = jnp.concatenate([both[:, :HD], empty], axis=0)
        pay[target, pl.ds(VALUES + LC, 8), :] = jnp.concatenate([both[:, HD:], empty], axis=0)
        for r in range(ROWS_DEV):
            pay[target, pl.ds(QUERY + 16 * r, 16), :] = q_ref[k * ROWS_DEV + r]
    o0[...] = pay[0]
    o3[...] = pay[3].astype(BF16)
    o2[...] = pay[2].astype(BF16)
    o1[...] = pay[1].astype(BF16)


def attend_kernel(
    len_ref, p0, p1, p2, p3, cos_ref, sin_ref, kv, key_out, value_out, attn_out, attn
):
    total = p0[...] + p1[...].astype(F32) + p2[...].astype(F32) + p3[...].astype(F32)
    turned = total * cos_ref[...] + pltpu.roll(total, HD // 2, 1) * sin_ref[...]
    turned = turned.astype(BF16)
    key_out[...] = turned[:LC]
    value_out[...] = turned[VALUES : VALUES + LC]
    scale = 1.0 / math.sqrt(HD)
    more_key = turned[:VALUES]
    more_value = turned[VALUES:QUERY]
    slots = kv.shape[2]
    contract = (((1,), (1,)), ((), ()))
    for r in range(ROWS_DEV):
        q = turned[QUERY + 16 * r : QUERY + 16 * (r + 1)]
        s = lax.dot_general(q, kv[0, r], contract, preferred_element_type=F32) * scale
        live = lax.broadcasted_iota(jnp.int32, s.shape, 1) < len_ref[r]
        s = jnp.where(live, s, -jnp.inf)
        s_more = lax.dot_general(q, more_key, contract, preferred_element_type=F32) * scale
        lane = lax.broadcasted_iota(jnp.int32, s_more.shape, 1)
        live = lane <= LC if r == 0 else lane == LC + r
        s_more = jnp.where(live, s_more, -jnp.inf)
        highest = jnp.maximum(
            jnp.max(s, axis=1, keepdims=True), jnp.max(s_more, axis=1, keepdims=True)
        )
        e = jnp.exp(s - highest)
        e_more = jnp.exp(s_more - highest)
        total_e = jnp.sum(e, axis=1, keepdims=True) + jnp.sum(e_more, axis=1, keepdims=True)
        out = jnp.dot((e / total_e).astype(BF16), kv[1, r], preferred_element_type=F32)
        out += jnp.dot((e_more / total_e).astype(BF16), more_value, preferred_element_type=F32)
        for h in range(out.shape[0]):
            attn[pl.ds(r, 1), pl.ds(h * HD, HD)] = out[h : h + 1]
    attn_out[...] = attn[...].astype(BF16)


def out_kernel(a0, a1, a2, a3, w0, w1, o0, o3, o2, o1, blocks):
    tag = lax.axis_index("gx") ^ lax.axis_index("gy")
    for s, a in enumerate((a0, a1, a2, a3)):
        blocks[s ^ tag] = a[...].astype(F32)
    lhs = jnp.concatenate([blocks[k] for k in range(4)], axis=0).astype(BF16)
    first = 0
    acc = jnp.zeros((lhs.shape[0], w0.shape[1]), F32)
    for w in (w0, w1):
        last = first + w.shape[0]
        acc += jnp.dot(lhs[:, first:last], w[...], preferred_element_type=F32)
        first = last
    o0[...] = acc[0:2]
    o1[...] = acc[2:4].astype(BF16)
    o2[...] = acc[4:6].astype(BF16)
    o3[...] = acc[6:8].astype(BF16)


def others(blocks, axis):
    return [swap(b, axis, 3 - k) for k, b in enumerate(blocks)]


def per_device(stored_rows, new_rows, w_query, w_key, w_value, w_out, kv_cache, cache_len, owner):
    shape = jax.ShapeDtypeStruct
    depth, query_cols = w_query.shape
    width = w_out.shape[1]
    heads = query_cols // HD
    quarter = query_cols // 4
    semaphores = pltpu.SemaphoreType.DMA
    in_vmem = lambda x: pltpu.with_memory_space_constraint(x, pltpu.VMEM)
    in_hbm = lambda x: pltpu.with_memory_space_constraint(x, pltpu.HBM)
    far = swap(stored_rows, "gy", 2)
    near = swap(stored_rows, "gy", 1)
    fresh = [swap(new_rows, "gy", k) for k in (1, 2, 3)]
    cos, sin, wo_first, wkv = pl.pallas_call(
        load_kernel,
        out_shape=[pltpu.VMEM((PAY, HD), F32)] * 2
        + [
            pltpu.VMEM((query_cols - quarter, width), BF16),
            pltpu.VMEM((depth, 2 * HD), BF16),
        ],
        in_specs=[whole(pltpu.HBM)] * 4,
        out_specs=[whole()] * 4,
        scratch_shapes=[pltpu.SMEM(cache_len.shape, jnp.int32), semaphores((9,))],
        compiler_params=params(4),
        cost_estimate=cost(1000, 2 * depth * query_cols),
        name="load",
    )(
        in_hbm(cache_len), in_hbm(w_out), in_hbm(w_key), in_hbm(w_value)
    )
    own = pl.pallas_call(
        own_kernel,
        out_shape=pltpu.VMEM((LC, 2 * HD), F32),
        in_specs=[whole()] * 2,
        out_specs=whole(),
        compiler_params=params(4),
        cost_estimate=cost(2 * LC * depth * 256, 4 * depth * HD),
        name="own",
    )(stored_rows, wkv)
    far, own, *fresh = lax.optimization_barrier((far, own, *fresh))
    far_near = swap(far, "gy", 1)
    fresh = [new_rows] + fresh
    query, wo_second = pl.pallas_call(
        functools.partial(query_kernel, query_cols - quarter),
        out_shape=[
            pltpu.VMEM((4 * ROWS_DEV, heads, HD), F32),
            pltpu.VMEM((quarter, width), BF16),
        ],
        in_specs=[whole(pl.ANY)] + [whole()] * 5 + [whole(pltpu.HBM)],
        out_specs=[whole()] * 2,
        scratch_shapes=[pltpu.VMEM((4 * ROWS_DEV, query_cols), F32), semaphores((2,))],
        compiler_params=params(4),
        cost_estimate=cost(2 * 8 * depth * query_cols, 4 * depth * HD),
        name="query",
    )(far, *fresh, in_vmem(w_query), in_hbm(w_out))
    payload = pl.pallas_call(
        payload_kernel,
        out_shape=[shape((PAY, HD), F32)] + [shape((PAY, HD), BF16)] * 3,
        in_specs=[whole(pltpu.SMEM)] + [whole()] * 10,
        out_specs=[whole()] * 4,
        scratch_shapes=[
            pltpu.VMEM((3 * ROW_TILE + 16, depth), BF16),
            pltpu.VMEM((4, PAY, HD), F32),
        ],
        compiler_params=params(8),
        cost_estimate=cost(2 * 208 * depth * 256, 4 * depth * HD),
        name="payload",
    )(owner, own, near, far, far_near, *fresh, wkv, query)
    sums = [payload[0]] + others(payload[1:], "gx")
    rebuilt_key, rebuilt_value, attn = pl.pallas_call(
        attend_kernel,
        out_shape=[pltpu.VMEM((LC, HD), BF16)] * 2 + [pltpu.VMEM((ROWS_DEV, query_cols), BF16)],
        in_specs=[whole(pltpu.SMEM)] + [whole()] * 7,
        out_specs=[whole()] * 3,
        scratch_shapes=[pltpu.VMEM((ROWS_DEV, query_cols), F32)],
        compiler_params=params(4),
        cost_estimate=cost(10000000, 1000000),
        name="attend",
    )(cache_len, *sums, cos, sin, kv_cache)
    attn_all = [attn] + [swap(attn, "gx", k) for k in (1, 2, 3)]
    parts = pl.pallas_call(
        out_kernel,
        out_shape=[shape((ROWS_DEV, width), F32)] + [shape((ROWS_DEV, width), BF16)] * 3,
        in_specs=[whole()] * 6,
        out_specs=[whole()] * 4,
        scratch_shapes=[pltpu.VMEM((4, ROWS_DEV, query_cols), F32)],
        compiler_params=params(4),
        cost_estimate=cost(2 * 8 * width * query_cols, 2 * width * query_cols),
        name="project",
    )(*attn_all, wo_first, wo_second)
    arrived = others(parts[1:], "gy")
    mixed = parts[0] + arrived[0].astype(F32) + arrived[1].astype(F32) + arrived[2].astype(F32)
    return (mixed.astype(BF16), rebuilt_key[None], rebuilt_value[None])


def solution(mesh):
    direct = mesh.shape["gx"] == 4 and mesh.shape["gy"] == 4
    in_specs = (
        P(("groups", "gy"), "gx"),
        P(("groups", "gy"), "gx"),
        P("gx", "gy"),
        P("gx", "gy"),
        P("gx", "gy"),
        P("gy", "gx"),
        P(None, ("groups", "gx"), None, "gy"),
        P(("groups", "gx")),
        P("groups"),
    )
    out_specs = (
        P(("groups", "gy"), "gx"),
        P(("groups", "gx"), None, "gy"),
        P(("groups", "gx"), None, "gy"),
    )
    return jax.shard_map(
        per_device if direct else general, mesh=mesh, in_specs=in_specs, out_specs=out_specs, check_vma=False
    )
```

```python
import functools
import math

import jax
import jax.numpy as jnp
from jax import lax
from jax.experimental import pallas as pl
from jax.experimental.pallas import tpu as pltpu
from jax.sharding import PartitionSpec as P

HD = 128
LC = 40
ROWS_DEV = 2
BASE = 500000.0
DIRECT = 8


def rotate(values, position):
    half = values.shape[-1] // 2
    index_row = jnp.arange(half).astype(jnp.float32)
    frequency = jnp.exp(index_row * (-2.0 * math.log(BASE) / values.shape[-1]))
    angle = position.astype(jnp.float32)[..., None] * frequency
    cosine = jnp.cos(angle)
    sine = jnp.sin(angle)
    first_half = values[..., :half]
    second_half = values[..., half:]
    return jnp.concatenate(
        [first_half * cosine - second_half * sine, second_half * cosine + first_half * sine],
        axis=-1,
    )


def swap(x, axis, k):
    n = lax.axis_size(axis)
    return lax.ppermute(x, axis, [(i, i ^ k) for i in range(n)])


def gather(x, axis):
    n = lax.axis_size(axis)
    if n > DIRECT or n & (n - 1):
        return lax.all_gather(x, axis, axis=0)
    me = lax.axis_index(axis)
    out = jnp.zeros((n,) + x.shape, x.dtype)
    for k in range(n):
        block = x if k == 0 else swap(x, axis, k)
        out = lax.dynamic_update_index_in_dim(out, block, me ^ k, 0)
    return out


def scatter_sum(parts, axis):
    n = lax.axis_size(axis)
    me = lax.axis_index(axis)
    if n > DIRECT or n & (n - 1):
        whole = jnp.stack([parts(d) for d in range(n)])
        return lax.psum_scatter(whole.astype(jnp.float32), axis, scatter_dimension=0)
    total = parts(me).astype(jnp.float32)
    for k in range(1, n):
        total = total + swap(parts(me ^ k).astype(jnp.bfloat16), axis, k).astype(jnp.float32)
    return total


def general(stored_rows, new_rows, w_query, w_key, w_value, w_out, kv_cache, cache_len, owner):
    owners = lax.axis_size("gx")
    key_cols = w_key.shape[1]
    query_cols = w_query.shape[1]
    heads_here = key_cols // HD
    group_size = query_cols // key_cols
    slot_ids = jnp.arange(owners, dtype=jnp.int32)
    inverse = jnp.sum(jnp.where(owner[None, :] == slot_ids[:, None], slot_ids[None, :], 0), axis=1)

    fresh_all = gather(new_rows, "gy").reshape(-1, new_rows.shape[1])
    stored_all = gather(stored_rows, "gy").reshape(owners, LC, stored_rows.shape[1])
    flat = stored_all.reshape(owners * LC, stored_rows.shape[1])
    query_part = jnp.dot(fresh_all, w_query, preferred_element_type=jnp.float32)
    new_key_part = jnp.dot(fresh_all, w_key, preferred_element_type=jnp.float32)
    new_value_part = jnp.dot(fresh_all, w_value, preferred_element_type=jnp.float32)
    key_part = jnp.dot(flat, w_key, preferred_element_type=jnp.float32)
    value_part = jnp.dot(flat, w_value, preferred_element_type=jnp.float32)

    small = jnp.concatenate([query_part, new_key_part, new_value_part], axis=1)
    small = small.reshape(owners, ROWS_DEV, -1)
    large = jnp.concatenate([key_part, value_part], axis=1).reshape(owners, LC, -1)

    small_sum = scatter_sum(lambda d: lax.dynamic_index_in_dim(small, d, 0, False), "gx")
    large_sum = scatter_sum(
        lambda d: lax.dynamic_index_in_dim(
            large, lax.dynamic_index_in_dim(inverse, d, 0, False), 0, False
        ),
        "gx",
    )
    query = small_sum[:, :query_cols]
    fresh_key = small_sum[:, query_cols : query_cols + key_cols]
    fresh_value = small_sum[:, query_cols + key_cols :]
    own_key = large_sum[:, :key_cols]
    own_value = large_sum[:, key_cols:]

    first_len = cache_len[0]
    tail_pos = first_len + jnp.arange(LC, dtype=jnp.int32)
    rebuilt_key = (
        rotate(own_key.reshape(LC, heads_here, HD), tail_pos[:, None])
        .reshape(LC, key_cols)
        .astype(jnp.bfloat16)
    )
    rebuilt_value = own_value.astype(jnp.bfloat16)
    resumed = jnp.arange(ROWS_DEV, dtype=jnp.int32) == 0
    new_pos = cache_len + jnp.where(resumed, LC, 0).astype(jnp.int32)
    query_rot = rotate(query.reshape(ROWS_DEV, query_cols // HD, HD), new_pos[:, None]).astype(
        jnp.bfloat16
    )
    key_rot = rotate(fresh_key.reshape(ROWS_DEV, heads_here, HD), new_pos[:, None]).astype(
        jnp.bfloat16
    )
    value_new = fresh_value.reshape(ROWS_DEV, heads_here, HD).astype(jnp.bfloat16)
    scale = 1.0 / math.sqrt(HD)
    slots = kv_cache.shape[2]
    grouped = query_rot.reshape(ROWS_DEV, heads_here, group_size, HD)
    cache_key = kv_cache[0].reshape(ROWS_DEV, slots, heads_here, HD)
    cache_value = kv_cache[1].reshape(ROWS_DEV, slots, heads_here, HD)
    tail_key = rebuilt_key.reshape(LC, heads_here, HD)
    tail_value = rebuilt_value.reshape(LC, heads_here, HD)
    live = jnp.arange(slots, dtype=jnp.int32)[None, :] < cache_len[:, None]
    dot = lambda spec, a, b: jnp.einsum(spec, a, b, preferred_element_type=jnp.float32)
    s_cache = dot("bkgd,blkd->bkgl", grouped, cache_key) * scale
    s_cache = jnp.where(live[:, None, None, :], s_cache, -jnp.inf)
    s_tail = dot("bkgd,tkd->bkgt", grouped, tail_key) * scale
    s_tail = jnp.where(resumed[:, None, None, None], s_tail, -jnp.inf)
    s_self = dot("bkgd,bkd->bkg", grouped, key_rot) * scale
    highest = jnp.maximum(jnp.maximum(jnp.max(s_cache, axis=-1), jnp.max(s_tail, axis=-1)), s_self)
    e_cache = jnp.exp(s_cache - highest[..., None])
    e_tail = jnp.exp(s_tail - highest[..., None])
    e_self = jnp.exp(s_self - highest)
    denominator = jnp.sum(e_cache, axis=-1) + jnp.sum(e_tail, axis=-1) + e_self
    w_cache = (e_cache / denominator[..., None]).astype(jnp.bfloat16)
    w_tail = (e_tail / denominator[..., None]).astype(jnp.bfloat16)
    w_self = (e_self / denominator).astype(jnp.bfloat16)
    attn = dot("bkgl,blkd->bkgd", w_cache, cache_value)
    attn = attn + dot("bkgt,tkd->bkgd", w_tail, tail_value)
    attn = (
        attn + w_self.astype(jnp.float32)[..., None] * value_new.astype(jnp.float32)[:, :, None, :]
    )
    attn = attn.reshape(ROWS_DEV, query_cols).astype(jnp.bfloat16)

    attn_all = gather(attn, "gx").reshape(owners * ROWS_DEV, query_cols)
    out_part = jnp.dot(attn_all, w_out, preferred_element_type=jnp.float32)
    out_part = out_part.reshape(lax.axis_size("gy"), -1, w_out.shape[1])
    mixed = scatter_sum(lambda d: lax.dynamic_index_in_dim(out_part, d, 0, False), "gy")
    return (mixed.astype(jnp.bfloat16), rebuilt_key[None], rebuilt_value[None])


ROW_TILE = 48
PAY = 128
VALUES = 48
QUERY = 96
F32 = jnp.float32
BF16 = jnp.bfloat16


def whole(space=pltpu.VMEM):
    return pl.BlockSpec(memory_space=space)


def params(limit):
    return pltpu.CompilerParams(vmem_limit_bytes=limit * 1024 * 1024)


def cost(flops, bytes_accessed):
    return pl.CostEstimate(flops=flops, bytes_accessed=bytes_accessed, transcendentals=0)


def angles(len_ref, cos_ref, sin_ref):
    first, second = len_ref[0], len_ref[1]
    row = lax.broadcasted_iota(jnp.int32, (PAY, HD), 0)
    lane = lax.broadcasted_iota(jnp.int32, (PAY, HD), 1)
    resumed = (row == LC) | ((row >= QUERY) & (row < QUERY + 16))
    other = (row == LC + 1) | (row >= QUERY + 16)
    position = jnp.where(row < LC, first + row, 0)
    position = jnp.where(resumed, first + LC, jnp.where(other, second, position))
    half = lax.rem(lane, HD // 2).astype(F32)
    frequency = jnp.exp(half * (-2.0 * math.log(BASE) / HD))
    angle = position.astype(F32) * frequency
    sine = jnp.sin(angle)
    cos_ref[...] = jnp.cos(angle)
    sin_ref[...] = jnp.where(lane < HD // 2, -sine, sine)


def start_load(source, target, sems, first, pieces):
    copies = []
    rows = source.shape[0] // pieces
    for c in range(pieces):
        part = pl.ds(c * rows, rows)
        copy = pltpu.make_async_copy(source.at[part], target.at[part], sems.at[first + c])
        copy.start()
        copies.append(copy)
    return copies


def start_column_load(source, target, sems, first):
    copies = []
    for c in range(target.shape[0]):
        block = source.at[:, pl.ds(c * HD, HD)]
        copy = pltpu.make_async_copy(block, target.at[c], sems.at[first + c])
        copy.start()
        copies.append(copy)
    return copies


def load_kernel(
    len_hbm, wo_hbm, wk_hbm, wv_hbm, cos_ref, sin_ref, wo, wkv, len_ref, sems
):
    lengths = pltpu.make_async_copy(len_hbm, len_ref, sems.at[0])
    lengths.start()
    copies = start_load(wk_hbm, wkv.at[:, pl.ds(0, HD)], sems, 1, 1)
    copies += start_load(wv_hbm, wkv.at[:, pl.ds(HD, HD)], sems, 2, 1)
    copies += start_column_load(wo_hbm.at[pl.ds(0, wo.shape[1])], wo, sems, 3)
    lengths.wait()
    angles(len_ref, cos_ref, sin_ref)
    for copy in copies:
        copy.wait()


def own_kernel(s, wkv, out):
    out[...] = jnp.dot(s[...], wkv[...], preferred_element_type=F32)


def query_kernel(first, far, b0, b1, b2, b3, w, wo_hbm, out_ref, wo, acc, sems):
    copies = start_column_load(wo_hbm.at[pl.ds(first, wo.shape[1])], wo, sems, 0)
    lhs = jnp.concatenate([b[...].astype(F32) for b in (b0, b1, b2, b3)], axis=0).astype(BF16)
    acc[...] = jnp.dot(lhs, w[...], preferred_element_type=F32)
    for r in range(acc.shape[0]):
        for h in range(out_ref.shape[1]):
            out_ref[r, pl.ds(h, 1), :] = acc[pl.ds(r, 1), pl.ds(h * HD, HD)]
    for copy in copies:
        copy.wait()


def payload_kernel(
    owner_ref, own, s1, s2, s3, b0, b1, b2, b3, wkv, q_ref, o0, o3, o2, o1, x, pay
):
    gx, gy = lax.axis_index("gx"), lax.axis_index("gy")
    for k, s in enumerate((s1, s2, s3)):
        x[pl.ds(k * ROW_TILE, LC), :] = s[...]
    fresh = [b[...].astype(F32) for b in (b0, b1, b2, b3)]
    fresh.append(jnp.zeros((8, x.shape[1]), F32))
    base = 3 * ROW_TILE
    x[pl.ds(base, 16), :] = jnp.concatenate(fresh, axis=0).astype(BF16)
    late = jnp.dot(x[...], wkv[...], preferred_element_type=F32)
    empty = jnp.zeros((8 - ROWS_DEV, HD), F32)
    for k in range(4):
        target = owner_ref[gy ^ k] ^ gx
        both = late[(k - 1) * ROW_TILE : (k - 1) * ROW_TILE + LC] if k else own[...]
        pay[target, pl.ds(0, LC), :] = both[:, :HD]
        pay[target, pl.ds(VALUES, LC), :] = both[:, HD:]
        both = late[base + k * ROWS_DEV : base + (k + 1) * ROWS_DEV]
        target = k ^ gx ^ gy
        pay[target, pl.ds(LC, 8), :] = jnp.concatenate([both[:, :HD], empty], axis=0)
        pay[target, pl.ds(VALUES + LC, 8), :] = jnp.concatenate([both[:, HD:], empty], axis=0)
        for r in range(ROWS_DEV):
            pay[target, pl.ds(QUERY + 16 * r, 16), :] = q_ref[k * ROWS_DEV + r]
    o0[...] = pay[0]
    o3[...] = pay[3].astype(BF16)
    o2[...] = pay[2].astype(BF16)
    o1[...] = pay[1].astype(BF16)


def attend_kernel(
    len_ref, p0, p1, p2, p3, cos_ref, sin_ref, kv, key_out, value_out, attn_out, attn
):
    total = p0[...] + p1[...].astype(F32) + p2[...].astype(F32) + p3[...].astype(F32)
    turned = total * cos_ref[...] + pltpu.roll(total, HD // 2, 1) * sin_ref[...]
    turned = turned.astype(BF16)
    key_out[...] = turned[:LC]
    value_out[...] = turned[VALUES : VALUES + LC]
    scale = 1.0 / math.sqrt(HD)
    more_key = turned[:VALUES]
    more_value = turned[VALUES:QUERY]
    slots = kv.shape[2]
    contract = (((1,), (1,)), ((), ()))
    for r in range(ROWS_DEV):
        q = turned[QUERY + 16 * r : QUERY + 16 * (r + 1)]
        s = lax.dot_general(q, kv[0, r], contract, preferred_element_type=F32) * scale
        live = lax.broadcasted_iota(jnp.int32, s.shape, 1) < len_ref[r]
        s = jnp.where(live, s, -jnp.inf)
        s_more = lax.dot_general(q, more_key, contract, preferred_element_type=F32) * scale
        lane = lax.broadcasted_iota(jnp.int32, s_more.shape, 1)
        live = lane <= LC if r == 0 else lane == LC + r
        s_more = jnp.where(live, s_more, -jnp.inf)
        highest = jnp.maximum(
            jnp.max(s, axis=1, keepdims=True), jnp.max(s_more, axis=1, keepdims=True)
        )
        e = jnp.exp(s - highest)
        e_more = jnp.exp(s_more - highest)
        total_e = jnp.sum(e, axis=1, keepdims=True) + jnp.sum(e_more, axis=1, keepdims=True)
        out = jnp.dot((e / total_e).astype(BF16), kv[1, r], preferred_element_type=F32)
        out += jnp.dot((e_more / total_e).astype(BF16), more_value, preferred_element_type=F32)
        for h in range(out.shape[0]):
            attn[pl.ds(r, 1), pl.ds(h * HD, HD)] = out[h : h + 1]
    attn_out[...] = attn[...].astype(BF16)


def out_kernel(a0, a1, a2, a3, w0, w1, o0, o3, o2, o1, blocks):
    tag = lax.axis_index("gx") ^ lax.axis_index("gy")
    for s, a in enumerate((a0, a1, a2, a3)):
        blocks[s ^ tag] = a[...].astype(F32)
    lhs = jnp.concatenate([blocks[k] for k in range(4)], axis=0).astype(BF16)
    acc = None
    first = 0
    for w in (w0, w1):
        last = first + w.shape[1]
        columns = jnp.concatenate([w[c] for c in range(w.shape[0])], axis=1)
        part = jnp.dot(lhs[:, first:last], columns, preferred_element_type=F32)
        acc = part if acc is None else acc + part
        first = last
    o0[...] = acc[0:2]
    o1[...] = acc[2:4].astype(BF16)
    o2[...] = acc[4:6].astype(BF16)
    o3[...] = acc[6:8].astype(BF16)


def others(blocks, axis):
    return [swap(b, axis, 3 - k) for k, b in enumerate(blocks)]


def per_device(stored_rows, new_rows, w_query, w_key, w_value, w_out, kv_cache, cache_len, owner):
    shape = jax.ShapeDtypeStruct
    depth, query_cols = w_query.shape
    width = w_out.shape[1]
    heads = query_cols // HD
    quarter = query_cols // 4
    semaphores = pltpu.SemaphoreType.DMA
    in_vmem = lambda x: pltpu.with_memory_space_constraint(x, pltpu.VMEM)
    in_hbm = lambda x: pltpu.with_memory_space_constraint(x, pltpu.HBM)
    far = swap(stored_rows, "gy", 2)
    near = swap(stored_rows, "gy", 1)
    fresh = [swap(new_rows, "gy", k) for k in (1, 2, 3)]
    cos, sin, wo_first, wkv = pl.pallas_call(
        load_kernel,
        out_shape=[pltpu.VMEM((PAY, HD), F32)] * 2
        + [
            pltpu.VMEM((width // HD, query_cols - quarter, HD), BF16),
            pltpu.VMEM((depth, 2 * HD), BF16),
        ],
        in_specs=[whole(pltpu.HBM)] * 4,
        out_specs=[whole()] * 4,
        scratch_shapes=[pltpu.SMEM(cache_len.shape, jnp.int32), semaphores((3 + width // HD,))],
        compiler_params=params(4),
        cost_estimate=cost(1000, 2 * depth * query_cols),
        name="load",
    )(
        in_hbm(cache_len), in_hbm(w_out), in_hbm(w_key), in_hbm(w_value)
    )
    own = pl.pallas_call(
        own_kernel,
        out_shape=pltpu.VMEM((LC, 2 * HD), F32),
        in_specs=[whole()] * 2,
        out_specs=whole(),
        compiler_params=params(4),
        cost_estimate=cost(2 * LC * depth * 256, 4 * depth * HD),
        name="own",
    )(stored_rows, wkv)
    far, own, *fresh = lax.optimization_barrier((far, own, *fresh))
    far_near = swap(far, "gy", 1)
    fresh = [new_rows] + fresh
    query, wo_second = pl.pallas_call(
        functools.partial(query_kernel, query_cols - quarter),
        out_shape=[
            pltpu.VMEM((4 * ROWS_DEV, heads, HD), F32),
            pltpu.VMEM((width // HD, quarter, HD), BF16),
        ],
        in_specs=[whole(pl.ANY)] + [whole()] * 5 + [whole(pltpu.HBM)],
        out_specs=[whole()] * 2,
        scratch_shapes=[pltpu.VMEM((4 * ROWS_DEV, query_cols), F32), semaphores((width // HD,))],
        compiler_params=params(4),
        cost_estimate=cost(2 * 8 * depth * query_cols, 4 * depth * HD),
        name="query",
    )(far, *fresh, in_vmem(w_query), in_hbm(w_out))
    payload = pl.pallas_call(
        payload_kernel,
        out_shape=[shape((PAY, HD), F32)] + [shape((PAY, HD), BF16)] * 3,
        in_specs=[whole(pltpu.SMEM)] + [whole()] * 10,
        out_specs=[whole()] * 4,
        scratch_shapes=[
            pltpu.VMEM((3 * ROW_TILE + 16, depth), BF16),
            pltpu.VMEM((4, PAY, HD), F32),
        ],
        compiler_params=params(8),
        cost_estimate=cost(2 * 208 * depth * 256, 4 * depth * HD),
        name="payload",
    )(owner, own, near, far, far_near, *fresh, wkv, query)
    sums = [payload[0]] + others(payload[1:], "gx")
    rebuilt_key, rebuilt_value, attn = pl.pallas_call(
        attend_kernel,
        out_shape=[pltpu.VMEM((LC, HD), BF16)] * 2 + [pltpu.VMEM((ROWS_DEV, query_cols), BF16)],
        in_specs=[whole(pltpu.SMEM)] + [whole()] * 7,
        out_specs=[whole()] * 3,
        scratch_shapes=[pltpu.VMEM((ROWS_DEV, query_cols), F32)],
        compiler_params=params(4),
        cost_estimate=cost(10000000, 1000000),
        name="attend",
    )(cache_len, *sums, cos, sin, kv_cache)
    attn_all = [attn] + [swap(attn, "gx", k) for k in (1, 2, 3)]
    parts = pl.pallas_call(
        out_kernel,
        out_shape=[shape((ROWS_DEV, width), F32)] + [shape((ROWS_DEV, width), BF16)] * 3,
        in_specs=[whole()] * 6,
        out_specs=[whole()] * 4,
        scratch_shapes=[pltpu.VMEM((4, ROWS_DEV, query_cols), F32)],
        compiler_params=params(4),
        cost_estimate=cost(2 * 8 * width * query_cols, 2 * width * query_cols),
        name="project",
    )(*attn_all, wo_first, wo_second)
    arrived = others(parts[1:], "gy")
    mixed = parts[0] + arrived[0].astype(F32) + arrived[1].astype(F32) + arrived[2].astype(F32)
    return (mixed.astype(BF16), rebuilt_key[None], rebuilt_value[None])


def solution(mesh):
    direct = mesh.shape["gx"] == 4 and mesh.shape["gy"] == 4
    in_specs = (
        P(("groups", "gy"), "gx"),
        P(("groups", "gy"), "gx"),
        P("gx", "gy"),
        P("gx", "gy"),
        P("gx", "gy"),
        P("gy", "gx"),
        P(None, ("groups", "gx"), None, "gy"),
        P(("groups", "gx")),
        P("groups"),
    )
    out_specs = (
        P(("groups", "gy"), "gx"),
        P(("groups", "gx"), None, "gy"),
        P(("groups", "gx"), None, "gy"),
    )
    return jax.shard_map(
        per_device if direct else general, mesh=mesh, in_specs=in_specs, out_specs=out_specs, check_vma=False
    )
```

```python
import functools
import math

import jax
import jax.numpy as jnp
from jax import lax
from jax.experimental import pallas as pl
from jax.experimental.pallas import tpu as pltpu
from jax.sharding import PartitionSpec as P

HD = 128
LC = 40
ROWS_DEV = 2
BASE = 500000.0
DIRECT = 8


def rotate(values, position):
    half = values.shape[-1] // 2
    index_row = jnp.arange(half).astype(jnp.float32)
    frequency = jnp.exp(index_row * (-2.0 * math.log(BASE) / values.shape[-1]))
    angle = position.astype(jnp.float32)[..., None] * frequency
    cosine = jnp.cos(angle)
    sine = jnp.sin(angle)
    first_half = values[..., :half]
    second_half = values[..., half:]
    return jnp.concatenate(
        [first_half * cosine - second_half * sine, second_half * cosine + first_half * sine],
        axis=-1,
    )


def swap(x, axis, k):
    n = lax.axis_size(axis)
    return lax.ppermute(x, axis, [(i, i ^ k) for i in range(n)])


def gather(x, axis):
    n = lax.axis_size(axis)
    if n > DIRECT or n & (n - 1):
        return lax.all_gather(x, axis, axis=0)
    me = lax.axis_index(axis)
    out = jnp.zeros((n,) + x.shape, x.dtype)
    for k in range(n):
        block = x if k == 0 else swap(x, axis, k)
        out = lax.dynamic_update_index_in_dim(out, block, me ^ k, 0)
    return out


def scatter_sum(parts, axis):
    n = lax.axis_size(axis)
    me = lax.axis_index(axis)
    if n > DIRECT or n & (n - 1):
        whole = jnp.stack([parts(d) for d in range(n)])
        return lax.psum_scatter(whole.astype(jnp.float32), axis, scatter_dimension=0)
    total = parts(me).astype(jnp.float32)
    for k in range(1, n):
        total = total + swap(parts(me ^ k).astype(jnp.bfloat16), axis, k).astype(jnp.float32)
    return total


def general(stored_rows, new_rows, w_query, w_key, w_value, w_out, kv_cache, cache_len, owner):
    owners = lax.axis_size("gx")
    key_cols = w_key.shape[1]
    query_cols = w_query.shape[1]
    heads_here = key_cols // HD
    group_size = query_cols // key_cols
    slot_ids = jnp.arange(owners, dtype=jnp.int32)
    inverse = jnp.sum(jnp.where(owner[None, :] == slot_ids[:, None], slot_ids[None, :], 0), axis=1)

    fresh_all = gather(new_rows, "gy").reshape(-1, new_rows.shape[1])
    stored_all = gather(stored_rows, "gy").reshape(owners, LC, stored_rows.shape[1])
    flat = stored_all.reshape(owners * LC, stored_rows.shape[1])
    query_part = jnp.dot(fresh_all, w_query, preferred_element_type=jnp.float32)
    new_key_part = jnp.dot(fresh_all, w_key, preferred_element_type=jnp.float32)
    new_value_part = jnp.dot(fresh_all, w_value, preferred_element_type=jnp.float32)
    key_part = jnp.dot(flat, w_key, preferred_element_type=jnp.float32)
    value_part = jnp.dot(flat, w_value, preferred_element_type=jnp.float32)

    small = jnp.concatenate([query_part, new_key_part, new_value_part], axis=1)
    small = small.reshape(owners, ROWS_DEV, -1)
    large = jnp.concatenate([key_part, value_part], axis=1).reshape(owners, LC, -1)

    small_sum = scatter_sum(lambda d: lax.dynamic_index_in_dim(small, d, 0, False), "gx")
    large_sum = scatter_sum(
        lambda d: lax.dynamic_index_in_dim(
            large, lax.dynamic_index_in_dim(inverse, d, 0, False), 0, False
        ),
        "gx",
    )
    query = small_sum[:, :query_cols]
    fresh_key = small_sum[:, query_cols : query_cols + key_cols]
    fresh_value = small_sum[:, query_cols + key_cols :]
    own_key = large_sum[:, :key_cols]
    own_value = large_sum[:, key_cols:]

    first_len = cache_len[0]
    tail_pos = first_len + jnp.arange(LC, dtype=jnp.int32)
    rebuilt_key = (
        rotate(own_key.reshape(LC, heads_here, HD), tail_pos[:, None])
        .reshape(LC, key_cols)
        .astype(jnp.bfloat16)
    )
    rebuilt_value = own_value.astype(jnp.bfloat16)
    resumed = jnp.arange(ROWS_DEV, dtype=jnp.int32) == 0
    new_pos = cache_len + jnp.where(resumed, LC, 0).astype(jnp.int32)
    query_rot = rotate(query.reshape(ROWS_DEV, query_cols // HD, HD), new_pos[:, None]).astype(
        jnp.bfloat16
    )
    key_rot = rotate(fresh_key.reshape(ROWS_DEV, heads_here, HD), new_pos[:, None]).astype(
        jnp.bfloat16
    )
    value_new = fresh_value.reshape(ROWS_DEV, heads_here, HD).astype(jnp.bfloat16)
    scale = 1.0 / math.sqrt(HD)
    slots = kv_cache.shape[2]
    grouped = query_rot.reshape(ROWS_DEV, heads_here, group_size, HD)
    cache_key = kv_cache[0].reshape(ROWS_DEV, slots, heads_here, HD)
    cache_value = kv_cache[1].reshape(ROWS_DEV, slots, heads_here, HD)
    tail_key = rebuilt_key.reshape(LC, heads_here, HD)
    tail_value = rebuilt_value.reshape(LC, heads_here, HD)
    live = jnp.arange(slots, dtype=jnp.int32)[None, :] < cache_len[:, None]
    dot = lambda spec, a, b: jnp.einsum(spec, a, b, preferred_element_type=jnp.float32)
    s_cache = dot("bkgd,blkd->bkgl", grouped, cache_key) * scale
    s_cache = jnp.where(live[:, None, None, :], s_cache, -jnp.inf)
    s_tail = dot("bkgd,tkd->bkgt", grouped, tail_key) * scale
    s_tail = jnp.where(resumed[:, None, None, None], s_tail, -jnp.inf)
    s_self = dot("bkgd,bkd->bkg", grouped, key_rot) * scale
    highest = jnp.maximum(jnp.maximum(jnp.max(s_cache, axis=-1), jnp.max(s_tail, axis=-1)), s_self)
    e_cache = jnp.exp(s_cache - highest[..., None])
    e_tail = jnp.exp(s_tail - highest[..., None])
    e_self = jnp.exp(s_self - highest)
    denominator = jnp.sum(e_cache, axis=-1) + jnp.sum(e_tail, axis=-1) + e_self
    w_cache = (e_cache / denominator[..., None]).astype(jnp.bfloat16)
    w_tail = (e_tail / denominator[..., None]).astype(jnp.bfloat16)
    w_self = (e_self / denominator).astype(jnp.bfloat16)
    attn = dot("bkgl,blkd->bkgd", w_cache, cache_value)
    attn = attn + dot("bkgt,tkd->bkgd", w_tail, tail_value)
    attn = (
        attn + w_self.astype(jnp.float32)[..., None] * value_new.astype(jnp.float32)[:, :, None, :]
    )
    attn = attn.reshape(ROWS_DEV, query_cols).astype(jnp.bfloat16)

    attn_all = gather(attn, "gx").reshape(owners * ROWS_DEV, query_cols)
    out_part = jnp.dot(attn_all, w_out, preferred_element_type=jnp.float32)
    out_part = out_part.reshape(lax.axis_size("gy"), -1, w_out.shape[1])
    mixed = scatter_sum(lambda d: lax.dynamic_index_in_dim(out_part, d, 0, False), "gy")
    return (mixed.astype(jnp.bfloat16), rebuilt_key[None], rebuilt_value[None])


ROW_TILE = 48
PAY = 128
VALUES = 48
QUERY = 96
F32 = jnp.float32
BF16 = jnp.bfloat16


def whole(space=pltpu.VMEM):
    return pl.BlockSpec(memory_space=space)


def params(limit):
    return pltpu.CompilerParams(vmem_limit_bytes=limit * 1024 * 1024)


def cost(flops, bytes_accessed):
    return pl.CostEstimate(flops=flops, bytes_accessed=bytes_accessed, transcendentals=0)


def angles(len_ref, cos_ref, sin_ref):
    first, second = len_ref[0], len_ref[1]
    row = lax.broadcasted_iota(jnp.int32, (PAY, HD), 0)
    lane = lax.broadcasted_iota(jnp.int32, (PAY, HD), 1)
    resumed = (row == LC) | ((row >= QUERY) & (row < QUERY + 16))
    other = (row == LC + 1) | (row >= QUERY + 16)
    position = jnp.where(row < LC, first + row, 0)
    position = jnp.where(resumed, first + LC, jnp.where(other, second, position))
    half = lax.rem(lane, HD // 2).astype(F32)
    frequency = jnp.exp(half * (-2.0 * math.log(BASE) / HD))
    angle = position.astype(F32) * frequency
    sine = jnp.sin(angle)
    cos_ref[...] = jnp.cos(angle)
    sin_ref[...] = jnp.where(lane < HD // 2, -sine, sine)


def start_load(source, target, sems, first, pieces):
    copies = []
    rows = source.shape[0] // pieces
    for c in range(pieces):
        part = pl.ds(c * rows, rows)
        copy = pltpu.make_async_copy(source.at[part], target.at[part], sems.at[first + c])
        copy.start()
        copies.append(copy)
    return copies


def load_kernel(
    len_hbm, wo_hbm, wk_hbm, wv_hbm, cos_ref, sin_ref, wo, wkv, len_ref, sems
):
    lengths = pltpu.make_async_copy(len_hbm, len_ref, sems.at[0])
    lengths.start()
    copies = start_load(wk_hbm, wkv.at[:, pl.ds(0, HD)], sems, 1, 1)
    copies += start_load(wv_hbm, wkv.at[:, pl.ds(HD, HD)], sems, 2, 1)
    copies += start_load(wo_hbm.at[pl.ds(0, wo.shape[0])], wo, sems, 3, 6)
    lengths.wait()
    angles(len_ref, cos_ref, sin_ref)
    for copy in copies:
        copy.wait()


def own_kernel(s, wkv, out):
    out[...] = jnp.dot(s[...], wkv[...], preferred_element_type=F32)


def query_kernel(first, far, b0, b1, b2, b3, w, wo_hbm, out_ref, wo, acc, sems):
    rows = wo.shape[0]
    copies = start_load(wo_hbm.at[pl.ds(first, rows)], wo, sems, 0, 2)
    lhs = jnp.concatenate([b[...].astype(F32) for b in (b0, b1, b2, b3)], axis=0).astype(BF16)
    acc[...] = jnp.dot(lhs, w[...], preferred_element_type=F32)
    for r in range(acc.shape[0]):
        for h in range(out_ref.shape[1]):
            out_ref[r, pl.ds(h, 1), :] = acc[pl.ds(r, 1), pl.ds(h * HD, HD)]
    for copy in copies:
        copy.wait()


def payload_kernel(
    owner_ref, own, s1, s2, s3, b0, b1, b2, b3, wkv, q_ref, o0, o2, o3, o1, x, pay
):
    gx, gy = lax.axis_index("gx"), lax.axis_index("gy")
    for k, s in enumerate((s1, s2, s3)):
        x[pl.ds(k * ROW_TILE, LC), :] = s[...]
    fresh = [b[...].astype(F32) for b in (b0, b1, b2, b3)]
    fresh.append(jnp.zeros((8, x.shape[1]), F32))
    base = 3 * ROW_TILE
    x[pl.ds(base, 16), :] = jnp.concatenate(fresh, axis=0).astype(BF16)
    late = jnp.dot(x[...], wkv[...], preferred_element_type=F32)
    empty = jnp.zeros((8 - ROWS_DEV, HD), F32)
    for k in range(4):
        target = owner_ref[gy ^ k] ^ gx
        both = late[(k - 1) * ROW_TILE : (k - 1) * ROW_TILE + LC] if k else own[...]
        pay[target, pl.ds(0, LC), :] = both[:, :HD]
        pay[target, pl.ds(VALUES, LC), :] = both[:, HD:]
        both = late[base + k * ROWS_DEV : base + (k + 1) * ROWS_DEV]
        target = k ^ gx ^ gy
        pay[target, pl.ds(LC, 8), :] = jnp.concatenate([both[:, :HD], empty], axis=0)
        pay[target, pl.ds(VALUES + LC, 8), :] = jnp.concatenate([both[:, HD:], empty], axis=0)
        for r in range(ROWS_DEV):
            pay[target, pl.ds(QUERY + 16 * r, 16), :] = q_ref[k * ROWS_DEV + r]
    o0[...] = pay[0]
    o3[...] = pay[3].astype(BF16)
    o2[...] = pay[2].astype(BF16)
    o1[...] = pay[1].astype(BF16)


def attend_kernel(
    len_ref, p0, p1, p2, p3, cos_ref, sin_ref, kv, key_out, value_out, attn_out, attn
):
    total = p0[...] + p1[...].astype(F32) + p2[...].astype(F32) + p3[...].astype(F32)
    turned = total * cos_ref[...] + pltpu.roll(total, HD // 2, 1) * sin_ref[...]
    turned = turned.astype(BF16)
    key_out[...] = turned[:LC]
    value_out[...] = turned[VALUES : VALUES + LC]
    scale = 1.0 / math.sqrt(HD)
    more_key = turned[:VALUES]
    more_value = turned[VALUES:QUERY]
    slots = kv.shape[2]
    contract = (((1,), (1,)), ((), ()))
    for r in range(ROWS_DEV):
        q = turned[QUERY + 16 * r : QUERY + 16 * (r + 1)]
        s = lax.dot_general(q, kv[0, r], contract, preferred_element_type=F32) * scale
        live = lax.broadcasted_iota(jnp.int32, s.shape, 1) < len_ref[r]
        s = jnp.where(live, s, -jnp.inf)
        s_more = lax.dot_general(q, more_key, contract, preferred_element_type=F32) * scale
        lane = lax.broadcasted_iota(jnp.int32, s_more.shape, 1)
        live = lane <= LC if r == 0 else lane == LC + r
        s_more = jnp.where(live, s_more, -jnp.inf)
        highest = jnp.maximum(
            jnp.max(s, axis=1, keepdims=True), jnp.max(s_more, axis=1, keepdims=True)
        )
        e = jnp.exp(s - highest)
        e_more = jnp.exp(s_more - highest)
        total_e = jnp.sum(e, axis=1, keepdims=True) + jnp.sum(e_more, axis=1, keepdims=True)
        out = jnp.dot((e / total_e).astype(BF16), kv[1, r], preferred_element_type=F32)
        out += jnp.dot((e_more / total_e).astype(BF16), more_value, preferred_element_type=F32)
        for h in range(out.shape[0]):
            attn[pl.ds(r, 1), pl.ds(h * HD, HD)] = out[h : h + 1]
    attn_out[...] = attn[...].astype(BF16)


def out_kernel(a0, a1, a2, a3, w0, w1, o0, o3, o2, o1, blocks):
    tag = lax.axis_index("gx") ^ lax.axis_index("gy")
    for s, a in enumerate((a0, a1, a2, a3)):
        blocks[s ^ tag] = a[...].astype(F32)
    lhs = jnp.concatenate([blocks[k] for k in range(4)], axis=0).astype(BF16)
    first = 0
    acc = jnp.zeros((lhs.shape[0], w0.shape[1]), F32)
    for w in (w0, w1):
        last = first + w.shape[0]
        acc += jnp.dot(lhs[:, first:last], w[...], preferred_element_type=F32)
        first = last
    o0[...] = acc[0:2]
    o1[...] = acc[2:4].astype(BF16)
    o2[...] = acc[4:6].astype(BF16)
    o3[...] = acc[6:8].astype(BF16)


def others(blocks, axis, order):
    return [swap(b, axis, k) for k, b in zip(order, blocks)]


def per_device(stored_rows, new_rows, w_query, w_key, w_value, w_out, kv_cache, cache_len, owner):
    shape = jax.ShapeDtypeStruct
    depth, query_cols = w_query.shape
    width = w_out.shape[1]
    heads = query_cols // HD
    quarter = query_cols // 4
    semaphores = pltpu.SemaphoreType.DMA
    in_vmem = lambda x: pltpu.with_memory_space_constraint(x, pltpu.VMEM)
    in_hbm = lambda x: pltpu.with_memory_space_constraint(x, pltpu.HBM)
    far = swap(stored_rows, "gy", 2)
    near = swap(stored_rows, "gy", 1)
    fresh = [swap(new_rows, "gy", k) for k in (1, 2, 3)]
    cos, sin, wo_first, wkv = pl.pallas_call(
        load_kernel,
        out_shape=[pltpu.VMEM((PAY, HD), F32)] * 2
        + [
            pltpu.VMEM((query_cols - quarter, width), BF16),
            pltpu.VMEM((depth, 2 * HD), BF16),
        ],
        in_specs=[whole(pltpu.HBM)] * 4,
        out_specs=[whole()] * 4,
        scratch_shapes=[pltpu.SMEM(cache_len.shape, jnp.int32), semaphores((9,))],
        compiler_params=params(4),
        cost_estimate=cost(1000, 2 * depth * query_cols),
        name="load",
    )(
        in_hbm(cache_len), in_hbm(w_out), in_hbm(w_key), in_hbm(w_value)
    )
    own = pl.pallas_call(
        own_kernel,
        out_shape=pltpu.VMEM((LC, 2 * HD), F32),
        in_specs=[whole()] * 2,
        out_specs=whole(),
        compiler_params=params(4),
        cost_estimate=cost(2 * LC * depth * 256, 4 * depth * HD),
        name="own",
    )(stored_rows, wkv)
    far, own, *fresh = lax.optimization_barrier((far, own, *fresh))
    far_near = swap(far, "gy", 1)
    fresh = [new_rows] + fresh
    query, wo_second = pl.pallas_call(
        functools.partial(query_kernel, query_cols - quarter),
        out_shape=[
            pltpu.VMEM((4 * ROWS_DEV, heads, HD), F32),
            pltpu.VMEM((quarter, width), BF16),
        ],
        in_specs=[whole(pl.ANY)] + [whole()] * 5 + [whole(pltpu.HBM)],
        out_specs=[whole()] * 2,
        scratch_shapes=[pltpu.VMEM((4 * ROWS_DEV, query_cols), F32), semaphores((2,))],
        compiler_params=params(4),
        cost_estimate=cost(2 * 8 * depth * query_cols, 4 * depth * HD),
        name="query",
    )(far, *fresh, in_vmem(w_query), in_hbm(w_out))
    payload = pl.pallas_call(
        payload_kernel,
        out_shape=[shape((PAY, HD), F32)] + [shape((PAY, HD), BF16)] * 3,
        in_specs=[whole(pltpu.SMEM)] + [whole()] * 10,
        out_specs=[whole()] * 4,
        scratch_shapes=[
            pltpu.VMEM((3 * ROW_TILE + 16, depth), BF16),
            pltpu.VMEM((4, PAY, HD), F32),
        ],
        compiler_params=params(8),
        cost_estimate=cost(2 * 208 * depth * 256, 4 * depth * HD),
        name="payload",
    )(owner, own, near, far, far_near, *fresh, wkv, query)
    sums = [payload[0]] + others(payload[1:], "gx", (2, 3, 1))
    rebuilt_key, rebuilt_value, attn = pl.pallas_call(
        attend_kernel,
        out_shape=[pltpu.VMEM((LC, HD), BF16)] * 2 + [pltpu.VMEM((ROWS_DEV, query_cols), BF16)],
        in_specs=[whole(pltpu.SMEM)] + [whole()] * 7,
        out_specs=[whole()] * 3,
        scratch_shapes=[pltpu.VMEM((ROWS_DEV, query_cols), F32)],
        compiler_params=params(4),
        cost_estimate=cost(10000000, 1000000),
        name="attend",
    )(cache_len, *sums, cos, sin, kv_cache)
    attn_all = [attn] + [swap(attn, "gx", k) for k in (1, 2, 3)]
    parts = pl.pallas_call(
        out_kernel,
        out_shape=[shape((ROWS_DEV, width), F32)] + [shape((ROWS_DEV, width), BF16)] * 3,
        in_specs=[whole()] * 6,
        out_specs=[whole()] * 4,
        scratch_shapes=[pltpu.VMEM((4, ROWS_DEV, query_cols), F32)],
        compiler_params=params(4),
        cost_estimate=cost(2 * 8 * width * query_cols, 2 * width * query_cols),
        name="project",
    )(*attn_all, wo_first, wo_second)
    arrived = others(parts[1:], "gy", (3, 2, 1))
    mixed = parts[0] + arrived[0].astype(F32) + arrived[1].astype(F32) + arrived[2].astype(F32)
    return (mixed.astype(BF16), rebuilt_key[None], rebuilt_value[None])


def solution(mesh):
    direct = mesh.shape["gx"] == 4 and mesh.shape["gy"] == 4
    in_specs = (
        P(("groups", "gy"), "gx"),
        P(("groups", "gy"), "gx"),
        P("gx", "gy"),
        P("gx", "gy"),
        P("gx", "gy"),
        P("gy", "gx"),
        P(None, ("groups", "gx"), None, "gy"),
        P(("groups", "gx")),
        P("groups"),
    )
    out_specs = (
        P(("groups", "gy"), "gx"),
        P(("groups", "gx"), None, "gy"),
        P(("groups", "gx"), None, "gy"),
    )
    return jax.shard_map(
        per_device if direct else general, mesh=mesh, in_specs=in_specs, out_specs=out_specs, check_vma=False
    )
```

```python
import functools
import math

import jax
import jax.numpy as jnp
from jax import lax
from jax.experimental import pallas as pl
from jax.experimental.pallas import tpu as pltpu
from jax.sharding import PartitionSpec as P

HD = 128
LC = 40
ROWS_DEV = 2
BASE = 500000.0
DIRECT = 8


def rotate(values, position):
    half = values.shape[-1] // 2
    index_row = jnp.arange(half).astype(jnp.float32)
    frequency = jnp.exp(index_row * (-2.0 * math.log(BASE) / values.shape[-1]))
    angle = position.astype(jnp.float32)[..., None] * frequency
    cosine = jnp.cos(angle)
    sine = jnp.sin(angle)
    first_half = values[..., :half]
    second_half = values[..., half:]
    return jnp.concatenate(
        [first_half * cosine - second_half * sine, second_half * cosine + first_half * sine],
        axis=-1,
    )


def swap(x, axis, k):
    n = lax.axis_size(axis)
    return lax.ppermute(x, axis, [(i, i ^ k) for i in range(n)])


def gather(x, axis):
    n = lax.axis_size(axis)
    if n > DIRECT or n & (n - 1):
        return lax.all_gather(x, axis, axis=0)
    me = lax.axis_index(axis)
    out = jnp.zeros((n,) + x.shape, x.dtype)
    for k in range(n):
        block = x if k == 0 else swap(x, axis, k)
        out = lax.dynamic_update_index_in_dim(out, block, me ^ k, 0)
    return out


def scatter_sum(parts, axis):
    n = lax.axis_size(axis)
    me = lax.axis_index(axis)
    if n > DIRECT or n & (n - 1):
        whole = jnp.stack([parts(d) for d in range(n)])
        return lax.psum_scatter(whole.astype(jnp.float32), axis, scatter_dimension=0)
    total = parts(me).astype(jnp.float32)
    for k in range(1, n):
        total = total + swap(parts(me ^ k).astype(jnp.bfloat16), axis, k).astype(jnp.float32)
    return total


def general(stored_rows, new_rows, w_query, w_key, w_value, w_out, kv_cache, cache_len, owner):
    owners = lax.axis_size("gx")
    key_cols = w_key.shape[1]
    query_cols = w_query.shape[1]
    heads_here = key_cols // HD
    group_size = query_cols // key_cols
    slot_ids = jnp.arange(owners, dtype=jnp.int32)
    inverse = jnp.sum(jnp.where(owner[None, :] == slot_ids[:, None], slot_ids[None, :], 0), axis=1)

    fresh_all = gather(new_rows, "gy").reshape(-1, new_rows.shape[1])
    stored_all = gather(stored_rows, "gy").reshape(owners, LC, stored_rows.shape[1])
    flat = stored_all.reshape(owners * LC, stored_rows.shape[1])
    query_part = jnp.dot(fresh_all, w_query, preferred_element_type=jnp.float32)
    new_key_part = jnp.dot(fresh_all, w_key, preferred_element_type=jnp.float32)
    new_value_part = jnp.dot(fresh_all, w_value, preferred_element_type=jnp.float32)
    key_part = jnp.dot(flat, w_key, preferred_element_type=jnp.float32)
    value_part = jnp.dot(flat, w_value, preferred_element_type=jnp.float32)

    small = jnp.concatenate([query_part, new_key_part, new_value_part], axis=1)
    small = small.reshape(owners, ROWS_DEV, -1)
    large = jnp.concatenate([key_part, value_part], axis=1).reshape(owners, LC, -1)

    small_sum = scatter_sum(lambda d: lax.dynamic_index_in_dim(small, d, 0, False), "gx")
    large_sum = scatter_sum(
        lambda d: lax.dynamic_index_in_dim(
            large, lax.dynamic_index_in_dim(inverse, d, 0, False), 0, False
        ),
        "gx",
    )
    query = small_sum[:, :query_cols]
    fresh_key = small_sum[:, query_cols : query_cols + key_cols]
    fresh_value = small_sum[:, query_cols + key_cols :]
    own_key = large_sum[:, :key_cols]
    own_value = large_sum[:, key_cols:]

    first_len = cache_len[0]
    tail_pos = first_len + jnp.arange(LC, dtype=jnp.int32)
    rebuilt_key = (
        rotate(own_key.reshape(LC, heads_here, HD), tail_pos[:, None])
        .reshape(LC, key_cols)
        .astype(jnp.bfloat16)
    )
    rebuilt_value = own_value.astype(jnp.bfloat16)
    resumed = jnp.arange(ROWS_DEV, dtype=jnp.int32) == 0
    new_pos = cache_len + jnp.where(resumed, LC, 0).astype(jnp.int32)
    query_rot = rotate(query.reshape(ROWS_DEV, query_cols // HD, HD), new_pos[:, None]).astype(
        jnp.bfloat16
    )
    key_rot = rotate(fresh_key.reshape(ROWS_DEV, heads_here, HD), new_pos[:, None]).astype(
        jnp.bfloat16
    )
    value_new = fresh_value.reshape(ROWS_DEV, heads_here, HD).astype(jnp.bfloat16)
    scale = 1.0 / math.sqrt(HD)
    slots = kv_cache.shape[2]
    grouped = query_rot.reshape(ROWS_DEV, heads_here, group_size, HD)
    cache_key = kv_cache[0].reshape(ROWS_DEV, slots, heads_here, HD)
    cache_value = kv_cache[1].reshape(ROWS_DEV, slots, heads_here, HD)
    tail_key = rebuilt_key.reshape(LC, heads_here, HD)
    tail_value = rebuilt_value.reshape(LC, heads_here, HD)
    live = jnp.arange(slots, dtype=jnp.int32)[None, :] < cache_len[:, None]
    dot = lambda spec, a, b: jnp.einsum(spec, a, b, preferred_element_type=jnp.float32)
    s_cache = dot("bkgd,blkd->bkgl", grouped, cache_key) * scale
    s_cache = jnp.where(live[:, None, None, :], s_cache, -jnp.inf)
    s_tail = dot("bkgd,tkd->bkgt", grouped, tail_key) * scale
    s_tail = jnp.where(resumed[:, None, None, None], s_tail, -jnp.inf)
    s_self = dot("bkgd,bkd->bkg", grouped, key_rot) * scale
    highest = jnp.maximum(jnp.maximum(jnp.max(s_cache, axis=-1), jnp.max(s_tail, axis=-1)), s_self)
    e_cache = jnp.exp(s_cache - highest[..., None])
    e_tail = jnp.exp(s_tail - highest[..., None])
    e_self = jnp.exp(s_self - highest)
    denominator = jnp.sum(e_cache, axis=-1) + jnp.sum(e_tail, axis=-1) + e_self
    w_cache = (e_cache / denominator[..., None]).astype(jnp.bfloat16)
    w_tail = (e_tail / denominator[..., None]).astype(jnp.bfloat16)
    w_self = (e_self / denominator).astype(jnp.bfloat16)
    attn = dot("bkgl,blkd->bkgd", w_cache, cache_value)
    attn = attn + dot("bkgt,tkd->bkgd", w_tail, tail_value)
    attn = (
        attn + w_self.astype(jnp.float32)[..., None] * value_new.astype(jnp.float32)[:, :, None, :]
    )
    attn = attn.reshape(ROWS_DEV, query_cols).astype(jnp.bfloat16)

    attn_all = gather(attn, "gx").reshape(owners * ROWS_DEV, query_cols)
    out_part = jnp.dot(attn_all, w_out, preferred_element_type=jnp.float32)
    out_part = out_part.reshape(lax.axis_size("gy"), -1, w_out.shape[1])
    mixed = scatter_sum(lambda d: lax.dynamic_index_in_dim(out_part, d, 0, False), "gy")
    return (mixed.astype(jnp.bfloat16), rebuilt_key[None], rebuilt_value[None])


CHUNK = 512
ROW_TILE = 48
PAY = 120
VALUES = 40
FRESH = 80
QUERY = 88
F32 = jnp.float32
BF16 = jnp.bfloat16


def whole(space=pltpu.VMEM):
    return pl.BlockSpec(memory_space=space)


def params(limit):
    return pltpu.CompilerParams(vmem_limit_bytes=limit * 1024 * 1024)


def cost(flops, bytes_accessed):
    return pl.CostEstimate(flops=flops, bytes_accessed=bytes_accessed, transcendentals=0)


def angles(len_ref, cos_ref, sin_ref):
    first, second = len_ref[0], len_ref[1]
    row = lax.broadcasted_iota(jnp.int32, (PAY, HD), 0)
    lane = lax.broadcasted_iota(jnp.int32, (PAY, HD), 1)
    resumed = (row == FRESH) | ((row >= QUERY) & (row < QUERY + 16))
    other = (row == FRESH + 1) | (row >= QUERY + 16)
    position = jnp.where(row < LC, first + row, 0)
    position = jnp.where(resumed, first + LC, jnp.where(other, second, position))
    half = lax.rem(lane, HD // 2).astype(F32)
    frequency = jnp.exp(half * (-2.0 * math.log(BASE) / HD))
    angle = position.astype(F32) * frequency
    sine = jnp.sin(angle)
    cos_ref[...] = jnp.cos(angle)
    sin_ref[...] = jnp.where(lane < HD // 2, -sine, sine)


def start_load(source, target, sems, first, pieces):
    copies = []
    rows = source.shape[0] // pieces
    for c in range(pieces):
        part = pl.ds(c * rows, rows)
        copy = pltpu.make_async_copy(source.at[part], target.at[part], sems.at[first + c])
        copy.start()
        copies.append(copy)
    return copies


def project_rows(x, wkv):
    both = jnp.zeros((x.shape[0], wkv.shape[1]), F32)
    for c in range(x.shape[1] // CHUNK):
        part = slice(c * CHUNK, (c + 1) * CHUNK)
        both += jnp.dot(x[:, part], wkv[part, :], preferred_element_type=F32)
    return both


def load_kernel(
    len_hbm, wo_hbm, wk_hbm, wv_hbm, cos_ref, sin_ref, wo, wkv, len_ref, sems
):
    lengths = pltpu.make_async_copy(len_hbm, len_ref, sems.at[0])
    lengths.start()
    copies = start_load(wk_hbm, wkv.at[:, pl.ds(0, HD)], sems, 1, 1)
    copies += start_load(wv_hbm, wkv.at[:, pl.ds(HD, HD)], sems, 2, 1)
    copies += start_load(wo_hbm.at[pl.ds(0, wo.shape[0])], wo, sems, 3, 6)
    lengths.wait()
    angles(len_ref, cos_ref, sin_ref)
    for copy in copies:
        copy.wait()


def own_kernel(s, wkv, out):
    out[...] = project_rows(s, wkv)


def query_kernel(first, far, b0, b1, b2, b3, w, wo_hbm, out_ref, wo, acc, sems):
    rows = wo.shape[0]
    copies = start_load(wo_hbm.at[pl.ds(first, rows)], wo, sems, 0, 2)
    lhs = jnp.concatenate([b[...].astype(F32) for b in (b0, b1, b2, b3)], axis=0).astype(BF16)
    acc[...] = jnp.dot(lhs, w[...], preferred_element_type=F32)
    for r in range(acc.shape[0]):
        for h in range(out_ref.shape[1]):
            out_ref[r, pl.ds(h, 1), :] = acc[pl.ds(r, 1), pl.ds(h * HD, HD)]
    for copy in copies:
        copy.wait()


def payload_kernel(
    owner_ref, own, s1, s2, s3, b0, b1, b2, b3, wkv, q_ref, o0, o3, o2, o1, x, pay
):
    gx, gy = lax.axis_index("gx"), lax.axis_index("gy")
    for k, s in enumerate((s1, s2, s3)):
        x[pl.ds(k * ROW_TILE, LC), :] = s[...]
    fresh = [b[...].astype(F32) for b in (b0, b1, b2, b3)]
    fresh.append(jnp.zeros((8, x.shape[1]), F32))
    base = 3 * ROW_TILE
    x[pl.ds(base, 16), :] = jnp.concatenate(fresh, axis=0).astype(BF16)
    late = project_rows(x, wkv)
    empty = jnp.zeros((8 - 2 * ROWS_DEV, HD), F32)
    for k in range(4):
        target = owner_ref[gy ^ k] ^ gx
        both = late[(k - 1) * ROW_TILE : (k - 1) * ROW_TILE + LC] if k else own[...]
        pay[target, pl.ds(0, LC), :] = both[:, :HD]
        pay[target, pl.ds(VALUES, LC), :] = both[:, HD:]
        both = late[base + k * ROWS_DEV : base + (k + 1) * ROWS_DEV]
        target = k ^ gx ^ gy
        pay[target, pl.ds(FRESH, 8), :] = jnp.concatenate(
            [both[:, :HD], both[:, HD:], empty], axis=0
        )
        for r in range(ROWS_DEV):
            pay[target, pl.ds(QUERY + 16 * r, 16), :] = q_ref[k * ROWS_DEV + r]
    o0[...] = pay[0]
    o3[...] = pay[3].astype(BF16)
    o2[...] = pay[2].astype(BF16)
    o1[...] = pay[1].astype(BF16)


def attend_kernel(
    len_ref, p0, p1, p2, p3, cos_ref, sin_ref, kv, key_out, value_out, attn_out, attn
):
    total = p0[...] + p1[...].astype(F32) + p2[...].astype(F32) + p3[...].astype(F32)
    turned = total * cos_ref[...] + pltpu.roll(total, HD // 2, 1) * sin_ref[...]
    tail_value = turned[VALUES : VALUES + LC]
    key_out[...] = turned[:LC].astype(BF16)
    value_out[...] = tail_value.astype(BF16)
    scale = 1.0 / math.sqrt(HD)
    more_key = jnp.concatenate([turned[:LC], turned[FRESH:QUERY]], axis=0).astype(BF16)
    fresh_value = turned[FRESH + ROWS_DEV : FRESH + 2 * ROWS_DEV]
    empty = jnp.zeros((8 - ROWS_DEV, HD), F32)
    more_value = jnp.concatenate([tail_value, fresh_value, empty], axis=0).astype(BF16)
    slots = kv.shape[2]
    contract = (((1,), (1,)), ((), ()))
    for r in range(ROWS_DEV):
        q = turned[QUERY + 16 * r : QUERY + 16 * (r + 1)].astype(BF16)
        s = lax.dot_general(q, kv[0, r], contract, preferred_element_type=F32) * scale
        live = lax.broadcasted_iota(jnp.int32, s.shape, 1) < len_ref[r]
        s = jnp.where(live, s, -jnp.inf)
        s_more = lax.dot_general(q, more_key, contract, preferred_element_type=F32) * scale
        lane = lax.broadcasted_iota(jnp.int32, s_more.shape, 1)
        live = lane <= LC if r == 0 else lane == LC + r
        s_more = jnp.where(live, s_more, -jnp.inf)
        highest = jnp.maximum(
            jnp.max(s, axis=1, keepdims=True), jnp.max(s_more, axis=1, keepdims=True)
        )
        e = jnp.exp(s - highest)
        e_more = jnp.exp(s_more - highest)
        total_e = jnp.sum(e, axis=1, keepdims=True) + jnp.sum(e_more, axis=1, keepdims=True)
        out = jnp.dot((e / total_e).astype(BF16), kv[1, r], preferred_element_type=F32)
        out += jnp.dot((e_more / total_e).astype(BF16), more_value, preferred_element_type=F32)
        for h in range(out.shape[0]):
            attn[pl.ds(r, 1), pl.ds(h * HD, HD)] = out[h : h + 1]
    attn_out[...] = attn[...].astype(BF16)


def out_kernel(a0, a1, a2, a3, w0, w1, o0, o3, o2, o1, blocks):
    tag = lax.axis_index("gx") ^ lax.axis_index("gy")
    for s, a in enumerate((a0, a1, a2, a3)):
        blocks[s ^ tag] = a[...].astype(F32)
    lhs = jnp.concatenate([blocks[k] for k in range(4)], axis=0).astype(BF16)
    first = 0
    acc = jnp.zeros((lhs.shape[0], w0.shape[1]), F32)
    for w in (w0, w1):
        last = first + w.shape[0]
        acc += jnp.dot(lhs[:, first:last], w[...], preferred_element_type=F32)
        first = last
    o0[...] = acc[0:2]
    o1[...] = acc[2:4].astype(BF16)
    o2[...] = acc[4:6].astype(BF16)
    o3[...] = acc[6:8].astype(BF16)


def others(blocks, axis):
    return [swap(b, axis, 3 - k) for k, b in enumerate(blocks)]


def per_device(stored_rows, new_rows, w_query, w_key, w_value, w_out, kv_cache, cache_len, owner):
    shape = jax.ShapeDtypeStruct
    depth, query_cols = w_query.shape
    width = w_out.shape[1]
    heads = query_cols // HD
    quarter = query_cols // 4
    semaphores = pltpu.SemaphoreType.DMA
    in_vmem = lambda x: pltpu.with_memory_space_constraint(x, pltpu.VMEM)
    in_hbm = lambda x: pltpu.with_memory_space_constraint(x, pltpu.HBM)
    far = swap(stored_rows, "gy", 2)
    near = swap(stored_rows, "gy", 1)
    fresh = [swap(new_rows, "gy", k) for k in (1, 2, 3)]
    cos, sin, wo_first, wkv = pl.pallas_call(
        load_kernel,
        out_shape=[pltpu.VMEM((PAY, HD), F32)] * 2
        + [
            pltpu.VMEM((query_cols - quarter, width), BF16),
            pltpu.VMEM((depth, 2 * HD), BF16),
        ],
        in_specs=[whole(pltpu.HBM)] * 4,
        out_specs=[whole()] * 4,
        scratch_shapes=[pltpu.SMEM(cache_len.shape, jnp.int32), semaphores((9,))],
        compiler_params=params(4),
        cost_estimate=cost(1000, 2 * depth * query_cols),
        name="load",
    )(
        in_hbm(cache_len), in_hbm(w_out), in_hbm(w_key), in_hbm(w_value)
    )
    own = pl.pallas_call(
        own_kernel,
        out_shape=pltpu.VMEM((LC, 2 * HD), F32),
        in_specs=[whole()] * 2,
        out_specs=whole(),
        compiler_params=params(4),
        cost_estimate=cost(2 * LC * depth * 256, 4 * depth * HD),
        name="own",
    )(stored_rows, wkv)
    far, own, *fresh = lax.optimization_barrier((far, own, *fresh))
    far_near = swap(far, "gy", 1)
    fresh = [new_rows] + fresh
    query, wo_second = pl.pallas_call(
        functools.partial(query_kernel, query_cols - quarter),
        out_shape=[
            pltpu.VMEM((4 * ROWS_DEV, heads, HD), F32),
            pltpu.VMEM((quarter, width), BF16),
        ],
        in_specs=[whole(pl.ANY)] + [whole()] * 5 + [whole(pltpu.HBM)],
        out_specs=[whole()] * 2,
        scratch_shapes=[pltpu.VMEM((4 * ROWS_DEV, query_cols), F32), semaphores((2,))],
        compiler_params=params(4),
        cost_estimate=cost(2 * 8 * depth * query_cols, 4 * depth * HD),
        name="query",
    )(far, *fresh, in_vmem(w_query), in_hbm(w_out))
    payload = pl.pallas_call(
        payload_kernel,
        out_shape=[shape((PAY, HD), F32)] + [shape((PAY, HD), BF16)] * 3,
        in_specs=[whole(pltpu.SMEM)] + [whole()] * 10,
        out_specs=[whole()] * 4,
        scratch_shapes=[
            pltpu.VMEM((3 * ROW_TILE + 16, depth), BF16),
            pltpu.VMEM((4, PAY, HD), F32),
        ],
        compiler_params=params(8),
        cost_estimate=cost(2 * 208 * depth * 256, 4 * depth * HD),
        name="payload",
    )(owner, own, near, far, far_near, *fresh, wkv, query)
    sums = [payload[0]] + others(payload[1:], "gx")
    rebuilt_key, rebuilt_value, attn = pl.pallas_call(
        attend_kernel,
        out_shape=[pltpu.VMEM((LC, HD), BF16)] * 2 + [pltpu.VMEM((ROWS_DEV, query_cols), BF16)],
        in_specs=[whole(pltpu.SMEM)] + [whole()] * 7,
        out_specs=[whole()] * 3,
        scratch_shapes=[pltpu.VMEM((ROWS_DEV, query_cols), F32)],
        compiler_params=params(4),
        cost_estimate=cost(10000000, 1000000),
        name="attend",
    )(cache_len, *sums, cos, sin, kv_cache)
    attn_all = [attn] + [swap(attn, "gx", k) for k in (1, 2, 3)]
    parts = pl.pallas_call(
        out_kernel,
        out_shape=[shape((ROWS_DEV, width), F32)] + [shape((ROWS_DEV, width), BF16)] * 3,
        in_specs=[whole()] * 6,
        out_specs=[whole()] * 4,
        scratch_shapes=[pltpu.VMEM((4, ROWS_DEV, query_cols), F32)],
        compiler_params=params(4),
        cost_estimate=cost(2 * 8 * width * query_cols, 2 * width * query_cols),
        name="project",
    )(*attn_all, wo_first, wo_second)
    arrived = others(parts[1:], "gy")
    mixed = parts[0] + arrived[0].astype(F32) + arrived[1].astype(F32) + arrived[2].astype(F32)
    return (mixed.astype(BF16), rebuilt_key[None], rebuilt_value[None])


def solution(mesh):
    direct = mesh.shape["gx"] == 4 and mesh.shape["gy"] == 4
    in_specs = (
        P(("groups", "gy"), "gx"),
        P(("groups", "gy"), "gx"),
        P("gx", "gy"),
        P("gx", "gy"),
        P("gx", "gy"),
        P("gy", "gx"),
        P(None, ("groups", "gx"), None, "gy"),
        P(("groups", "gx")),
        P("groups"),
    )
    out_specs = (
        P(("groups", "gy"), "gx"),
        P(("groups", "gx"), None, "gy"),
        P(("groups", "gx"), None, "gy"),
    )
    return jax.shard_map(
        per_device if direct else general, mesh=mesh, in_specs=in_specs, out_specs=out_specs, check_vma=False
    )
```

```python
import functools
import math

import jax
import jax.numpy as jnp
from jax import lax
from jax.experimental import pallas as pl
from jax.experimental.pallas import tpu as pltpu
from jax.sharding import PartitionSpec as P

HD = 128
LC = 40
ROWS_DEV = 2
BASE = 500000.0
DIRECT = 8


def rotate(values, position):
    half = values.shape[-1] // 2
    index_row = jnp.arange(half).astype(jnp.float32)
    frequency = jnp.exp(index_row * (-2.0 * math.log(BASE) / values.shape[-1]))
    angle = position.astype(jnp.float32)[..., None] * frequency
    cosine = jnp.cos(angle)
    sine = jnp.sin(angle)
    first_half = values[..., :half]
    second_half = values[..., half:]
    return jnp.concatenate(
        [first_half * cosine - second_half * sine, second_half * cosine + first_half * sine],
        axis=-1,
    )


def swap(x, axis, k):
    n = lax.axis_size(axis)
    return lax.ppermute(x, axis, [(i, i ^ k) for i in range(n)])


def gather(x, axis):
    n = lax.axis_size(axis)
    if n > DIRECT or n & (n - 1):
        return lax.all_gather(x, axis, axis=0)
    me = lax.axis_index(axis)
    out = jnp.zeros((n,) + x.shape, x.dtype)
    for k in range(n):
        block = x if k == 0 else swap(x, axis, k)
        out = lax.dynamic_update_index_in_dim(out, block, me ^ k, 0)
    return out


def scatter_sum(parts, axis):
    n = lax.axis_size(axis)
    me = lax.axis_index(axis)
    if n > DIRECT or n & (n - 1):
        whole = jnp.stack([parts(d) for d in range(n)])
        return lax.psum_scatter(whole.astype(jnp.float32), axis, scatter_dimension=0)
    total = parts(me).astype(jnp.float32)
    for k in range(1, n):
        total = total + swap(parts(me ^ k).astype(jnp.bfloat16), axis, k).astype(jnp.float32)
    return total


def general(stored_rows, new_rows, w_query, w_key, w_value, w_out, kv_cache, cache_len, owner):
    owners = lax.axis_size("gx")
    key_cols = w_key.shape[1]
    query_cols = w_query.shape[1]
    heads_here = key_cols // HD
    group_size = query_cols // key_cols
    slot_ids = jnp.arange(owners, dtype=jnp.int32)
    inverse = jnp.sum(jnp.where(owner[None, :] == slot_ids[:, None], slot_ids[None, :], 0), axis=1)

    fresh_all = gather(new_rows, "gy").reshape(-1, new_rows.shape[1])
    stored_all = gather(stored_rows, "gy").reshape(owners, LC, stored_rows.shape[1])
    flat = stored_all.reshape(owners * LC, stored_rows.shape[1])
    query_part = jnp.dot(fresh_all, w_query, preferred_element_type=jnp.float32)
    new_key_part = jnp.dot(fresh_all, w_key, preferred_element_type=jnp.float32)
    new_value_part = jnp.dot(fresh_all, w_value, preferred_element_type=jnp.float32)
    key_part = jnp.dot(flat, w_key, preferred_element_type=jnp.float32)
    value_part = jnp.dot(flat, w_value, preferred_element_type=jnp.float32)

    small = jnp.concatenate([query_part, new_key_part, new_value_part], axis=1)
    small = small.reshape(owners, ROWS_DEV, -1)
    large = jnp.concatenate([key_part, value_part], axis=1).reshape(owners, LC, -1)

    small_sum = scatter_sum(lambda d: lax.dynamic_index_in_dim(small, d, 0, False), "gx")
    large_sum = scatter_sum(
        lambda d: lax.dynamic_index_in_dim(
            large, lax.dynamic_index_in_dim(inverse, d, 0, False), 0, False
        ),
        "gx",
    )
    query = small_sum[:, :query_cols]
    fresh_key = small_sum[:, query_cols : query_cols + key_cols]
    fresh_value = small_sum[:, query_cols + key_cols :]
    own_key = large_sum[:, :key_cols]
    own_value = large_sum[:, key_cols:]

    first_len = cache_len[0]
    tail_pos = first_len + jnp.arange(LC, dtype=jnp.int32)
    rebuilt_key = (
        rotate(own_key.reshape(LC, heads_here, HD), tail_pos[:, None])
        .reshape(LC, key_cols)
        .astype(jnp.bfloat16)
    )
    rebuilt_value = own_value.astype(jnp.bfloat16)
    resumed = jnp.arange(ROWS_DEV, dtype=jnp.int32) == 0
    new_pos = cache_len + jnp.where(resumed, LC, 0).astype(jnp.int32)
    query_rot = rotate(query.reshape(ROWS_DEV, query_cols // HD, HD), new_pos[:, None]).astype(
        jnp.bfloat16
    )
    key_rot = rotate(fresh_key.reshape(ROWS_DEV, heads_here, HD), new_pos[:, None]).astype(
        jnp.bfloat16
    )
    value_new = fresh_value.reshape(ROWS_DEV, heads_here, HD).astype(jnp.bfloat16)
    scale = 1.0 / math.sqrt(HD)
    slots = kv_cache.shape[2]
    grouped = query_rot.reshape(ROWS_DEV, heads_here, group_size, HD)
    cache_key = kv_cache[0].reshape(ROWS_DEV, slots, heads_here, HD)
    cache_value = kv_cache[1].reshape(ROWS_DEV, slots, heads_here, HD)
    tail_key = rebuilt_key.reshape(LC, heads_here, HD)
    tail_value = rebuilt_value.reshape(LC, heads_here, HD)
    live = jnp.arange(slots, dtype=jnp.int32)[None, :] < cache_len[:, None]
    dot = lambda spec, a, b: jnp.einsum(spec, a, b, preferred_element_type=jnp.float32)
    s_cache = dot("bkgd,blkd->bkgl", grouped, cache_key) * scale
    s_cache = jnp.where(live[:, None, None, :], s_cache, -jnp.inf)
    s_tail = dot("bkgd,tkd->bkgt", grouped, tail_key) * scale
    s_tail = jnp.where(resumed[:, None, None, None], s_tail, -jnp.inf)
    s_self = dot("bkgd,bkd->bkg", grouped, key_rot) * scale
    highest = jnp.maximum(jnp.maximum(jnp.max(s_cache, axis=-1), jnp.max(s_tail, axis=-1)), s_self)
    e_cache = jnp.exp(s_cache - highest[..., None])
    e_tail = jnp.exp(s_tail - highest[..., None])
    e_self = jnp.exp(s_self - highest)
    denominator = jnp.sum(e_cache, axis=-1) + jnp.sum(e_tail, axis=-1) + e_self
    w_cache = (e_cache / denominator[..., None]).astype(jnp.bfloat16)
    w_tail = (e_tail / denominator[..., None]).astype(jnp.bfloat16)
    w_self = (e_self / denominator).astype(jnp.bfloat16)
    attn = dot("bkgl,blkd->bkgd", w_cache, cache_value)
    attn = attn + dot("bkgt,tkd->bkgd", w_tail, tail_value)
    attn = (
        attn + w_self.astype(jnp.float32)[..., None] * value_new.astype(jnp.float32)[:, :, None, :]
    )
    attn = attn.reshape(ROWS_DEV, query_cols).astype(jnp.bfloat16)

    attn_all = gather(attn, "gx").reshape(owners * ROWS_DEV, query_cols)
    out_part = jnp.dot(attn_all, w_out, preferred_element_type=jnp.float32)
    out_part = out_part.reshape(lax.axis_size("gy"), -1, w_out.shape[1])
    mixed = scatter_sum(lambda d: lax.dynamic_index_in_dim(out_part, d, 0, False), "gy")
    return (mixed.astype(jnp.bfloat16), rebuilt_key[None], rebuilt_value[None])


ROW_TILE = 48
PAY = 120
VALUES = 40
FRESH = 80
QUERY = 88
F32 = jnp.float32
BF16 = jnp.bfloat16


def whole(space=pltpu.VMEM):
    return pl.BlockSpec(memory_space=space)


def params(limit):
    return pltpu.CompilerParams(vmem_limit_bytes=limit * 1024 * 1024)


def cost(flops, bytes_accessed):
    return pl.CostEstimate(flops=flops, bytes_accessed=bytes_accessed, transcendentals=0)


def angles(len_ref, cos_ref, sin_ref):
    first, second = len_ref[0], len_ref[1]
    row = lax.broadcasted_iota(jnp.int32, (PAY, HD), 0)
    lane = lax.broadcasted_iota(jnp.int32, (PAY, HD), 1)
    resumed = (row == FRESH) | ((row >= QUERY) & (row < QUERY + 16))
    other = (row == FRESH + 1) | (row >= QUERY + 16)
    position = jnp.where(row < LC, first + row, 0)
    position = jnp.where(resumed, first + LC, jnp.where(other, second, position))
    half = lax.rem(lane, HD // 2).astype(F32)
    frequency = jnp.exp(half * (-2.0 * math.log(BASE) / HD))
    angle = position.astype(F32) * frequency
    sine = jnp.sin(angle)
    cos_ref[...] = jnp.cos(angle)
    sin_ref[...] = jnp.where(lane < HD // 2, -sine, sine)


def start_load(source, target, sems, first, pieces):
    copies = []
    rows = source.shape[0] // pieces
    for c in range(pieces):
        part = pl.ds(c * rows, rows)
        copy = pltpu.make_async_copy(source.at[part], target.at[part], sems.at[first + c])
        copy.start()
        copies.append(copy)
    return copies


def load_kernel(
    len_hbm, wo_hbm, wk_hbm, wv_hbm, cos_ref, sin_ref, wo, wkv, len_ref, sems
):
    lengths = pltpu.make_async_copy(len_hbm, len_ref, sems.at[0])
    lengths.start()
    copies = start_load(wk_hbm, wkv.at[:, pl.ds(0, HD)], sems, 1, 1)
    copies += start_load(wv_hbm, wkv.at[:, pl.ds(HD, HD)], sems, 2, 1)
    copies += start_load(wo_hbm.at[pl.ds(0, wo.shape[0])], wo, sems, 3, 6)
    lengths.wait()
    angles(len_ref, cos_ref, sin_ref)
    for copy in copies:
        copy.wait()


def own_kernel(s, wkv, out):
    out[...] = jnp.dot(s[...], wkv[...], preferred_element_type=F32)


def query_kernel(first, far, b0, b1, b2, b3, w, wo_hbm, out_ref, wo, acc, sems):
    rows = wo.shape[0]
    copies = start_load(wo_hbm.at[pl.ds(first, rows)], wo, sems, 0, 2)
    lhs = jnp.concatenate([b[...].astype(F32) for b in (b0, b1, b2, b3)], axis=0).astype(BF16)
    acc[...] = jnp.dot(lhs, w[...], preferred_element_type=F32)
    for r in range(acc.shape[0]):
        for h in range(out_ref.shape[1]):
            out_ref[r, pl.ds(h, 1), :] = acc[pl.ds(r, 1), pl.ds(h * HD, HD)]
    for copy in copies:
        copy.wait()


def payload_kernel(
    owner_ref, own, s1, s2, s3, b0, b1, b2, b3, wkv, q_ref, o0, o3, o2, o1, x, pay
):
    gx, gy = lax.axis_index("gx"), lax.axis_index("gy")
    for k, s in enumerate((s1, s2, s3)):
        x[pl.ds(k * ROW_TILE, LC), :] = s[...]
    fresh = [b[...].astype(F32) for b in (b0, b1, b2, b3)]
    fresh.append(jnp.zeros((8, x.shape[1]), F32))
    base = 3 * ROW_TILE
    x[pl.ds(base, 16), :] = jnp.concatenate(fresh, axis=0).astype(BF16)
    late = jnp.dot(x[...], wkv[...], preferred_element_type=F32)
    empty = jnp.zeros((8 - 2 * ROWS_DEV, HD), F32)
    for k in range(4):
        target = owner_ref[gy ^ k] ^ gx
        both = late[(k - 1) * ROW_TILE : (k - 1) * ROW_TILE + LC] if k else own[...]
        pay[target, pl.ds(0, LC), :] = both[:, :HD]
        pay[target, pl.ds(VALUES, LC), :] = both[:, HD:]
        both = late[base + k * ROWS_DEV : base + (k + 1) * ROWS_DEV]
        target = k ^ gx ^ gy
        pay[target, pl.ds(FRESH, 8), :] = jnp.concatenate(
            [both[:, :HD], both[:, HD:], empty], axis=0
        )
        for r in range(ROWS_DEV):
            pay[target, pl.ds(QUERY + 16 * r, 16), :] = q_ref[k * ROWS_DEV + r]
    o0[...] = pay[0]
    o3[...] = pay[3].astype(BF16)
    o2[...] = pay[2].astype(BF16)
    o1[...] = pay[1].astype(BF16)


def attend_kernel(
    len_ref, p0, p1, p2, p3, cos_ref, sin_ref, kv, key_out, value_out, attn_out, attn
):
    total = p0[...] + p1[...].astype(F32) + p2[...].astype(F32) + p3[...].astype(F32)
    turned = total * cos_ref[...] + pltpu.roll(total, HD // 2, 1) * sin_ref[...]
    tail_value = turned[VALUES : VALUES + LC]
    key_out[...] = turned[:LC].astype(BF16)
    value_out[...] = tail_value.astype(BF16)
    scale = 1.0 / math.sqrt(HD)
    more_key = jnp.concatenate([turned[:LC], turned[FRESH:QUERY]], axis=0).astype(BF16)
    fresh_value = turned[FRESH + ROWS_DEV : FRESH + 2 * ROWS_DEV]
    empty = jnp.zeros((8 - ROWS_DEV, HD), F32)
    more_value = jnp.concatenate([tail_value, fresh_value, empty], axis=0).astype(BF16)
    slots = kv.shape[2]
    contract = (((1,), (1,)), ((), ()))
    for r in range(ROWS_DEV):
        q = turned[QUERY + 16 * r : QUERY + 16 * (r + 1)].astype(BF16)
        s = lax.dot_general(q, kv[0, r], contract, preferred_element_type=F32) * scale
        live = lax.broadcasted_iota(jnp.int32, s.shape, 1) < len_ref[r]
        s = jnp.where(live, s, -jnp.inf)
        s_more = lax.dot_general(q, more_key, contract, preferred_element_type=F32) * scale
        lane = lax.broadcasted_iota(jnp.int32, s_more.shape, 1)
        live = lane <= LC if r == 0 else lane == LC + r
        s_more = jnp.where(live, s_more, -jnp.inf)
        highest = jnp.maximum(
            jnp.max(s, axis=1, keepdims=True), jnp.max(s_more, axis=1, keepdims=True)
        )
        e = jnp.exp(s - highest)
        e_more = jnp.exp(s_more - highest)
        total_e = jnp.sum(e, axis=1, keepdims=True) + jnp.sum(e_more, axis=1, keepdims=True)
        out = jnp.dot((e / total_e).astype(BF16), kv[1, r], preferred_element_type=F32)
        out += jnp.dot((e_more / total_e).astype(BF16), more_value, preferred_element_type=F32)
        for h in range(out.shape[0]):
            attn[pl.ds(r, 1), pl.ds(h * HD, HD)] = out[h : h + 1]
    attn_out[...] = attn[...].astype(BF16)


def out_kernel(a0, a1, a2, a3, w0, w1, o0, o3, o2, o1, blocks):
    tag = lax.axis_index("gx") ^ lax.axis_index("gy")
    for s, a in enumerate((a0, a1, a2, a3)):
        blocks[s ^ tag] = a[...].astype(F32)
    lhs = jnp.concatenate([blocks[k] for k in range(4)], axis=0).astype(BF16)
    first = 0
    acc = jnp.zeros((lhs.shape[0], w0.shape[1]), F32)
    for w in (w0, w1):
        last = first + w.shape[0]
        acc += jnp.dot(lhs[:, first:last], w[...], preferred_element_type=F32)
        first = last
    o0[...] = acc[0:2]
    o1[...] = acc[2:4].astype(BF16)
    o2[...] = acc[4:6].astype(BF16)
    o3[...] = acc[6:8].astype(BF16)


def others(blocks, axis):
    return [swap(b, axis, 3 - k) for k, b in enumerate(blocks)]


def per_device(stored_rows, new_rows, w_query, w_key, w_value, w_out, kv_cache, cache_len, owner):
    shape = jax.ShapeDtypeStruct
    depth, query_cols = w_query.shape
    width = w_out.shape[1]
    heads = query_cols // HD
    quarter = query_cols // 4
    semaphores = pltpu.SemaphoreType.DMA
    in_vmem = lambda x: pltpu.with_memory_space_constraint(x, pltpu.VMEM)
    in_hbm = lambda x: pltpu.with_memory_space_constraint(x, pltpu.HBM)
    far = swap(stored_rows, "gy", 2)
    near = swap(stored_rows, "gy", 1)
    fresh = [swap(new_rows, "gy", k) for k in (1, 2, 3)]
    cos, sin, wo_first, wkv = pl.pallas_call(
        load_kernel,
        out_shape=[pltpu.VMEM((PAY, HD), F32)] * 2
        + [
            pltpu.VMEM((query_cols - quarter, width), BF16),
            pltpu.VMEM((depth, 2 * HD), BF16),
        ],
        in_specs=[whole(pltpu.HBM)] * 4,
        out_specs=[whole()] * 4,
        scratch_shapes=[pltpu.SMEM(cache_len.shape, jnp.int32), semaphores((9,))],
        compiler_params=params(4),
        cost_estimate=cost(1000, 2 * depth * query_cols),
        name="load",
    )(
        in_hbm(cache_len), in_hbm(w_out), in_hbm(w_key), in_hbm(w_value)
    )
    own = pl.pallas_call(
        own_kernel,
        out_shape=pltpu.VMEM((LC, 2 * HD), F32),
        in_specs=[whole()] * 2,
        out_specs=whole(),
        compiler_params=params(4),
        cost_estimate=cost(2 * LC * depth * 256, 4 * depth * HD),
        name="own",
    )(stored_rows, wkv)
    far, own, *fresh = lax.optimization_barrier((far, own, *fresh))
    far_near = swap(far, "gy", 1)
    fresh = [new_rows] + fresh
    query, wo_second = pl.pallas_call(
        functools.partial(query_kernel, query_cols - quarter),
        out_shape=[
            pltpu.VMEM((4 * ROWS_DEV, heads, HD), F32),
            pltpu.VMEM((quarter, width), BF16),
        ],
        in_specs=[whole(pl.ANY)] + [whole()] * 5 + [whole(pltpu.HBM)],
        out_specs=[whole()] * 2,
        scratch_shapes=[pltpu.VMEM((4 * ROWS_DEV, query_cols), F32), semaphores((2,))],
        compiler_params=params(4),
        cost_estimate=cost(2 * 8 * depth * query_cols, 4 * depth * HD),
        name="query",
    )(far, *fresh, in_vmem(w_query), in_hbm(w_out))
    payload = pl.pallas_call(
        payload_kernel,
        out_shape=[shape((PAY, HD), F32)] + [shape((PAY, HD), BF16)] * 3,
        in_specs=[whole(pltpu.SMEM)] + [whole()] * 10,
        out_specs=[whole()] * 4,
        scratch_shapes=[
            pltpu.VMEM((3 * ROW_TILE + 16, depth), BF16),
            pltpu.VMEM((4, PAY, HD), F32),
        ],
        compiler_params=params(8),
        cost_estimate=cost(2 * 208 * depth * 256, 4 * depth * HD),
        name="payload",
    )(owner, own, near, far, far_near, *fresh, wkv, query)
    sums = [payload[0]] + others(payload[1:], "gx")
    rebuilt_key, rebuilt_value, attn = pl.pallas_call(
        attend_kernel,
        out_shape=[pltpu.VMEM((LC, HD), BF16)] * 2 + [pltpu.VMEM((ROWS_DEV, query_cols), BF16)],
        in_specs=[whole(pltpu.SMEM)] + [whole()] * 7,
        out_specs=[whole()] * 3,
        scratch_shapes=[pltpu.VMEM((ROWS_DEV, query_cols), F32)],
        compiler_params=params(4),
        cost_estimate=cost(10000000, 1000000),
        name="attend",
    )(cache_len, *sums, cos, sin, kv_cache)
    attn_all = [attn] + [swap(attn, "gx", k) for k in (1, 2, 3)]
    parts = pl.pallas_call(
        out_kernel,
        out_shape=[shape((ROWS_DEV, width), F32)] + [shape((ROWS_DEV, width), BF16)] * 3,
        in_specs=[whole()] * 6,
        out_specs=[whole()] * 4,
        scratch_shapes=[pltpu.VMEM((4, ROWS_DEV, query_cols), F32)],
        compiler_params=params(4),
        cost_estimate=cost(2 * 8 * width * query_cols, 2 * width * query_cols),
        name="project",
    )(*attn_all, wo_first, wo_second)
    arrived = others(parts[1:], "gy")
    mixed = parts[0] + arrived[0].astype(F32) + arrived[1].astype(F32) + arrived[2].astype(F32)
    return (mixed.astype(BF16), rebuilt_key[None], rebuilt_value[None])


def solution(mesh):
    direct = mesh.shape["gx"] == 4 and mesh.shape["gy"] == 4
    in_specs = (
        P(("groups", "gy"), "gx"),
        P(("groups", "gy"), "gx"),
        P("gx", "gy"),
        P("gx", "gy"),
        P("gx", "gy"),
        P("gy", "gx"),
        P(None, ("groups", "gx"), None, "gy"),
        P(("groups", "gx")),
        P("groups"),
    )
    out_specs = (
        P(("groups", "gy"), "gx"),
        P(("groups", "gx"), None, "gy"),
        P(("groups", "gx"), None, "gy"),
    )
    return jax.shard_map(
        per_device if direct else general, mesh=mesh, in_specs=in_specs, out_specs=out_specs, check_vma=False
    )
```
